32 devices in a mesh: blk: 16 (over z, y, core), head: 2 (over x).
Axes of the slice: x: 2, y: 2, z: 4, core: 2. Of those that a mesh axis runs over, the one named last changes fastest.
Arguments:
- layer_input: bfloat16 [2, 2048, 2048], P(None, ('blk', 'head')), may hold values from -6 to 6
- attn_gain: bfloat16 [2048], P(('blk', 'head')), may hold values from 0.5 to 1.5
- query_weight: bfloat16 [2048, 2048], P(('blk', 'head')), may hold values from -0.125 to 0.125
- key_matrix: bfloat16 [2048, 512], P(('blk', 'head')), may hold values from -0.125 to 0.125
- value_matrix: bfloat16 [2048, 512], P(('blk', 'head')), may hold values from -0.125 to 0.125
- output_weight: bfloat16 [2048, 2048], P(('blk', 'head')), may hold values from -3 to 3
- ffn_gain: bfloat16 [2048], P(('blk', 'head')), may hold values from 0.5 to 1.5
- gate_weight: bfloat16 [2048, 8192], P(('blk', 'head')), may hold values from -0.125 to 0.125
- up_weight: bfloat16 [2048, 8192], P(('blk', 'head')), may hold values from -0.125 to 0.125
- down_weight: bfloat16 [2048, 8192], P(('blk', 'head')), may hold values from -0.0625 to 0.0625
- block_ids: int32 [2, 2048], replicated, may hold values from 0 to 15, never falling along the last dimension, each value on 1 to 256 neighbouring positions
- cotangent: bfloat16 [2, 2048, 2048], P(None, ('blk', 'head')), may hold values from -6 to 6
Outputs:
- layer_output: float32 [2, 2048, 2048], P(None, ('blk', 'head'))
- input_grad: float32 [2, 2048, 2048], P(None, ('blk', 'head'))
- grad_attn_gain: float32 [2048], P(('blk', 'head'))
- grad_query: float32 [2048, 2048], P(('blk', 'head'))
- grad_key: float32 [2048, 512], P(('blk', 'head'))
- grad_value: float32 [2048, 512], P(('blk', 'head'))
- grad_output: float32 [2048, 2048], P(('blk', 'head'))
- grad_ffn_gain: float32 [2048], P(('blk', 'head'))
- grad_gate: float32 [2048, 8192], P(('blk', 'head'))
- grad_up: float32 [2048, 8192], P(('blk', 'head'))
- grad_down: float32 [2048, 8192], P(('blk', 'head'))
The draws below stay inside these ranges and needn't reach their ends.
Inputs may be any that keep to these rules, and one draw needn't show every extreme that they name: `block_ids`: along each sequence the ids start at 0 and never fall, every id of 0 to 15 is used, a block holds 1 to 256 tokens, and some block holds exactly 256.
All inputs are finite; a program needn't handle non-finite values.
Results may differ from the reference program's by a relative error of at most 0.023.
Values may be sent and summed in bfloat16 or wider, within the bound.
A program may use at most 576 MiB of HBM per device.

```python
import math
import jax
import jax.numpy as jnp
import numpy as np
from jax import lax

MODEL_DIM = 2048
QUERY_HEADS = 32
KEY_HEADS = 8
HEAD_DIM = 64
FF = 8192
SEQS = 2
BLOCK = 256
SEQ = 2048
NBLOCKS = 16


def shard_levels(rng, shape, cuts, least, top_value):
    factor_of = 1.0
    for position, shards_of in cuts:
        draws = jax.random.uniform(jax.random.fold_in(jax.random.fold_in(rng, 6), position), (shards_of,), jnp.float32, least / len(cuts), top_value / len(cuts))
        factor_of = factor_of * jnp.repeat(jnp.exp(draws), shape[position] // shards_of).reshape((-1,) + (1,) * (len(shape) - 1 - position))
    return factor_of


def profile(number_of, total, reach, lean):
    weights = [(1 << 20) // math.isqrt(standing ** lean) + 1 for standing in range(2, number_of + 1)]
    surplus, given = total - reach - (number_of - 1), [1] * (number_of - 1)
    while surplus > 0:
        candidates = [i for i in range(number_of - 1) if given[i] < reach]
        whole, budget = sum([weights[i] for i in candidates]), surplus
        for i in candidates:
            extra = min(reach - given[i], max(1, budget * weights[i] // whole), surplus)
            given[i] = given[i] + extra
            surplus = surplus - extra
    return np.array([reach] + given)


def uneven(stream_key, count, total, bound, skew):
    if count == 2:
        one = jax.random.randint(stream_key, (), max(1, total - bound), min(bound, total - 1) + 1)
        return jnp.stack([one, total - one])
    tallies = jnp.asarray(profile(count, total, bound, skew), jnp.int32)
    pairs = (count - 1) // 2
    donor, receiver = tallies[1:1 + 2 * pairs:2], tallies[2:2 + 2 * pairs:2]
    slack = jnp.minimum(donor - 1, bound - receiver)
    shifted = jax.random.randint(jax.random.fold_in(stream_key, 1), (pairs,), 0, 1 << 20) % (slack + 1)
    tallies = tallies.at[1:1 + 2 * pairs:2].set(donor - shifted).at[2:2 + 2 * pairs:2].set(receiver + shifted)
    return tallies[jax.random.permutation(jax.random.fold_in(stream_key, 2), count)]


def bell_draw(stream_key, dims, width, limit, cuts=(), kind=jnp.bfloat16):
    entries = jax.random.normal(stream_key, dims, jnp.float32) * width
    if len(cuts) > 0:
        entries = shard_levels(stream_key, dims, cuts, -0.22, 0.18) * entries
    return jnp.clip(entries, min=-limit, max=limit).astype(kind)


def setup_inputs(seed: int = 0) -> dict:
    streams_of = jax.random.split(jax.random.key(seed), 13)
    layer_input = bell_draw(streams_of[0], (SEQS, SEQ, MODEL_DIM), 1.0, 6.0, ((1, 32),))
    attn_gain = jnp.clip(1.0 + 0.1 * jax.random.normal(streams_of[1], (MODEL_DIM,), jnp.float32), 0.5, 1.5).astype(jnp.bfloat16)
    query_weight = bell_draw(streams_of[2], (MODEL_DIM, QUERY_HEADS * HEAD_DIM), MODEL_DIM ** -0.5, 0.125, ((0, 32),))
    key_matrix = bell_draw(streams_of[3], (MODEL_DIM, KEY_HEADS * HEAD_DIM), MODEL_DIM ** -0.5, 0.125, ((0, 32),))
    value_matrix = bell_draw(streams_of[4], (MODEL_DIM, KEY_HEADS * HEAD_DIM), MODEL_DIM ** -0.5, 0.125, ((0, 32),))
    output_weight = bell_draw(streams_of[5], (QUERY_HEADS * HEAD_DIM, MODEL_DIM), (max(1, QUERY_HEADS * HEAD_DIM * 4 // SEQ)) ** -0.5, 3.0, ((0, 32),))
    ffn_gain = jnp.clip(1.0 + 0.1 * jax.random.normal(streams_of[6], (MODEL_DIM,), jnp.float32), 0.5, 1.5).astype(jnp.bfloat16)
    gate_weight = bell_draw(streams_of[7], (MODEL_DIM, FF), MODEL_DIM ** -0.5, 0.125, ((0, 32),))
    up_weight = bell_draw(streams_of[8], (MODEL_DIM, FF), MODEL_DIM ** -0.5, 0.125, ((0, 32),))
    down_weight = bell_draw(streams_of[9], (MODEL_DIM, FF), FF ** -0.5, 0.0625, ((0, 32),))
    block_ids = jax.vmap(lambda own: jnp.searchsorted(jnp.cumsum(uneven(own, NBLOCKS, SEQ, BLOCK, 1)), jnp.arange(SEQ), side="right"))(jax.random.split(streams_of[10], SEQS)).reshape((SEQS, SEQ)).astype(jnp.int32)
    cotangent = bell_draw(streams_of[11], (SEQS, SEQ, MODEL_DIM), 1.0, 6.0, ((1, 32),))
    return {"layer_input": layer_input, "attn_gain": attn_gain, "query_weight": query_weight, "key_matrix": key_matrix, "value_matrix": value_matrix, "output_weight": output_weight, "ffn_gain": ffn_gain, "gate_weight": gate_weight, "up_weight": up_weight, "down_weight": down_weight, "block_ids": block_ids, "cotangent": cotangent}


epsilon = 1e-05
rope_base = 500000.0
highest = lax.Precision.HIGHEST

@jax.custom_vjp
def low(v):
    return lax.optimization_barrier(v.astype(jnp.bfloat16)).astype(jnp.float32)

@jax.custom_vjp
def low_back(v):
    return v

def low_keep(v):
    return (low(v), None)

def low_pass(kept, grad):
    return (grad,)

def back_keep(v):
    return (v, None)

def back_low(kept, grad):
    return (low(grad),)
low.defvjp(low_keep, low_pass)
low_back.defvjp(back_keep, back_low)

def matmul(left, right):
    return jnp.dot(left, right, precision=highest, preferred_element_type=jnp.float32)

def rotation_tables(positions, head_size):
    half = head_size // 2
    freqs = rope_base ** (-jnp.arange(half, dtype=jnp.float32) * 2.0 / head_size)
    angles = positions.astype(jnp.float32)[:, None] * freqs[None, :]
    return (jnp.cos(angles), jnp.sin(angles))

def rotate(value_rows, cosine_table, sine_table, direction):
    count_of_rows = value_rows.shape[0]
    half = cosine_table.shape[1]
    shaped = value_rows.reshape(count_of_rows, -1, 2 * half)
    first = shaped[..., :half]
    second = shaped[..., half:]
    cos_wide = cosine_table[:, None, :]
    sin_wide = direction * sine_table[:, None, :]
    turned = jnp.concatenate([first * cos_wide - second * sin_wide, second * cos_wide + first * sin_wide], axis=-1)
    return turned.reshape(count_of_rows, -1)

def attention(query_rows, key_rows, value_rows, blocks):
    sequence_length = query_rows.shape[0]
    query_group_width = QUERY_HEADS // KEY_HEADS
    rows_per_block = min(512, sequence_length)
    heads_of_query = query_rows.reshape(sequence_length // rows_per_block, rows_per_block, KEY_HEADS, query_group_width, HEAD_DIM)
    query_blocks = blocks.reshape(sequence_length // rows_per_block, rows_per_block)
    heads_of_key = key_rows.reshape(sequence_length, KEY_HEADS, HEAD_DIM)
    heads_of_value = value_rows.reshape(sequence_length, KEY_HEADS, HEAD_DIM)
    score_scale = HEAD_DIM ** (-0.5)

    def one_block(inputs):
        block_queries, block_here = inputs
        products = jnp.einsum('qkgd,nkd->qkgn', block_queries, heads_of_key, precision=highest) * score_scale
        scores = low_back(products)
        allowed = (blocks[None, :] <= block_here[:, None])[:, None, None, :]
        masked = jnp.where(allowed, scores, -1e+30)
        weights = jax.nn.softmax(masked, axis=-1)
        blended = jnp.einsum('qkgn,nkd->qkgd', low(weights), heads_of_value, precision=highest)
        return blended.reshape(rows_per_block, QUERY_HEADS * HEAD_DIM)
    outputs = lax.map(jax.checkpoint(one_block), (heads_of_query, query_blocks))
    return outputs.reshape(sequence_length, QUERY_HEADS * HEAD_DIM)

def layer(inputs, attn_gain, query_weight, key_matrix, value_matrix, output_weight, ffn_gain, gate_weight, up_weight, down_weight, blocks):
    sequence_length = inputs.shape[0]
    positions = jnp.arange(sequence_length, dtype=jnp.int32)
    cosine_table, sine_table = rotation_tables(positions, HEAD_DIM)
    norm_one = lax.rsqrt(lax.optimization_barrier(jnp.mean(inputs * inputs, axis=-1, keepdims=True)) + epsilon)
    normed_one = low(inputs * norm_one * attn_gain)
    query_rows = low(rotate(low_back(matmul(normed_one, query_weight)), cosine_table, sine_table, 1.0))
    key_rows = low(rotate(low_back(matmul(normed_one, key_matrix)), cosine_table, sine_table, 1.0))
    value_rows = low(low_back(matmul(normed_one, value_matrix)))
    attended = low(low_back(attention(query_rows, key_rows, value_rows, blocks)))
    middle = inputs + low_back(matmul(attended, output_weight))
    norm_two = lax.rsqrt(lax.optimization_barrier(jnp.mean(middle * middle, axis=-1, keepdims=True)) + epsilon)
    normed_two = low(middle * norm_two * ffn_gain)
    gate = low_back(matmul(normed_two, gate_weight))
    upper = low_back(matmul(normed_two, up_weight))
    active = low(jax.nn.silu(gate) * upper)
    return middle + matmul(active, down_weight.T)

def reference(layer_input, attn_gain, query_weight, key_matrix, value_matrix, output_weight, ffn_gain, gate_weight, up_weight, down_weight, block_ids, cotangent):
    params = tuple((matrix.astype(jnp.float32) for matrix in (attn_gain, query_weight, key_matrix, value_matrix, output_weight, ffn_gain, gate_weight, up_weight, down_weight)))

    def one_sequence(totals, inputs):
        sequence, blocks, upstream = inputs

        def forward(value_rows, *weights):
            return layer(value_rows, *weights, blocks)
        output, pullback = jax.vjp(forward, sequence.astype(jnp.float32), *params)
        grads = pullback(upstream.astype(jnp.float32))
        totals = jax.tree.map(jnp.add, totals, tuple(grads[1:]))
        return (totals, (output, grads[0]))
    zeros = tuple((jnp.zeros_like(matrix) for matrix in params))
    totals, (outputs, input_grads) = lax.scan(one_sequence, zeros, (layer_input, block_ids, cotangent))
    return (outputs, input_grads, totals[0], totals[1], totals[2], totals[3], totals[4], totals[5], totals[6], totals[7], totals[8])
```

```python
import itertools

import jax
import jax.numpy as jnp
from jax import lax
from jax.experimental import pallas as pl
from jax.experimental.pallas import tpu as pltpu
from jax.sharding import Mesh
from jax.sharding import PartitionSpec as P

QUERY_HEADS = 32
KEY_HEADS = 8
HEAD_DIM = 64
TEAM = 16
SCALE = HEAD_DIM ** (-0.5)
epsilon = 1e-05
rope_base = 500000.0
NT = (((1,), (1,)), ((), ()))
TN = (((0,), (0,)), ((), ()))
TEAM_AXES = ("z", "y", "c", "x")
ALL = ("dp",) + TEAM_AXES

DIMS = ("z", "y", "c", "x")
WEIGHT = {"z": 8, "y": 4, "c": 2, "x": 1}
LINKS = ("x", "y", "z")
ORDERS = (("x", "y", "z"), ("y", "z", "x"), ("z", "x", "y"))
MESH = pl.DeviceIdType.MESH


def part_rows(rows):
    tiles = rows // 16
    base = [tiles // 3 + (1 if i < tiles % 3 else 0) for i in range(3)]
    out, at = [], 0
    for b in base:
        out.append((at * 16, b * 16))
        at += b
    return out


def coords():
    return {d: lax.axis_index(d) for d in DIMS}


def slot_of(me, flips=()):
    return sum(((1 - me[d]) if d in flips else me[d]) * WEIGHT[d] for d in DIMS)


def greet(me):
    barrier = pltpu.get_barrier_semaphore()
    for d in DIMS:
        pl.semaphore_signal(barrier, inc=1, device_id={d: 1 - me[d]}, device_id_type=MESH)
    pl.semaphore_wait(barrier, len(DIMS))


def ag_kernel(x_ref, g_ref, ssem, rsem, lsem):
    me = coords()
    rows = x_ref.shape[0]
    parts = part_rows(rows)
    greet(me)
    mine = slot_of(me)
    local = pltpu.make_async_copy(x_ref, g_ref.at[mine], lsem)
    local.start()
    counter = itertools.count()
    copies = []

    def send(flips, r0, rn, dim, own):
        i = next(counter)
        s = slot_of(me, flips)
        src = x_ref.at[pl.ds(r0, rn)] if own else g_ref.at[s, pl.ds(r0, rn)]
        cp = pltpu.make_async_remote_copy(
            src_ref=src, dst_ref=g_ref.at[s, pl.ds(r0, rn)],
            send_sem=ssem.at[i], recv_sem=rsem.at[i],
            device_id={dim: 1 - me[dim]}, device_id_type=MESH)
        cp.start()
        copies.append(cp)
        return cp

    step1, step2, step3 = {}, {}, {}
    for p, (r0, rn) in enumerate(parts):
        step1[p] = [send((), r0, rn, ORDERS[p][0], True)]
    for p, (r0, rn) in enumerate(parts):
        step2[p] = [send((), r0, rn, ORDERS[p][1], True)]
    for p, (r0, rn) in enumerate(parts):
        step3[p] = [send((), r0, rn, ORDERS[p][2], True)]
    core = [send((), 0, rows, "c", True)]
    for p, (r0, rn) in enumerate(parts):
        a, b, c = ORDERS[p]
        step1[p][0].wait_recv()
        step2[p].append(send((a,), r0, rn, b, False))
        step3[p].append(send((a,), r0, rn, c, False))
        core.append(send((a,), r0, rn, "c", False))
    for p, (r0, rn) in enumerate(parts):
        a, b, c = ORDERS[p]
        for cp, fl in zip(step2[p], ((b,), (a, b))):
            cp.wait_recv()
            step3[p].append(send(fl, r0, rn, c, False))
            core.append(send(fl, r0, rn, "c", False))
    for p, (r0, rn) in enumerate(parts):
        a, b, c = ORDERS[p]
        for cp, fl in zip(step3[p], ((c,), (a, c), (b, c), (a, b, c))):
            cp.wait_recv()
            core.append(send(fl, r0, rn, "c", False))
    for cp in core:
        cp.wait_recv()
    for cp in copies:
        cp.wait_send()
    local.wait()


def all_gather16(x, cid=1):
    rows, cols = x.shape
    return pl.pallas_call(
        ag_kernel,
        out_shape=jax.ShapeDtypeStruct((16, rows, cols), x.dtype),
        in_specs=[pl.BlockSpec(memory_space=pltpu.VMEM)],
        out_specs=pl.BlockSpec(memory_space=pltpu.VMEM),
        scratch_shapes=[pltpu.SemaphoreType.DMA((64,)), pltpu.SemaphoreType.DMA((64,)), pltpu.SemaphoreType.DMA],
        compiler_params=pltpu.CompilerParams(collective_id=cid, has_side_effects=True, vmem_limit_bytes=50 << 20),
    )(x)


FULL = list(itertools.product((0, 1), repeat=3))


def flips_of(bits, order):
    return tuple(d for b, d in zip(bits, order) if b)


def add_rows(dst, a, b, r0, rn):
    def body(i, _):
        r = pl.multiple_of(r0 + i * 16, 16)
        dst[pl.ds(r, 16)] = (a[pl.ds(r, 16)].astype(jnp.float32) + b[pl.ds(r, 16)].astype(jnp.float32)).astype(dst.dtype)
        return 0
    lax.fori_loop(0, rn // 16, body, 0)


def rs_kernel(p_ref, o_ref, acc, cbuf, b1, b2, b3, ssem, rsem):
    me = coords()
    rows = p_ref.shape[1]
    parts = part_rows(rows)
    greet(me)
    counter = itertools.count()
    copies = []

    def send(src, dst, dim):
        i = next(counter)
        cp = pltpu.make_async_remote_copy(
            src_ref=src, dst_ref=dst, send_sem=ssem.at[i], recv_sem=rsem.at[i],
            device_id={dim: 1 - me[dim]}, device_id_type=MESH)
        cp.start()
        copies.append(cp)
        return cp

    def key(flips):
        return sum((1 << i) for i, d in enumerate(LINKS) if d in flips)

    order0 = [(1, 1, 1), (0, 1, 1), (1, 0, 1), (1, 1, 0), (1, 0, 0), (0, 1, 0), (0, 0, 1), (0, 0, 0)]
    core = {}
    for bits in order0:
        fl = flips_of(bits, LINKS)
        core[fl] = send(p_ref.at[slot_of(me, fl + ("c",))], cbuf.at[key(fl)], "c")
    s1 = {p: {} for p in range(3)}
    for bits in order0:
        fl = flips_of(bits, LINKS)
        core[fl].wait_recv()
        k = key(fl)
        add_rows(acc.at[k], p_ref.at[slot_of(me, fl)], cbuf.at[k], 0, rows)
        for p, (r0, rn) in enumerate(parts):
            a, b, c = ORDERS[p]
            if a in fl:
                rest = tuple(d for d in fl if d != a)
                j = (1 if b in fl else 0) + (2 if c in fl else 0)
                s1[p][rest] = send(acc.at[k, pl.ds(r0, rn)], b1.at[j, pl.ds(r0, rn)], a)
    s2 = {p: {} for p in range(3)}
    for (bb, cc) in ((1, 1), (1, 0), (0, 1), (0, 0)):
        for p, (r0, rn) in enumerate(parts):
            a, b, c = ORDERS[p]
            fl = flips_of((bb, cc), (b, c))
            match = [q for q in s1[p] if set(q) == set(fl)][0]
            s1[p][match].wait_recv()
            k = key(fl)
            add_rows(acc.at[k], acc.at[k], b1.at[bb + 2 * cc], r0, rn)
            if bb:
                s2[p][cc] = send(acc.at[k, pl.ds(r0, rn)], b2.at[cc, pl.ds(r0, rn)], b)
    s3 = {}
    for cc in (1, 0):
        for p, (r0, rn) in enumerate(parts):
            a, b, c = ORDERS[p]
            s2[p][cc].wait_recv()
            k = key((c,) if cc else ())
            add_rows(acc.at[k], acc.at[k], b2.at[cc], r0, rn)
            if cc:
                s3[p] = send(acc.at[k, pl.ds(r0, rn)], b3.at[pl.ds(r0, rn)], c)
    for p, (r0, rn) in enumerate(parts):
        s3[p].wait_recv()
        add_rows(o_ref, acc.at[0], b3, r0, rn)
    for cp in copies:
        cp.wait_send()


def reduce_scatter16(p, cid=2, out_dtype=jnp.float32):
    _, rows, cols = p.shape
    return pl.pallas_call(
        rs_kernel,
        out_shape=jax.ShapeDtypeStruct((rows, cols), out_dtype),
        in_specs=[pl.BlockSpec(memory_space=pltpu.VMEM)],
        out_specs=pl.BlockSpec(memory_space=pltpu.VMEM),
        scratch_shapes=[
            pltpu.VMEM((8, rows, cols), p.dtype), pltpu.VMEM((8, rows, cols), p.dtype),
            pltpu.VMEM((4, rows, cols), p.dtype), pltpu.VMEM((2, rows, cols), p.dtype), pltpu.VMEM((rows, cols), p.dtype),
            pltpu.SemaphoreType.DMA((32,)), pltpu.SemaphoreType.DMA((32,))],
        compiler_params=pltpu.CompilerParams(collective_id=cid, has_side_effects=True, vmem_limit_bytes=56 << 20),
    )(p)
NEG = -1e30
Q_CHUNK = 256
K_CHUNK = 512


def attend_kernel(count_ref, q_ref, k_ref, v_ref, qid_ref, kid_ref, o_ref, lse_ref):
    s, i = pl.program_id(0), pl.program_id(1)
    heads, chunk, width = q_ref.shape[1:]
    rows = heads * chunk
    q = q_ref[0].reshape(rows, width)
    qid = qid_ref[0]
    qids = jnp.concatenate([qid] * heads, axis=0)

    def step(j, state):
        top, total, acc = state
        at = pl.multiple_of(j * K_CHUNK, K_CHUNK)
        k = k_ref[0, pl.ds(at, K_CHUNK), :]
        v = v_ref[0, pl.ds(at, K_CHUNK), :]
        kid = kid_ref[0, :, pl.ds(at, K_CHUNK)]
        scores = lax.dot_general(q, k, NT, preferred_element_type=jnp.float32) * SCALE
        scores = jnp.where(kid <= qids, scores, NEG)
        new_top = jnp.maximum(top, jnp.max(scores, axis=-1, keepdims=True))
        p = jnp.exp(scores - new_top)
        factor = jnp.exp(top - new_top)
        total = total * factor + jnp.sum(p, axis=-1, keepdims=True)
        acc = acc * factor + jnp.dot(p.astype(jnp.bfloat16), v, preferred_element_type=jnp.float32)
        return new_top, total, acc

    start = (
        jnp.full((rows, 1), NEG, jnp.float32),
        jnp.zeros((rows, 1), jnp.float32),
        jnp.zeros((rows, width), jnp.float32),
    )
    top, total, acc = lax.fori_loop(0, count_ref[s, i], step, start)
    o_ref[0] = (acc / total).astype(jnp.bfloat16).reshape(heads, chunk, width)
    lse_ref[0] = (top + jnp.log(total)).reshape(heads, chunk, 1)


def attend(counts, q, k, v, qid, kid):
    seqs, heads, n, width = q.shape
    keys = k.shape[1]
    spec = pltpu.PrefetchScalarGridSpec(
        num_scalar_prefetch=1,
        grid=(seqs, n // Q_CHUNK),
        in_specs=[
            pl.BlockSpec((1, heads, Q_CHUNK, width), lambda s, i, c: (s, 0, i, 0)),
            pl.BlockSpec((1, keys, width), lambda s, i, c: (s, 0, 0)),
            pl.BlockSpec((1, keys, width), lambda s, i, c: (s, 0, 0)),
            pl.BlockSpec((1, Q_CHUNK, 1), lambda s, i, c: (s, i, 0)),
            pl.BlockSpec((1, 1, keys), lambda s, i, c: (s, 0, 0)),
        ],
        out_specs=[
            pl.BlockSpec((1, heads, Q_CHUNK, width), lambda s, i, c: (s, 0, i, 0)),
            pl.BlockSpec((1, heads, Q_CHUNK, 1), lambda s, i, c: (s, 0, i, 0)),
        ],
    )
    return pl.pallas_call(
        attend_kernel,
        grid_spec=spec,
        out_shape=[
            jax.ShapeDtypeStruct(q.shape, jnp.bfloat16),
            jax.ShapeDtypeStruct((seqs, heads, n, 1), jnp.float32),
        ],
        compiler_params=pltpu.CompilerParams(vmem_limit_bytes=48 << 20),
    )(counts, q, k, v, qid, kid)


def attend_back_kernel(count_ref, q_ref, g_ref, lse_ref, delta_ref, k_ref, v_ref, qid_ref, kid_ref, dq_ref, dk_ref, dv_ref):
    s, i = pl.program_id(0), pl.program_id(1)
    heads, chunk, width = q_ref.shape[1:]
    rows = heads * chunk
    q = q_ref[0].reshape(rows, width)
    g = g_ref[0].reshape(rows, width)
    lse = jnp.concatenate([lse_ref[0, h] for h in range(heads)], axis=1)
    delta = jnp.concatenate([delta_ref[0, h] for h in range(heads)], axis=1)
    qids = jnp.concatenate([qid_ref[0]] * heads, axis=1)

    @pl.when(i == 0)
    def _():
        dk_ref[...] = jnp.zeros_like(dk_ref)
        dv_ref[...] = jnp.zeros_like(dv_ref)

    def step(j, dq):
        at = pl.multiple_of(j * K_CHUNK, K_CHUNK)
        here = pl.ds(at, K_CHUNK)
        k = k_ref[0, here, :]
        v = v_ref[0, here, :]
        kid = kid_ref[0, here, :]
        scores = lax.dot_general(k, q, NT, preferred_element_type=jnp.float32) * SCALE
        p = jnp.where(kid <= qids, jnp.exp(scores - lse), 0.0)
        dp = lax.dot_general(v, g, NT, preferred_element_type=jnp.float32)
        ds = (p * (dp - delta)).astype(jnp.bfloat16)
        dv_ref[0, here, :] += jnp.dot(p.astype(jnp.bfloat16), g, preferred_element_type=jnp.float32)
        dk_ref[0, here, :] += jnp.dot(ds, q, preferred_element_type=jnp.float32) * SCALE
        return dq + lax.dot_general(ds, k, TN, preferred_element_type=jnp.float32)

    dq = lax.fori_loop(0, count_ref[s, i], step, jnp.zeros((rows, width), jnp.float32))
    dq_ref[0] = (dq * SCALE).reshape(heads, chunk, width)


def attend_back(counts, q, g, lse, delta, k, v, qid, kid):
    seqs, heads, n, width = q.shape
    keys = k.shape[1]
    wide = pl.BlockSpec((1, heads, Q_CHUNK, width), lambda s, i, c: (s, 0, i, 0))
    row = pl.BlockSpec((1, heads, 1, Q_CHUNK), lambda s, i, c: (s, 0, 0, i))
    whole = pl.BlockSpec((1, keys, width), lambda s, i, c: (s, 0, 0))
    spec = pltpu.PrefetchScalarGridSpec(
        num_scalar_prefetch=1,
        grid=(seqs, n // Q_CHUNK),
        in_specs=[
            wide, wide, row, row, whole, whole,
            pl.BlockSpec((1, 1, Q_CHUNK), lambda s, i, c: (s, 0, i)),
            pl.BlockSpec((1, keys, 1), lambda s, i, c: (s, 0, 0)),
        ],
        out_specs=[wide, whole, whole],
    )
    return pl.pallas_call(
        attend_back_kernel,
        grid_spec=spec,
        out_shape=[
            jax.ShapeDtypeStruct(q.shape, jnp.float32),
            jax.ShapeDtypeStruct(k.shape, jnp.float32),
            jax.ShapeDtypeStruct(k.shape, jnp.float32),
        ],
        compiler_params=pltpu.CompilerParams(vmem_limit_bytes=56 << 20),
    )(counts, q, g, lse, delta, k, v, qid, kid)


def rotation_tables(positions):
    half = HEAD_DIM // 2
    freqs = rope_base ** (-jnp.arange(half, dtype=jnp.float32) * 2.0 / HEAD_DIM)
    angles = positions.astype(jnp.float32)[:, None] * freqs[None, :]
    return jnp.cos(angles), jnp.sin(angles)


def rotate(values, cosine, sine):
    half = HEAD_DIM // 2
    first, second = values[..., :half], values[..., half:]
    return jnp.concatenate([first * cosine - second * sine, second * cosine + first * sine], axis=-1)


def norm_back(grad, normed, scale):
    return scale * (grad - normed * jnp.mean(grad * normed, axis=-1, keepdims=True))


def exchange(x):
    return lax.all_to_all(x, ALL, split_axis=0, concat_axis=0, tiled=True)


def local(
    layer_input, attn_gain, query_weight, key_matrix, value_matrix, output_weight, ffn_gain,
    gate_weight, up_weight, down_weight, block_ids, cotangent,
):
    f32, bf16 = jnp.float32, jnp.bfloat16
    seqs, tokens, model = layer_input.shape
    rows = seqs * tokens
    groups = lax.axis_size("dp")
    group = lax.axis_index("dp")
    devices = groups * TEAM
    share = query_weight.shape[0]
    span = TEAM * tokens
    heads = QUERY_HEADS // TEAM
    ff = gate_weight.shape[1] // TEAM
    twin = TEAM // KEY_HEADS

    gain_one = attn_gain.astype(f32)[:, None]
    gain_two = ffn_gain.astype(f32)[:, None]

    def scaled(weight, gain):
        return (weight.astype(f32) * gain).astype(bf16)

    def send_out(piece):
        piece = jnp.moveaxis(piece, 1, 0)
        return exchange(jnp.broadcast_to(piece[None], (groups,) + piece.shape).reshape((devices,) + piece.shape[1:]))

    def doubled(weight):
        split = weight.reshape(share, KEY_HEADS, 1, HEAD_DIM)
        return jnp.broadcast_to(split, (share, KEY_HEADS, twin, HEAD_DIM)).reshape(share, TEAM, HEAD_DIM)

    w_in = send_out(
        jnp.concatenate(
            [
                scaled(query_weight, gain_one).reshape(share, TEAM, heads * HEAD_DIM),
                doubled(scaled(key_matrix, gain_one)),
                doubled(scaled(value_matrix, gain_one)),
            ],
            axis=-1,
        )
    ).reshape(model, -1)
    w_ffn = send_out(
        jnp.concatenate(
            [
                scaled(gate_weight, gain_two).reshape(share, TEAM, ff),
                scaled(up_weight, gain_two).reshape(share, TEAM, ff),
                down_weight.reshape(share, TEAM, ff),
            ],
            axis=-1,
        )
    ).reshape(model, -1)
    w_gate_up, w_down = w_ffn[:, : 2 * ff], w_ffn[:, 2 * ff :]
    deal = [(j, (j % groups) * TEAM + j // groups) for j in range(devices)]
    w_out = lax.all_gather(lax.ppermute(output_weight, ALL, deal), "dp", axis=0, tiled=True)

    x = layer_input.reshape(rows, model).astype(f32)
    norm_one = lax.rsqrt(jnp.mean(x * x, axis=-1, keepdims=True) + epsilon)
    normed_one = x * norm_one
    c_own = cotangent.reshape(rows, model)
    h_one = all_gather16(normed_one.astype(bf16)).reshape(-1, model)
    c_all = all_gather16(c_own).reshape(-1, model)

    def by_sequence(piece, count):
        piece = piece.reshape(TEAM, seqs, tokens, count, HEAD_DIM)
        return piece.transpose(1, 3, 0, 2, 4).reshape(seqs, count, span, HEAD_DIM)

    def by_device(piece):
        count = piece.shape[1]
        piece = piece.reshape(seqs, count, TEAM, tokens, HEAD_DIM)
        return piece.transpose(2, 0, 3, 1, 4).reshape(TEAM * rows, count * HEAD_DIM)

    cosine, sine = rotation_tables(group * span + jnp.arange(span, dtype=jnp.int32))
    raw = jnp.dot(h_one, w_in, preferred_element_type=f32)
    qk = by_sequence(raw[:, : (heads + 1) * HEAD_DIM], heads + 1)
    qk = rotate(qk, cosine, sine).astype(bf16)
    q, k_own = qk[:, :heads], qk[:, heads]
    v_own = by_sequence(raw[:, (heads + 1) * HEAD_DIM :].astype(bf16), 1)[:, 0]
    kv = lax.all_gather(jnp.concatenate([k_own, v_own], axis=-1), "dp", axis=1, tiled=True)
    k, v = kv[..., :HEAD_DIM], kv[..., HEAD_DIM:]
    ids = lax.dynamic_slice_in_dim(block_ids, group * span, span, 1)
    counts = jnp.sum(
        block_ids[:, None, ::K_CHUNK] <= ids[:, Q_CHUNK - 1 :: Q_CHUNK, None], axis=-1
    ).astype(jnp.int32)
    o, lse = attend(counts, q, k, v, ids[:, :, None], block_ids[:, None, :])
    o_all = by_device(o)
    branch = reduce_scatter16(jnp.dot(o_all, w_out, preferred_element_type=f32).astype(bf16).reshape(TEAM, rows, model))
    middle = x + branch
    norm_two = lax.rsqrt(jnp.mean(middle * middle, axis=-1, keepdims=True) + epsilon)
    normed_two = middle * norm_two
    h_two = all_gather16(normed_two.astype(bf16)).reshape(-1, model)
    gate_up = jnp.dot(h_two, w_gate_up, preferred_element_type=f32)
    gate, up = gate_up[:, :ff], gate_up[:, ff:]
    sig = jax.nn.sigmoid(gate)
    silu = gate * sig
    active = (silu * up).astype(bf16)
    da = jnp.dot(c_all, w_down, preferred_element_type=f32)
    d_gate_up = jnp.concatenate(
        [(da * up * sig * (1.0 + gate * (1.0 - sig))).astype(bf16), (da * silu).astype(bf16)], axis=-1
    )
    produced = reduce_scatter16(
        lax.dot_general(active, w_down, NT, preferred_element_type=f32).astype(bf16).reshape(TEAM, rows, model)
    )
    layer_output = (middle + produced).reshape(seqs, tokens, model)
    dn_two = reduce_scatter16(
        lax.dot_general(d_gate_up, w_gate_up, NT, preferred_element_type=f32).astype(bf16).reshape(TEAM, rows, model)
    )
    middle_grad = c_own.astype(f32) + norm_back(dn_two, normed_two, norm_two)
    middle_low = all_gather16(middle_grad.astype(bf16)).reshape(-1, model)
    do = lax.dot_general(middle_low, w_out, NT, preferred_element_type=f32).astype(bf16)
    g = by_sequence(do, heads)
    delta = jnp.sum(g.astype(f32) * o.astype(f32), axis=-1)
    dq, dk, dv = attend_back(
        counts, q, g, lse.reshape(seqs, heads, 1, span), delta.reshape(seqs, heads, 1, span), k, v,
        ids[:, None, :], block_ids[:, :, None],
    )
    dkv = jnp.concatenate([dk, dv], axis=-1).astype(bf16).reshape(seqs, groups, span, 2 * HEAD_DIM)
    dkv = lax.all_to_all(dkv, "dp", split_axis=1, concat_axis=1, tiled=True)
    dkv = jnp.sum(dkv.astype(f32), axis=1)
    dqk = rotate(jnp.concatenate([dq, dkv[:, None, :, :HEAD_DIM]], axis=1), cosine, -sine)
    d_in = by_device(jnp.concatenate([dqk, dkv[:, None, :, HEAD_DIM:]], axis=1).astype(bf16))
    dn_one = reduce_scatter16(
        lax.dot_general(d_in, w_in, NT, preferred_element_type=f32).astype(bf16).reshape(TEAM, rows, model)
    )
    input_grad = (middle_grad + norm_back(dn_one, normed_one, norm_one)).reshape(seqs, tokens, model)

    def outer(left, right):
        return lax.dot_general(left, right, TN, preferred_element_type=f32)

    def gather_sum(piece):
        piece = exchange(piece.astype(bf16).reshape(devices, share, piece.shape[-1]))
        piece = jnp.sum(piece.reshape(groups, TEAM, share, -1).astype(f32), axis=0)
        return jnp.moveaxis(piece, 0, 1)

    ffn = gather_sum(jnp.concatenate([outer(h_two, d_gate_up), outer(c_all, active)], axis=-1))
    grad_gate = ffn[..., :ff].reshape(share, -1) * gain_two
    grad_up = ffn[..., ff : 2 * ff].reshape(share, -1) * gain_two
    grad_down = ffn[..., 2 * ff :].reshape(share, -1)
    attn = gather_sum(outer(h_one, d_in))
    cut = heads * HEAD_DIM
    grad_query = attn[..., :cut].reshape(share, -1) * gain_one
    pair = attn[..., cut:].reshape(share, KEY_HEADS, twin, 2, HEAD_DIM).sum(axis=2)
    grad_key = pair[:, :, 0].reshape(share, -1) * gain_one
    grad_value = pair[:, :, 1].reshape(share, -1) * gain_one
    w_out_part = outer(o_all, middle_low).astype(bf16).reshape(groups, -1, model)
    w_out_part = lax.all_to_all(w_out_part, "dp", split_axis=0, concat_axis=0, tiled=True)
    grad_output = lax.ppermute(
        jnp.sum(w_out_part.astype(f32), axis=0), ALL, [(b, a) for a, b in deal]
    )
    gains = jnp.stack(
        [jnp.sum(normed_one * dn_one, axis=0), jnp.sum(normed_two * dn_two, axis=0)], axis=0
    )
    gains = exchange(gains.reshape(2, devices, share).transpose(1, 0, 2)).sum(axis=0)
    return (
        layer_output, input_grad, gains[0] / gain_one[:, 0], grad_query, grad_key, grad_value, grad_output,
        gains[1] / gain_two[:, 0], grad_gate, grad_up, grad_down,
    )


def solution(mesh):
    fine = Mesh(mesh.devices.reshape(-1, 2, 2, 2, 2), ALL)
    token = P(None, ALL, None)
    row = P(ALL, None)
    vec = P(ALL)
    in_specs = (token, vec, row, row, row, row, vec, row, row, row, P(), token)
    out_specs = (token, token, vec, row, row, row, row, vec, row, row, row)
    return jax.shard_map(local, mesh=fine, in_specs=in_specs, out_specs=out_specs, check_vma=False)
```

```python
import functools
import itertools

import jax
import jax.numpy as jnp
from jax import lax
from jax.experimental import pallas as pl
from jax.experimental.pallas import tpu as pltpu
from jax.sharding import Mesh
from jax.sharding import PartitionSpec as P

QUERY_HEADS = 32
KEY_HEADS = 8
HEAD_DIM = 64
TEAM = 16
SCALE = HEAD_DIM ** (-0.5)
epsilon = 1e-05
rope_base = 500000.0
NT = (((1,), (1,)), ((), ()))
TN = (((0,), (0,)), ((), ()))
TEAM_AXES = ("z", "y", "c", "x")
ALL = ("dp",) + TEAM_AXES

DIMS = ("z", "y", "c", "x")
WEIGHT = {"z": 8, "y": 4, "c": 2, "x": 1}
LINKS = ("x", "y", "z")
ORDERS = (("x", "y", "z"), ("y", "z", "x"), ("z", "x", "y"))
MESH = pl.DeviceIdType.MESH


def part_rows(rows):
    tiles = rows // 16
    base = [tiles // 3 + (1 if i < tiles % 3 else 0) for i in range(3)]
    out, at = [], 0
    for b in base:
        out.append((at * 16, b * 16))
        at += b
    return out


def coords():
    return {d: lax.axis_index(d) for d in DIMS}


def slot_of(me, flips=()):
    return sum(((1 - me[d]) if d in flips else me[d]) * WEIGHT[d] for d in DIMS)


def greet(groups, team=True):
    barrier = pltpu.get_barrier_semaphore()
    me = coords()
    group = lax.axis_index("dp")
    if team:
        for d in DIMS:
            pl.semaphore_signal(barrier, inc=1, device_id={d: 1 - me[d]}, device_id_type=MESH)
    for k in range(1, groups):
        pl.semaphore_signal(barrier, inc=1, device_id={"dp": lax.rem(group + k, groups)}, device_id_type=MESH)
    pl.semaphore_wait(barrier, groups - 1 + (len(DIMS) if team else 0))


COST = pl.CostEstimate(flops=30_000_000_000, bytes_accessed=1 << 20, transcendentals=0)


class Errand:
    def __init__(self, array, first, count, own_block):
        self.arrays, self.first, self.count, self.own_block = [array], first, count, own_block
        self.steps = 0

    def outputs(self, groups):
        a = self.arrays[0]
        return [jax.ShapeDtypeStruct((max(groups - 1, 1), self.count, a.shape[-1]), a.dtype)]

    def in_specs(self):
        return [anywhere()]

    def out_specs(self, groups):
        return [anywhere()]

    def scratch(self, groups):
        n = max(1, groups - 1)
        return [pltpu.SemaphoreType.DMA((n,)), pltpu.SemaphoreType.DMA((n,))]

    def bind(self, groups, src, dst, scratch):
        me = lax.axis_index("dp")
        here = pl.ds(self.first, self.count)
        self.copies = []
        for k in range(1, groups):
            peer = lax.rem(me + k, groups)
            self.copies.append(
                pltpu.make_async_remote_copy(
                    src_ref=src[0].at[peer, here] if self.own_block else src[0].at[here],
                    dst_ref=dst[0].at[k - 1], send_sem=scratch[0].at[k - 1], recv_sem=scratch[1].at[k - 1],
                    device_id={"dp": peer}, device_id_type=MESH,
                )
            )

    def step(self, k):
        if k == 0:
            for cp in self.copies:
                cp.start()

    def finish(self):
        for cp in self.copies:
            cp.wait()


class Swap:
    def __init__(self, array, order, far=False):
        self.shape = array.shape[1:]
        self.arrays, self.order, self.far = [array.reshape((2, 2, 2, 2) + self.shape)], order, far
        self.steps = 5

    def outputs(self, groups):
        a = self.arrays[0]
        out = [jax.ShapeDtypeStruct(a.shape, a.dtype)]
        return out + [jax.ShapeDtypeStruct((max(groups - 1, 1),) + a.shape, a.dtype)] * self.far

    def in_specs(self):
        return [vmem()]

    def out_specs(self, groups):
        return [vmem()] + [anywhere()] * self.far

    def scratch(self, groups):
        a = self.arrays[0]
        n = max(1, groups - 1)
        sem = pltpu.SemaphoreType.DMA
        return [pltpu.VMEM(a.shape, a.dtype)] * 3 + [sem((4,)), sem((4,)), sem((4,)), sem((n,)), sem((n,))]

    def bind(self, groups, src, dst, scratch):
        me = coords()
        chain = [src[0], scratch[0], scratch[1], scratch[2], dst[0]]
        ssem, rsem, lsem, fs, fr = scratch[3:]
        self.moves, self.tail = [], []
        for k, d in enumerate(self.order):
            lead = (slice(None),) * DIMS.index(d)
            a, z = chain[k], chain[k + 1]
            self.moves.append(
                (
                    pltpu.make_async_remote_copy(
                        src_ref=a.at[lead + (1 - me[d],)], dst_ref=z.at[lead + (me[d],)], send_sem=ssem.at[k],
                        recv_sem=rsem.at[k], device_id={d: 1 - me[d]}, device_id_type=MESH,
                    ),
                    pltpu.make_async_copy(a.at[lead + (me[d],)], z.at[lead + (me[d],)], lsem.at[k]),
                )
            )
        if self.far:
            group = lax.axis_index("dp")
            for k in range(1, groups):
                self.tail.append(
                    pltpu.make_async_remote_copy(
                        src_ref=dst[0], dst_ref=dst[1].at[k - 1], send_sem=fs.at[k - 1], recv_sem=fr.at[k - 1],
                        device_id={"dp": lax.rem(group + k, groups)}, device_id_type=MESH,
                    )
                )

    def step(self, k):
        if 0 < k <= 4:
            self.moves[k - 1][0].wait_recv()
            self.moves[k - 1][1].wait()
        if k < 4:
            self.moves[k][0].start()
            self.moves[k][1].start()
        if k == 4:
            for cp in self.tail:
                cp.start()

    def finish(self):
        for cp, _ in self.moves:
            cp.wait_send()
        for cp in self.tail:
            cp.wait()


class Runner:
    def __init__(self, jobs):
        self.jobs, self.k = jobs, 0

    def tick(self):
        for job in self.jobs:
            if self.k == 0 or self.k < job.steps:
                job.step(self.k)
        self.k += 1

    def finish(self):
        while self.k < max([1] + [job.steps for job in self.jobs]):
            self.tick()
        for job in self.jobs:
            job.finish()


def anywhere():
    return pl.BlockSpec(memory_space=pl.ANY)


def vmem():
    return pl.BlockSpec(memory_space=pltpu.VMEM)


def call(body, inputs, outputs, scratch, jobs, cid, limit=58):
    groups = lax.axis_size("dp")
    jobs = list(jobs)
    n_in, n_out, n_scratch = len(inputs), len(outputs), len(scratch)
    job_in = [a for job in jobs for a in job.arrays]
    job_out = [job.outputs(groups) for job in jobs]
    job_scratch = [job.scratch(groups) for job in jobs]

    def kernel(*refs):
        def take(n):
            nonlocal refs
            head, refs = refs[:n], refs[n:]
            return head

        ins = take(n_in)
        src = [take(len(job.arrays)) for job in jobs]
        outs = take(n_out)
        dst = [take(len(o)) for o in job_out]
        scr = take(n_scratch)
        own = [take(len(o)) for o in job_scratch]
        greet(groups)
        for job, a, z, m in zip(jobs, src, dst, own):
            job.bind(groups, a, z, m)
        run = Runner(jobs)
        run.tick()
        body(groups, run.tick, *ins, *outs, *scr)
        run.finish()

    out = pl.pallas_call(
        kernel,
        out_shape=list(outputs) + [o for each in job_out for o in each],
        in_specs=[vmem()] * n_in + [p for job in jobs for p in job.in_specs()],
        out_specs=[vmem()] * n_out + [p for job in jobs for p in job.out_specs(groups)],
        scratch_shapes=list(scratch) + [o for each in job_scratch for o in each],
        cost_estimate=COST,
        compiler_params=pltpu.CompilerParams(collective_id=cid, has_side_effects=True, vmem_limit_bytes=limit << 20),
    )(*inputs, *job_in)
    main, rest = out[:n_out], list(out[n_out:])
    got = []
    for o in job_out:
        got.append(tuple(rest[: len(o)]))
        rest = rest[len(o) :]
    return main, got


def ag_kernel(groups, tick, x_ref, g_ref, ssem, rsem, lsem):
    me = coords()
    rows = x_ref.shape[0]
    parts = part_rows(rows)
    mine = slot_of(me)
    local = pltpu.make_async_copy(x_ref, g_ref.at[mine], lsem)
    local.start()
    counter = itertools.count()
    copies = []

    def send(flips, r0, rn, dim, own):
        i = next(counter)
        s = slot_of(me, flips)
        src = x_ref.at[pl.ds(r0, rn)] if own else g_ref.at[s, pl.ds(r0, rn)]
        cp = pltpu.make_async_remote_copy(
            src_ref=src, dst_ref=g_ref.at[s, pl.ds(r0, rn)],
            send_sem=ssem.at[i], recv_sem=rsem.at[i],
            device_id={dim: 1 - me[dim]}, device_id_type=MESH)
        cp.start()
        copies.append(cp)
        return cp

    step1, step2, step3 = {}, {}, {}
    for p, (r0, rn) in enumerate(parts):
        step1[p] = [send((), r0, rn, ORDERS[p][0], True)]
    for p, (r0, rn) in enumerate(parts):
        step2[p] = [send((), r0, rn, ORDERS[p][1], True)]
    for p, (r0, rn) in enumerate(parts):
        step3[p] = [send((), r0, rn, ORDERS[p][2], True)]
    core = [send((), 0, rows, "c", True)]
    tick()
    for p, (r0, rn) in enumerate(parts):
        a, b, c = ORDERS[p]
        step1[p][0].wait_recv()
        step2[p].append(send((a,), r0, rn, b, False))
        step3[p].append(send((a,), r0, rn, c, False))
        core.append(send((a,), r0, rn, "c", False))
    for p, (r0, rn) in enumerate(parts):
        a, b, c = ORDERS[p]
        for cp, fl in zip(step2[p], ((b,), (a, b))):
            cp.wait_recv()
            step3[p].append(send(fl, r0, rn, c, False))
            core.append(send(fl, r0, rn, "c", False))
    tick()
    for p, (r0, rn) in enumerate(parts):
        a, b, c = ORDERS[p]
        for cp, fl in zip(step3[p], ((c,), (a, c), (b, c), (a, b, c))):
            cp.wait_recv()
            core.append(send(fl, r0, rn, "c", False))
    tick()
    for cp in core:
        cp.wait_recv()
    for cp in copies:
        cp.wait_send()
    local.wait()


def all_gather16(x, cid, jobs=()):
    rows, cols = x.shape
    out = call(
        ag_kernel, [x], [jax.ShapeDtypeStruct((TEAM, rows, cols), x.dtype)],
        [pltpu.SemaphoreType.DMA((64,)), pltpu.SemaphoreType.DMA((64,)), pltpu.SemaphoreType.DMA], jobs, cid,
    )
    return out[0][0], out[1]


FULL = list(itertools.product((0, 1), repeat=3))


def flips_of(bits, order):
    return tuple(d for b, d in zip(bits, order) if b)


def add_rows(dst, a, b, r0, rn):
    def body(i, _):
        r = pl.multiple_of(r0 + i * 16, 16)
        dst[pl.ds(r, 16)] = (a[pl.ds(r, 16)].astype(jnp.float32) + b[pl.ds(r, 16)].astype(jnp.float32)).astype(dst.dtype)
        return 0
    lax.fori_loop(0, rn // 16, body, 0)


def matmul_scatter_kernel(flip, groups, tick, a_ref, w_ref, o_ref, part, acc, cbuf, b1, b2, b3, ssem, rsem):
    me = coords()
    rows, cols = o_ref.shape
    parts = part_rows(rows)
    counter = itertools.count()
    copies = []

    def send(src, dst, dim):
        i = next(counter)
        cp = pltpu.make_async_remote_copy(
            src_ref=src, dst_ref=dst, send_sem=ssem.at[i], recv_sem=rsem.at[i],
            device_id={dim: 1 - me[dim]}, device_id_type=MESH)
        cp.start()
        copies.append(cp)
        return cp

    def product(slot, dst):
        def column(j, _):
            here = pl.ds(pl.multiple_of(j * 512, 512), 512)
            if flip:
                out = lax.dot_general(a_ref[slot], w_ref[here, :], NT, preferred_element_type=jnp.float32)
            else:
                out = jnp.dot(a_ref[slot], w_ref[:, here], preferred_element_type=jnp.float32)
            dst[:, here] = out.astype(dst.dtype)
            return 0
        lax.fori_loop(0, cols // 512, column, 0)

    def key(flips):
        return sum((1 << i) for i, d in enumerate(LINKS) if d in flips)

    order0 = [(1, 1, 1), (0, 1, 1), (1, 0, 1), (1, 1, 0), (1, 0, 0), (0, 1, 0), (0, 0, 1), (0, 0, 0)]
    core = {}
    for bits in order0:
        fl = flips_of(bits, LINKS)
        product(slot_of(me, fl + ("c",)), part.at[key(fl)])
        core[fl] = send(part.at[key(fl)], cbuf.at[key(fl)], "c")
    s1 = {p: {} for p in range(3)}
    tick()
    for bits in order0:
        fl = flips_of(bits, LINKS)
        k = key(fl)
        product(slot_of(me, fl), acc.at[k])
        core[fl].wait_recv()
        add_rows(acc.at[k], acc.at[k], cbuf.at[k], 0, rows)
        for p, (r0, rn) in enumerate(parts):
            a, b, c = ORDERS[p]
            if a in fl:
                rest = tuple(d for d in fl if d != a)
                j = (1 if b in fl else 0) + (2 if c in fl else 0)
                s1[p][rest] = send(acc.at[k, pl.ds(r0, rn)], b1.at[j, pl.ds(r0, rn)], a)
    tick()
    s2 = {p: {} for p in range(3)}
    for (bb, cc) in ((1, 1), (1, 0), (0, 1), (0, 0)):
        for p, (r0, rn) in enumerate(parts):
            a, b, c = ORDERS[p]
            fl = flips_of((bb, cc), (b, c))
            match = [q for q in s1[p] if set(q) == set(fl)][0]
            s1[p][match].wait_recv()
            k = key(fl)
            add_rows(acc.at[k], acc.at[k], b1.at[bb + 2 * cc], r0, rn)
            if bb:
                s2[p][cc] = send(acc.at[k, pl.ds(r0, rn)], b2.at[cc, pl.ds(r0, rn)], b)
    tick()
    s3 = {}
    for cc in (1, 0):
        for p, (r0, rn) in enumerate(parts):
            a, b, c = ORDERS[p]
            s2[p][cc].wait_recv()
            k = key((c,) if cc else ())
            add_rows(acc.at[k], acc.at[k], b2.at[cc], r0, rn)
            if cc:
                s3[p] = send(acc.at[k, pl.ds(r0, rn)], b3.at[pl.ds(r0, rn)], c)
    for p, (r0, rn) in enumerate(parts):
        s3[p].wait_recv()
        add_rows(o_ref, acc.at[0], b3, r0, rn)
    for cp in copies:
        cp.wait_send()


def matmul_scatter16(a, w, flip, cid, jobs=()):
    _, rows, _ = a.shape
    cols = w.shape[0] if flip else w.shape[1]
    bf16 = jnp.bfloat16
    out = call(
        functools.partial(matmul_scatter_kernel, flip), [a, w], [jax.ShapeDtypeStruct((rows, cols), jnp.float32)],
        [
            pltpu.VMEM((8, rows, cols), bf16), pltpu.VMEM((8, rows, cols), bf16), pltpu.VMEM((8, rows, cols), bf16),
            pltpu.VMEM((4, rows, cols), bf16), pltpu.VMEM((2, rows, cols), bf16), pltpu.VMEM((rows, cols), bf16),
            pltpu.SemaphoreType.DMA((32,)), pltpu.SemaphoreType.DMA((32,)),
        ],
        jobs, cid,
    )
    return out[0][0], out[1]


NEG = -1e30
CHUNK = 256
SLOTS = 4
CUTS = (5, 5, 6)
BACK_CUTS = (5, 4, 7)
SWAP_ORDERS = (("x", "y", "z", "c"), ("y", "z", "x", "c"), ("z", "x", "y", "c"))


def swapped(v):
    lane = lax.broadcasted_iota(jnp.int32, v.shape, 1)
    low = lax.rem(lane, HEAD_DIM) < HEAD_DIM // 2
    return jnp.where(low, pltpu.roll(v, 128 - HEAD_DIM // 2, 1), pltpu.roll(v, HEAD_DIM // 2, 1))


def low_lanes(shape):
    return lax.broadcasted_iota(jnp.int32, shape, 1) < HEAD_DIM


def as_row(column):
    return jnp.transpose(jnp.broadcast_to(column, (column.shape[0], 128)))[0:1]


def attend_kernel(groups, tick, h_ref, w_ref, cos_ref, sin_ref, idc_ref, idr_ref, q_ref, kv_ref, o_ref, lse_ref, top, total, acc, ssem, rsem):
    me = lax.axis_index("dp")
    tokens = cos_ref.shape[1]
    span = TEAM * tokens
    steps = span // CHUNK
    heads = q_ref.shape[0]

    def project(g, _):
        raw = jnp.dot(h_ref[g], w_ref[...], preferred_element_type=jnp.float32)
        cos = jnp.concatenate([cos_ref[g]] * 2, axis=0)
        sin = jnp.concatenate([sin_ref[g]] * 2, axis=0)
        qp, kvp = raw[:, :128], raw[:, 128:]
        qp = qp * cos[:, :128] + swapped(qp) * sin[:, :128]
        kvp = kvp * cos[:, 128:] + swapped(kvp) * sin[:, 128:]
        low = low_lanes(qp.shape)
        q_ref[0, g] = jnp.where(low, qp, 0.0).astype(jnp.bfloat16)
        q_ref[1, g] = jnp.where(low, pltpu.roll(qp, HEAD_DIM, 1), 0.0).astype(jnp.bfloat16)
        kv_ref[me, g] = kvp.astype(jnp.bfloat16)
        return 0

    lax.fori_loop(0, TEAM, project, 0)
    copies = []
    for k in range(1, groups):
        copies.append(
            pltpu.make_async_remote_copy(
                src_ref=kv_ref.at[me], dst_ref=kv_ref.at[me], send_sem=ssem.at[k - 1], recv_sem=rsem.at[k - 1],
                device_id={"dp": lax.rem(me + k, groups)}, device_id_type=MESH,
            )
        )
        copies[-1].start()
    for k in range(groups):
        p = lax.rem(me + groups - k, groups)
        if k > 0:
            copies[k - 1].wait_recv()
        for s in range(2):
            kv = kv_ref[p, :, s * tokens : (s + 1) * tokens, :].reshape(span, 128)
            kid = idr_ref[s, :, pl.ds(pl.multiple_of(p * span, 128), span)]

            def block(i, _, s=s, kv=kv, kid=kid, k=k):
                at = s * steps + i
                q = q_ref[:, pl.ds(i * SLOTS, SLOTS), s * tokens : (s + 1) * tokens, :].reshape(heads * CHUNK, 128)
                qid = idc_ref[s, pl.ds(pl.multiple_of(i * CHUNK, CHUNK), CHUNK), :]
                qid = jnp.concatenate([qid] * heads, axis=0)
                scores = lax.dot_general(q, kv, NT, preferred_element_type=jnp.float32)
                scores = jnp.where(kid <= qid, scores, NEG)
                peak = jnp.max(scores, axis=-1, keepdims=True)
                if k > 0:
                    old = top[at]
                    peak = jnp.maximum(old, peak)
                weight = jnp.exp(scores - peak)
                summed = jnp.sum(weight, axis=-1, keepdims=True)
                mixed = jnp.dot(weight.astype(jnp.bfloat16), kv, preferred_element_type=jnp.float32)
                if k > 0:
                    factor = jnp.exp(old - peak)
                    summed = summed + total[at] * factor
                    mixed = mixed + acc[at] * factor
                if k < groups - 1:
                    top[at] = peak
                    total[at] = summed
                    acc[at] = mixed
                else:
                    mixed = mixed / summed
                    first, second = mixed[:CHUNK], mixed[CHUNK:]
                    out = jnp.where(low_lanes(first.shape), pltpu.roll(first, HEAD_DIM, 1), second)
                    o_ref[pl.ds(i * SLOTS, SLOTS), s * tokens : (s + 1) * tokens, :] = out.astype(jnp.bfloat16).reshape(SLOTS, tokens, 128)
                    lse_ref[at] = as_row(peak + jnp.log(summed))
                return 0

            lax.fori_loop(0, steps, block, 0)
            tick()
    for cp in copies:
        cp.wait_send()


def attend(groups, h, w, cos, sin, idc, idr, cid, jobs=()):
    tokens = cos.shape[1]
    rows = 2 * tokens
    blocks = 2 * TEAM * tokens // CHUNK
    peers = max(groups - 1, 1)
    f32, bf16 = jnp.float32, jnp.bfloat16
    out = call(
        attend_kernel, [h, w, cos, sin, idc, idr],
        [
            jax.ShapeDtypeStruct((2, TEAM, rows, 128), bf16),
            jax.ShapeDtypeStruct((groups, TEAM, rows, 128), bf16),
            jax.ShapeDtypeStruct((TEAM, rows, 128), bf16),
            jax.ShapeDtypeStruct((blocks, 1, 2 * CHUNK), f32),
        ],
        [
            pltpu.VMEM((blocks, 2 * CHUNK, 1), f32), pltpu.VMEM((blocks, 2 * CHUNK, 1), f32),
            pltpu.VMEM((blocks, 2 * CHUNK, 128), f32),
            pltpu.SemaphoreType.DMA((peers,)), pltpu.SemaphoreType.DMA((peers,)),
        ],
        jobs, cid,
    )
    return out


def attend_back_kernel(groups, tick, dm_ref, wo_ref, q_ref, kv_ref, o_ref, lse_ref, cos_ref, sin_ref, idc_ref, idr_ref, d_ref, do, gz, delta, dq, dkv, out_buf, in_buf, ssem, rsem):
    me = lax.axis_index("dp")
    tokens = cos_ref.shape[1]
    span = TEAM * tokens
    steps = span // CHUNK
    f32, bf16 = jnp.float32, jnp.bfloat16

    def project(g, _):
        part = lax.dot_general(dm_ref[g], wo_ref[...], NT, preferred_element_type=f32).astype(bf16)
        do[g] = part
        part = part.astype(f32)
        low = low_lanes(part.shape)
        gz[0, g] = jnp.where(low, 0.0, pltpu.roll(part, HEAD_DIM, 1)).astype(bf16)
        gz[1, g] = jnp.where(low, 0.0, part).astype(bf16)
        return 0

    lax.fori_loop(0, TEAM, project, 0)
    for s in range(2):

        def deltas(i, _, s=s):
            here = (pl.ds(i * SLOTS, SLOTS), slice(s * tokens, (s + 1) * tokens), slice(None))
            both = do[here].reshape(CHUNK, 128).astype(f32) * o_ref[here].reshape(CHUNK, 128).astype(f32)
            low = low_lanes(both.shape)
            first = jnp.sum(jnp.where(low, both, 0.0), axis=-1, keepdims=True)
            second = jnp.sum(jnp.where(low, 0.0, both), axis=-1, keepdims=True)
            delta[s * steps + i] = as_row(jnp.concatenate([first, second], axis=0))
            return 0

        lax.fori_loop(0, steps, deltas, 0)
    copies = []
    order = list(range(1, groups)) + [0]
    for turn, k in enumerate(order):
        p = lax.rem(me + k, groups)
        for s in range(2):
            kv = kv_ref[p, :, s * tokens : (s + 1) * tokens, :].reshape(span, 128)
            kid = idc_ref[s, pl.ds(pl.multiple_of(p * span, span), span), :]

            def block(i, _, s=s, kv=kv, kid=kid, turn=turn):
                at = s * steps + i
                here = (slice(None), pl.ds(i * SLOTS, SLOTS), slice(s * tokens, (s + 1) * tokens), slice(None))
                q = q_ref[here].reshape(2 * CHUNK, 128)
                g = gz[here].reshape(2 * CHUNK, 128)
                qid = idr_ref[s, :, pl.ds(pl.multiple_of(i * CHUNK, CHUNK), CHUNK)]
                qid = jnp.concatenate([qid] * 2, axis=1)
                scores = lax.dot_general(kv, q, NT, preferred_element_type=f32)
                prob = jnp.where(kid <= qid, jnp.exp(scores - lse_ref[at]), 0.0)
                dp = lax.dot_general(kv, g, NT, preferred_element_type=f32)
                ds = (prob * (dp - delta[at])).astype(bf16)
                part = jnp.dot(ds, q, preferred_element_type=f32)
                part = part + jnp.dot(prob.astype(bf16), g, preferred_element_type=f32)
                dkv[s] = dkv[s] + part
                mine = lax.dot_general(ds, kv, TN, preferred_element_type=f32)
                if turn == 0:
                    dq[at] = mine
                else:
                    dq[at] = dq[at] + mine
                return 0

            dkv[s] = jnp.zeros((span, 128), f32)
            lax.fori_loop(0, steps, block, 0)
            tick()
            if k > 0:
                out_buf[k - 1, :, s * tokens : (s + 1) * tokens, :] = dkv[s].astype(bf16).reshape(TEAM, tokens, 128)
        if k > 0:
            copies.append(
                pltpu.make_async_remote_copy(
                    src_ref=out_buf.at[k - 1], dst_ref=in_buf.at[k - 1], send_sem=ssem.at[k - 1], recv_sem=rsem.at[k - 1],
                    device_id={"dp": p}, device_id_type=MESH,
                )
            )
            copies[-1].start()
    for cp in copies:
        cp.wait_recv()
    for s in range(2):

        def finish(i, _, s=s):
            here = (pl.ds(i * SLOTS, SLOTS), slice(s * tokens, (s + 1) * tokens), slice(None))
            cos = cos_ref[pl.ds(i * SLOTS, SLOTS)].reshape(CHUNK, 256)
            sin = sin_ref[pl.ds(i * SLOTS, SLOTS)].reshape(CHUNK, 256)
            both = dq[s * steps + i]
            first, second = both[:CHUNK], both[CHUNK:]
            qp = jnp.where(low_lanes(first.shape), first, pltpu.roll(second, HEAD_DIM, 1))
            kvp = dkv[s, pl.ds(pl.multiple_of(i * CHUNK, CHUNK), CHUNK), :]
            for k in range(1, groups):
                kvp = kvp + in_buf[(k - 1,) + here].reshape(CHUNK, 128).astype(f32)
            qp = qp * cos[:, :128] - swapped(qp) * sin[:, :128]
            kvp = kvp * cos[:, 128:] - swapped(kvp) * sin[:, 128:]
            both = jnp.concatenate([qp, kvp], axis=1).astype(bf16)
            d_ref[here] = both.reshape(SLOTS, tokens, 256)
            return 0

        lax.fori_loop(0, steps, finish, 0)
    for cp in copies:
        cp.wait_send()


def attend_back(groups, dm, wo, q, kv, o, lse, cos, sin, idc, idr, cid, jobs=()):
    tokens = cos.shape[1]
    rows = 2 * tokens
    span = TEAM * tokens
    blocks = 2 * span // CHUNK
    peers = max(groups - 1, 1)
    f32, bf16 = jnp.float32, jnp.bfloat16
    out = call(
        attend_back_kernel, [dm, wo, q, kv, o, lse, cos, sin, idc, idr], [jax.ShapeDtypeStruct((TEAM, rows, 256), bf16)],
        [
            pltpu.VMEM((TEAM, rows, 128), bf16), pltpu.VMEM((2, TEAM, rows, 128), bf16),
            pltpu.VMEM((blocks, 1, 2 * CHUNK), f32), pltpu.VMEM((blocks, 2 * CHUNK, 128), f32),
            pltpu.VMEM((2, span, 128), f32),
            pltpu.VMEM((peers, TEAM, rows, 128), bf16), pltpu.VMEM((peers, TEAM, rows, 128), bf16),
            pltpu.SemaphoreType.DMA((peers,)), pltpu.SemaphoreType.DMA((peers,)),
        ],
        jobs, cid,
    )
    return out[0][0], out[1]


def rotation_tables(positions):
    half = HEAD_DIM // 2
    freqs = rope_base ** (-jnp.arange(half, dtype=jnp.float32) * 2.0 / HEAD_DIM)
    angles = positions.astype(jnp.float32)[:, None] * freqs[None, :]
    cos, sin = jnp.cos(angles), jnp.sin(angles)
    one, none = jnp.ones_like(cos), jnp.zeros_like(cos)
    c = jnp.concatenate([cos * SCALE] * 4 + [cos, cos, one, one], axis=-1)
    s = jnp.concatenate([-sin * SCALE, sin * SCALE] * 2 + [-sin, sin, none, none], axis=-1)
    return c.reshape(TEAM, -1, 256), s.reshape(TEAM, -1, 256)


def norm_back(grad, normed, scale):
    return scale * (grad - normed * jnp.mean(grad * normed, axis=-1, keepdims=True))


def after(x, *others):
    return lax.optimization_barrier((x,) + others)[0]


def local(
    layer_input, attn_gain, query_weight, key_matrix, value_matrix, output_weight, ffn_gain,
    gate_weight, up_weight, down_weight, block_ids, cotangent,
):
    f32, bf16 = jnp.float32, jnp.bfloat16
    seqs, tokens, model = layer_input.shape
    rows = seqs * tokens
    groups = lax.axis_size("dp")
    group = lax.axis_index("dp")
    devices = groups * TEAM
    share = query_weight.shape[0]
    span = TEAM * tokens
    heads = QUERY_HEADS // TEAM
    ff = gate_weight.shape[1] // TEAM
    twin = TEAM // KEY_HEADS

    gain_one = attn_gain.astype(f32)[:, None]
    gain_two = ffn_gain.astype(f32)[:, None]

    def scaled(weight, gain):
        return (weight.astype(f32) * gain).astype(bf16)

    def doubled(weight):
        split = weight.reshape(share, KEY_HEADS, 1, HEAD_DIM)
        return jnp.broadcast_to(split, (share, KEY_HEADS, twin, HEAD_DIM)).reshape(share, TEAM, HEAD_DIM)

    def deal(k):
        return [(j, ((j + k) % groups) * TEAM + j // groups) for j in range(devices)]

    pack_q = jnp.moveaxis(scaled(query_weight, gain_one).reshape(share, TEAM, heads * HEAD_DIM), 1, 0)
    pack_kv = jnp.concatenate(
        [doubled(scaled(key_matrix, gain_one)), doubled(scaled(value_matrix, gain_one))], axis=-1
    )
    pack_kv = jnp.moveaxis(pack_kv, 1, 0)

    def in_order(mine, far):
        mine = mine.reshape(TEAM * share, -1)
        far = far.reshape((-1,) + mine.shape)
        if groups == 1:
            return mine
        if groups == 2:
            first = group == 0
            return jnp.concatenate([jnp.where(first, mine, far[0]), jnp.where(first, far[0], mine)])
        blocks = jnp.concatenate([mine[None], far])
        return jnp.take(blocks, lax.rem(group - jnp.arange(groups) + groups, groups), axis=0).reshape(model, -1)

    x = layer_input.reshape(rows, model).astype(f32)
    norm_one = lax.rsqrt(jnp.mean(x * x, axis=-1, keepdims=True) + epsilon)
    normed_one = x * norm_one
    c_own = cotangent.reshape(rows, model)
    h_one, (w_q, w_kv) = all_gather16(
        normed_one.astype(bf16), 1, [Swap(pack_q, ("x", "y", "z", "c"), True), Swap(pack_kv, ("y", "z", "x", "c"), True)]
    )
    w_in = jnp.concatenate([in_order(*w_q), in_order(*w_kv)], axis=-1)

    dealt = jnp.stack([lax.ppermute(output_weight, ALL, deal(k)) for k in range(groups)])
    if groups > 1:
        dealt = jnp.take(dealt, lax.rem(group - jnp.arange(groups) + groups, groups), axis=0)
    w_out = dealt.reshape(-1, model)

    pack_gate = jnp.moveaxis(scaled(gate_weight, gain_two).reshape(share, TEAM, ff), 1, 0)
    pack_up = jnp.moveaxis(scaled(up_weight, gain_two).reshape(share, TEAM, ff), 1, 0)
    pack_down = jnp.moveaxis(down_weight.reshape(share, TEAM, ff), 1, 0)
    packs = list(zip((pack_gate, pack_up, pack_down), SWAP_ORDERS))

    def errands(pair, first, count, own_block):
        return [Errand(a, first * share, count * share, own_block) for a in pair]

    cos, sin = rotation_tables(group * span + jnp.arange(span, dtype=jnp.int32))
    ids = lax.dynamic_slice_in_dim(block_ids, group * span, span, 1)
    (q, kv, o, lse), own = attend(
        groups, h_one, w_in, cos, sin, ids[:, :, None], block_ids[:, None, :], 3, [Swap(a, order) for a, order in packs]
    )
    own = [a[0].reshape(TEAM * share, ff) for a in own]
    branch, far_a = matmul_scatter16(o, w_out, False, 4, errands(own, 0, CUTS[0], False))
    middle = x + branch
    norm_two = lax.rsqrt(jnp.mean(middle * middle, axis=-1, keepdims=True) + epsilon)
    normed_two = middle * norm_two
    h_two, far_b = all_gather16(normed_two.astype(bf16), 9, errands(own, CUTS[0], CUTS[1], False))
    c_all, far_c = all_gather16(after(c_own, h_two), 10, errands(own, CUTS[0] + CUTS[1], CUTS[2], False))

    w_gate, w_up, w_down = [
        in_order(own[i], jnp.concatenate([far_a[i][0], far_b[i][0], far_c[i][0]], axis=1)) for i in range(3)
    ]
    w_gate_up = jnp.concatenate([w_gate, w_up], axis=-1)
    c_flat, h_flat = c_all.reshape(-1, model), h_two.reshape(-1, model)
    gate_up = jnp.dot(h_flat, w_gate_up, preferred_element_type=f32)
    gate, up = gate_up[:, :ff], gate_up[:, ff:]
    sig = jax.nn.sigmoid(gate)
    silu = gate * sig
    active = (silu * up).astype(bf16)
    da = jnp.dot(c_flat, w_down, preferred_element_type=f32)
    d_gate_up = jnp.concatenate(
        [(da * up * sig * (1.0 + gate * (1.0 - sig))).astype(bf16), (da * silu).astype(bf16)], axis=-1
    )

    def outer(left, right):
        return lax.dot_general(left, right, TN, preferred_element_type=f32)

    def by_group(piece):
        return piece.astype(bf16).reshape(groups, TEAM * share, -1)

    g_all = [by_group(outer(h_flat, d_gate_up[:, :ff])), by_group(outer(h_flat, d_gate_up[:, ff:])), by_group(outer(c_flat, active))]
    dn_two, sum_a = matmul_scatter16(
        d_gate_up.reshape(TEAM, rows, 2 * ff), w_gate_up, True, 5, errands(g_all, 0, BACK_CUTS[0], True)
    )
    middle_grad = c_own.astype(f32) + norm_back(dn_two, normed_two, norm_two)
    middle_low, sum_b = all_gather16(middle_grad.astype(bf16), 11, errands(g_all, BACK_CUTS[0], BACK_CUTS[1], True))
    w_part = outer(o.reshape(-1, heads * HEAD_DIM), middle_low.reshape(-1, model)).astype(bf16).reshape(groups, -1, model)
    d_in, sum_c = attend_back(
        groups, middle_low, w_out, q, kv, o, lse, cos, sin, block_ids[:, :, None], ids[:, None, :], 6,
        errands(g_all, BACK_CUTS[0] + BACK_CUTS[1], BACK_CUTS[2], True),
    )

    def summed(mine, *far):
        total = lax.dynamic_index_in_dim(mine, group, 0, keepdims=False).astype(f32)
        far = jnp.concatenate([a[0] for a in far], axis=1)
        for k in range(groups - 1):
            total = total + far[k].astype(f32)
        return total.astype(bf16).reshape(TEAM, share, -1)

    def home(piece):
        return jnp.moveaxis(piece[0].reshape(TEAM, share, -1).astype(f32), 0, 1)

    parts = [summed(g_all[i], sum_a[i], sum_b[i], sum_c[i]) for i in range(3)]
    d_flat = d_in.reshape(-1, d_in.shape[-1])
    attn = by_group(outer(h_one.reshape(-1, model), d_flat))
    dn_one, got = matmul_scatter16(
        d_in, w_in, True, 7,
        [Swap(a, order) for a, order in zip(parts, SWAP_ORDERS)] + errands([attn], 0, TEAM, True),
    )
    input_grad = (middle_grad + norm_back(dn_one, normed_one, norm_one)).reshape(seqs, tokens, model)
    gate_home, up_home, down_home = got[:3]
    attn = summed(attn, got[3])
    pieces = []
    for k in range(groups):
        pick = lax.rem(group + groups - k, groups) if groups > 1 else 0
        mine = lax.dynamic_index_in_dim(w_part, pick, 0, keepdims=False)
        pieces.append(lax.ppermute(mine, ALL, [(b, a) for a, b in deal(k)]).astype(f32))
    grad_output = sum(pieces)
    gains = jnp.stack(
        [jnp.sum(normed_one * dn_one, axis=0), jnp.sum(normed_two * dn_two, axis=0)], axis=0
    )
    gains = gains.reshape(2, groups, TEAM, share).transpose(2, 1, 0, 3).reshape(TEAM, 2 * groups, share)
    gains = jnp.pad(gains, ((0, 0), (0, -2 * groups % 8), (0, -share % 128)))
    cut = heads * HEAD_DIM
    produced, got = matmul_scatter16(
        active.reshape(TEAM, rows, ff), w_down, True, 8,
        [
            Swap(attn[..., :cut], ("x", "y", "z", "c")), Swap(attn[..., cut:], ("y", "z", "x", "c")),
            Swap(gains, ("z", "x", "y", "c"), True),
        ],
    )
    layer_output = (middle + produced).reshape(seqs, tokens, model)
    total = jnp.sum(got[2][0].reshape((TEAM,) + gains.shape[1:]), axis=0)
    if groups > 1:
        total = total + jnp.sum(got[2][1].reshape((-1,) + gains.shape[1:]), axis=0)
    gains = lax.dynamic_slice_in_dim(total, 2 * group, 2, 0)[:, :share]

    grad_gate = home(gate_home).reshape(share, -1) * gain_two
    grad_up = home(up_home).reshape(share, -1) * gain_two
    grad_down = home(down_home).reshape(share, -1)
    grad_query = home(got[0]).reshape(share, -1) * gain_one
    pair = home(got[1]).reshape(share, KEY_HEADS, twin, 2, HEAD_DIM).sum(axis=2)
    grad_key = pair[:, :, 0].reshape(share, -1) * gain_one
    grad_value = pair[:, :, 1].reshape(share, -1) * gain_one
    return (
        layer_output, input_grad, gains[0] / gain_one[:, 0], grad_query, grad_key, grad_value, grad_output,
        gains[1] / gain_two[:, 0], grad_gate, grad_up, grad_down,
    )


def solution(mesh):
    fine = Mesh(mesh.devices.reshape(-1, 2, 2, 2, 2), ALL)
    token = P(None, ALL, None)
    row = P(ALL, None)
    vec = P(ALL)
    in_specs = (token, vec, row, row, row, row, vec, row, row, row, P(), token)
    out_specs = (token, token, vec, row, row, row, row, vec, row, row, row)
    return jax.shard_map(local, mesh=fine, in_specs=in_specs, out_specs=out_specs, check_vma=False)
```

```python
import functools
import itertools

import jax
import jax.numpy as jnp
from jax import lax
from jax.experimental import pallas as pl
from jax.experimental.pallas import tpu as pltpu
from jax.sharding import Mesh
from jax.sharding import PartitionSpec as P

QUERY_HEADS = 32
KEY_HEADS = 8
HEAD_DIM = 64
TEAM = 16
SCALE = HEAD_DIM ** (-0.5)
epsilon = 1e-05
rope_base = 500000.0
NT = (((1,), (1,)), ((), ()))
TN = (((0,), (0,)), ((), ()))
TEAM_AXES = ("z", "y", "c", "x")
ALL = ("dp",) + TEAM_AXES
DIMS = ("z", "y", "c", "x")
WEIGHT = {"z": 8, "y": 4, "c": 2, "x": 1}
LINKS = ("x", "y", "z")
MESH = pl.DeviceIdType.MESH
COST = pl.CostEstimate(flops=30_000_000_000, bytes_accessed=1 << 20, transcendentals=0)
EVEN = (("x", "y", "z"), ("y", "z", "x"), ("z", "x", "y"))
PARK = "park"
Z_FIRST = (("z", "x", "y"), ("z", "y", "x"))
Z_LAST = (("x", "y", "z"), ("y", "x", "z"))


def part_rows(rows, count):
    tiles = rows // 16
    base = [tiles // count + (1 if i < tiles % count else 0) for i in range(count)]
    out, at = [], 0
    for b in base:
        out.append((at * 16, b * 16))
        at += b
    return out


def coords():
    return {d: lax.axis_index(d) for d in DIMS}


def slot_of(me, flips=()):
    return sum(((1 - me[d]) if d in flips else me[d]) * WEIGHT[d] for d in DIMS)


def greet(groups):
    barrier = pltpu.get_barrier_semaphore()
    me = coords()
    group = lax.axis_index("dp")
    for d in DIMS:
        pl.semaphore_signal(barrier, inc=1, device_id={d: 1 - me[d]}, device_id_type=MESH)
    for k in range(1, groups):
        pl.semaphore_signal(barrier, inc=1, device_id={"dp": lax.rem(group + k, groups)}, device_id_type=MESH)
    pl.semaphore_wait(barrier, groups - 1 + len(DIMS))


def anywhere():
    return pl.BlockSpec(memory_space=pl.ANY)


def vmem():
    return pl.BlockSpec(memory_space=pltpu.VMEM)


def dma_sems(n):
    return pltpu.SemaphoreType.DMA((max(n, 1),))


def to_groups(groups, make, ssem, rsem):
    me = lax.axis_index("dp")
    copies = []
    for k in range(1, groups):
        peer = lax.rem(me + k, groups)
        src, dst = make(k, peer)
        copies.append(
            pltpu.make_async_remote_copy(
                src_ref=src, dst_ref=dst, send_sem=ssem.at[k - 1], recv_sem=rsem.at[k - 1],
                device_id={"dp": peer}, device_id_type=MESH,
            )
        )
        copies[-1].start()
    return copies


class Errand:
    def __init__(self, array, own_block):
        self.inputs, self.own_block = [(array, anywhere)], own_block

    def outputs(self, groups):
        a = self.inputs[0][0]
        shape = a.shape[1:] if self.own_block else a.shape
        return [(jax.ShapeDtypeStruct((max(groups - 1, 1),) + shape, a.dtype), anywhere)]

    def scratch(self, groups):
        return [dma_sems(groups - 1), dma_sems(groups - 1)]

    def run(self, groups, src, dst, scratch):
        copies = to_groups(
            groups, lambda k, peer: (src[0].at[peer] if self.own_block else src[0], dst[0].at[k - 1]), *scratch
        )
        yield PARK
        for cp in copies:
            cp.wait()


def swap_stages(chain, order, patience, ssem, rsem, lsem):
    me = coords()
    sent = []
    for k, d in enumerate(order):
        lead = (slice(None),) * DIMS.index(d)
        a, z = chain[k], chain[k + 1]
        far = pltpu.make_async_remote_copy(
            src_ref=a.at[lead + (1 - me[d],)], dst_ref=z.at[lead + (me[d],)], send_sem=ssem.at[k],
            recv_sem=rsem.at[k], device_id={d: 1 - me[d]}, device_id_type=MESH,
        )
        near = pltpu.make_async_copy(a.at[lead + (me[d],)], z.at[lead + (me[d],)], lsem.at[k])
        far.start()
        near.start()
        sent.append(far)
        for _ in range(1 if d == "c" else patience):
            yield
        far.wait_recv()
        near.wait()
    return sent


class Swap:
    def __init__(self, array, order, far=False, reduce=0, patience=1):
        lead = array.shape[:1] if reduce else ()
        shape = array.shape[len(lead) + 1 :]
        self.shape, self.dtype = (2, 2, 2, 2) + shape, array.dtype
        self.inputs = [(array.reshape(lead + self.shape), vmem)]
        self.order, self.far, self.reduce, self.patience = order, far, reduce, patience

    def outputs(self, groups):
        out = [(jax.ShapeDtypeStruct(self.shape, self.dtype), vmem)]
        return out + [(jax.ShapeDtypeStruct((max(groups - 1, 1),) + self.shape, self.dtype), anywhere)] * self.far

    def scratch(self, groups):
        extra = [pltpu.VMEM((max(groups - 1, 1),) + self.shape, self.dtype), pltpu.VMEM(self.shape, self.dtype)]
        return (
            [pltpu.VMEM(self.shape, self.dtype)] * 3
            + [dma_sems(4), dma_sems(4), dma_sems(4), dma_sems(groups - 1), dma_sems(groups - 1)]
            + extra * (self.reduce > 0)
        )

    def run(self, groups, src, dst, scratch):
        b1, b2, b3, ssem, rsem, lsem, fs, fr = scratch[:8]
        first = src[0]
        copies = []
        if self.reduce:
            landing, first = scratch[8:]
            copies = to_groups(groups, lambda k, peer: (src[0].at[peer], landing.at[k - 1]), fs, fr)
            for _ in range(self.reduce):
                yield
            for cp in copies:
                cp.wait()
            mine = lax.axis_index("dp")

            def add(i, _):
                at = tuple(lax.rem(i // w, 2) for w in (8, 4, 2, 1))
                total = src[0][(mine,) + at].astype(jnp.float32)
                for k in range(groups - 1):
                    total = total + landing[(k,) + at].astype(jnp.float32)
                first[at] = total.astype(first.dtype)
                return 0

            lax.fori_loop(0, TEAM, add, 0)
        sent = yield from swap_stages([first, b1, b2, b3, dst[0]], self.order, self.patience, ssem, rsem, lsem)
        if self.far:
            copies = to_groups(groups, lambda k, peer: (dst[0], dst[1].at[k - 1]), fs, fr)
            yield PARK
            for cp in copies:
                cp.wait()
        for cp in sent:
            cp.wait_send()


class Gather:
    def __init__(self, x, plan, patience=1):
        self.inputs, self.plan, self.patience = [(x, vmem)], plan, patience

    def outputs(self, groups):
        x = self.inputs[0][0]
        return [(jax.ShapeDtypeStruct((TEAM,) + x.shape, x.dtype), vmem)]

    def scratch(self, groups):
        return [dma_sems(64), dma_sems(64), pltpu.SemaphoreType.DMA]

    def run(self, groups, src, dst, scratch):
        (x_ref,), (g_ref,), (ssem, rsem, lsem) = src, dst, scratch
        me = coords()
        rows = x_ref.shape[0]
        plan = self.plan
        parts = part_rows(rows, len(plan))
        local = pltpu.make_async_copy(x_ref, g_ref.at[slot_of(me)], lsem)
        local.start()
        counter = itertools.count()
        copies = []

        def send(flips, r0, rn, dim):
            i = next(counter)
            s = slot_of(me, flips)
            cp = pltpu.make_async_remote_copy(
                src_ref=g_ref.at[s, pl.ds(r0, rn)] if flips else x_ref.at[pl.ds(r0, rn)],
                dst_ref=g_ref.at[s, pl.ds(r0, rn)], send_sem=ssem.at[i], recv_sem=rsem.at[i],
                device_id={dim: 1 - me[dim]}, device_id_type=MESH,
            )
            cp.start()
            copies.append(cp)
            return cp

        step1 = [send((), r0, rn, plan[p][0]) for p, (r0, rn) in enumerate(parts)]
        step2 = [[send((), r0, rn, plan[p][1])] for p, (r0, rn) in enumerate(parts)]
        step3 = [[send((), r0, rn, plan[p][2])] for p, (r0, rn) in enumerate(parts)]
        core = [send((), 0, rows, "c")]
        for _ in range(self.patience):
            yield
        for p, (r0, rn) in enumerate(parts):
            a, b, c = plan[p]
            step1[p].wait_recv()
            step2[p].append(send((a,), r0, rn, b))
            step3[p].append(send((a,), r0, rn, c))
            core.append(send((a,), r0, rn, "c"))
            yield
        for j in range(2):
            for p, (r0, rn) in enumerate(parts):
                a, b, c = plan[p]
                flips = ((b,), (a, b))[j]
                step2[p][j].wait_recv()
                step3[p].append(send(flips, r0, rn, c))
                core.append(send(flips, r0, rn, "c"))
                yield
        for j in range(4):
            for p, (r0, rn) in enumerate(parts):
                a, b, c = plan[p]
                step3[p][j].wait_recv()
                core.append(send(((c,), (a, c), (b, c), (a, b, c))[j], r0, rn, "c"))
            yield
        for cp in core:
            cp.wait_recv()
        for cp in copies:
            cp.wait_send()
        local.wait()


ROUND = [(1, 1, 1), (0, 1, 1), (1, 0, 1), (1, 1, 0), (1, 0, 0), (0, 1, 0), (0, 0, 1), (0, 0, 0)]


def flips_of(bits, order):
    return tuple(d for b, d in zip(bits, order) if b)


def add_rows(dst, a, b, r0, rn):
    def body(i, _):
        r = pl.multiple_of(r0 + i * 16, 16)
        dst[pl.ds(r, 16)] = (a[pl.ds(r, 16)].astype(jnp.float32) + b[pl.ds(r, 16)].astype(jnp.float32)).astype(dst.dtype)
        return 0

    lax.fori_loop(0, rn // 16, body, 0)


class Scatter:
    def __init__(self, pairs, flip, plan, patience=1):
        self.inputs = [(m, vmem) for pair in pairs for m in pair]
        self.flip, self.plan, self.patience = flip, plan, patience
        w = pairs[0][1]
        self.rows, self.cols = pairs[0][0].shape[1], w.shape[0] if flip else w.shape[1]

    def outputs(self, groups):
        return [(jax.ShapeDtypeStruct((self.rows, self.cols), jnp.float32), vmem)]

    def scratch(self, groups):
        block = [pltpu.VMEM((n, self.rows, self.cols), jnp.bfloat16) for n in (8, 8, 8, 4, 2)]
        return block + [pltpu.VMEM((self.rows, self.cols), jnp.bfloat16), dma_sems(32), dma_sems(32)]

    def run(self, groups, src, dst, scratch):
        part, acc, cbuf, b1, b2, b3, ssem, rsem = scratch
        (o_ref,) = dst
        pairs = list(zip(src[::2], src[1::2]))
        me = coords()
        plan, rows, cols = self.plan, self.rows, self.cols
        parts = part_rows(rows, len(plan))
        counter = itertools.count()
        copies = []

        def send(a, z, dim):
            i = next(counter)
            cp = pltpu.make_async_remote_copy(
                src_ref=a, dst_ref=z, send_sem=ssem.at[i], recv_sem=rsem.at[i],
                device_id={dim: 1 - me[dim]}, device_id_type=MESH,
            )
            cp.start()
            copies.append(cp)
            return cp

        def products(theirs, z, ours, y):
            def column(j, _):
                here = pl.ds(pl.multiple_of(j * 512, 512), 512)
                total = None
                for a, w in pairs:
                    left = jnp.concatenate([a[theirs], a[ours]], axis=0)
                    if self.flip:
                        out = lax.dot_general(left, w[here, :], NT, preferred_element_type=jnp.float32)
                    else:
                        out = jnp.dot(left, w[:, here], preferred_element_type=jnp.float32)
                    total = out if total is None else total + out
                total = total.astype(z.dtype)
                z[:, here] = total[:rows]
                y[:, here] = total[rows:]
                return 0

            lax.fori_loop(0, cols // 512, column, 0)

        def key(flips):
            return sum((1 << i) for i, d in enumerate(LINKS) if d in flips)

        s1 = [{} for _ in plan]
        core = []

        def own(fl):
            k = key(fl)
            core[ROUND.index(tuple(int(d in fl) for d in LINKS))].wait_recv()
            add_rows(acc.at[k], acc.at[k], cbuf.at[k], 0, rows)
            for p, (r0, rn) in enumerate(parts):
                a, b, c = plan[p]
                if a in fl:
                    j = (1 if b in fl else 0) + (2 if c in fl else 0)
                    s1[p][j] = send(acc.at[k, pl.ds(r0, rn)], b1.at[j, pl.ds(r0, rn)], a)

        for n, bits in enumerate(ROUND):
            fl = flips_of(bits, LINKS)
            products(slot_of(me, fl + ("c",)), part.at[key(fl)], slot_of(me, fl), acc.at[key(fl)])
            core.append(send(part.at[key(fl)], cbuf.at[key(fl)], "c"))
            if n > 0:
                own(flips_of(ROUND[n - 1], LINKS))
            if n % 2 == 1:
                yield
        own(())
        for _ in range(self.patience):
            yield
        s2 = [{} for _ in plan]
        for bb, cc in ((1, 1), (1, 0), (0, 1), (0, 0)):
            for p, (r0, rn) in enumerate(parts):
                a, b, c = plan[p]
                s1[p][bb + 2 * cc].wait_recv()
                k = key(flips_of((bb, cc), (b, c)))
                add_rows(acc.at[k], acc.at[k], b1.at[bb + 2 * cc], r0, rn)
                if bb:
                    s2[p][cc] = send(acc.at[k, pl.ds(r0, rn)], b2.at[cc, pl.ds(r0, rn)], b)
            if cc == 0:
                for _ in range(self.patience if bb == 0 else 1):
                    yield
        s3 = []
        for cc in (1, 0):
            for p, (r0, rn) in enumerate(parts):
                a, b, c = plan[p]
                s2[p][cc].wait_recv()
                k = key((c,) if cc else ())
                add_rows(acc.at[k], acc.at[k], b2.at[cc], r0, rn)
                if cc:
                    s3.append(send(acc.at[k, pl.ds(r0, rn)], b3.at[pl.ds(r0, rn)], c))
            yield
        for p, (r0, rn) in enumerate(parts):
            s3[p].wait_recv()
            add_rows(o_ref, acc.at[0], b3, r0, rn)
        for cp in copies:
            cp.wait_send()


def call(jobs, cid, body=None, inputs=(), outputs=(), scratch=()):
    groups = lax.axis_size("dp")
    jobs = list(jobs)
    n_in, n_out, n_scratch = len(inputs), len(outputs), len(scratch)
    job_in = [job.inputs for job in jobs]
    job_out = [job.outputs(groups) for job in jobs]
    job_scratch = [job.scratch(groups) for job in jobs]

    def kernel(*refs):
        def take(n):
            nonlocal refs
            head, refs = refs[:n], refs[n:]
            return head

        ins = take(n_in)
        src = [take(len(o)) for o in job_in]
        outs = take(n_out)
        dst = [take(len(o)) for o in job_out]
        scr = take(n_scratch)
        own = [take(len(o)) for o in job_scratch]
        greet(groups)
        alive = [job.run(groups, a, z, m) for job, a, z, m in zip(jobs, src, dst, own)]

        parked = []

        def tick():
            for job in list(alive):
                state = next(job, alive)
                if state is not None:
                    alive.remove(job)
                if state is PARK:
                    parked.append(job)

        tick()
        if body is not None:
            body(groups, tick, *ins, *outs, *scr)
        while alive:
            tick()
        for job in parked:
            next(job, None)

    out = pl.pallas_call(
        kernel,
        out_shape=list(outputs) + [o for each in job_out for o, _ in each],
        in_specs=[vmem()] * n_in + [place() for each in job_in for _, place in each],
        out_specs=[vmem()] * n_out + [place() for each in job_out for _, place in each],
        scratch_shapes=list(scratch) + [o for each in job_scratch for o in each],
        cost_estimate=COST,
        compiler_params=pltpu.CompilerParams(collective_id=cid, has_side_effects=True, vmem_limit_bytes=60 << 20),
    )(*inputs, *[a for each in job_in for a, _ in each])
    main, rest = list(out[:n_out]), list(out[n_out:])
    got = []
    for each in job_out:
        got.append(rest[: len(each)])
        rest = rest[len(each) :]
    return main, got


NEG = -1e30
CHUNK = 256
SLOTS = 4
FFN_SLOTS = 4
ORDER_A = ("c", "x", "y", "z")
ORDER_B = ("c", "y", "z", "x")
ORDER_C = ("c", "z", "x", "y")


def swapped(v):
    lane = lax.broadcasted_iota(jnp.int32, v.shape, 1)
    low = lax.rem(lane, HEAD_DIM) < HEAD_DIM // 2
    return jnp.where(low, pltpu.roll(v, 128 - HEAD_DIM // 2, 1), pltpu.roll(v, HEAD_DIM // 2, 1))


def low_lanes(shape):
    return lax.broadcasted_iota(jnp.int32, shape, 1) < HEAD_DIM


def as_row(column):
    return jnp.transpose(jnp.broadcast_to(column, (column.shape[0], 128)))[0:1]


def as_column(row):
    return jnp.transpose(jnp.broadcast_to(row, (128, row.shape[1])))[:, 0:1]


def attend_kernel(groups, tick, h_ref, w_ref, cos_ref, sin_ref, own_ref, idr_ref, q_ref, kv_ref, o_ref, lse_ref, top, total, acc, ssem, rsem):
    me = lax.axis_index("dp")
    tokens = cos_ref.shape[1]
    span = TEAM * tokens
    steps = span // CHUNK
    heads = q_ref.shape[0]

    def project(g, _):
        raw = jnp.dot(h_ref[g], w_ref[...], preferred_element_type=jnp.float32)
        cos = jnp.concatenate([cos_ref[g]] * 2, axis=0)
        sin = jnp.concatenate([sin_ref[g]] * 2, axis=0)
        qp, kvp = raw[:, :128], raw[:, 128:]
        low = low_lanes(qp.shape)
        qp = qp * cos + swapped(qp) * sin
        kvp = kvp * jnp.where(low, cos / SCALE, 1.0) + swapped(kvp) * jnp.where(low, sin / SCALE, 0.0)
        q_ref[0, g] = jnp.where(low, qp, 0.0).astype(jnp.bfloat16)
        q_ref[1, g] = jnp.where(low, pltpu.roll(qp, HEAD_DIM, 1), 0.0).astype(jnp.bfloat16)
        kv_ref[me, g] = kvp.astype(jnp.bfloat16)
        return 0

    lax.fori_loop(0, TEAM, project, 0)
    tick()
    copies = []
    for k in range(1, groups):
        copies.append(
            pltpu.make_async_remote_copy(
                src_ref=kv_ref.at[me], dst_ref=kv_ref.at[me], send_sem=ssem.at[k - 1], recv_sem=rsem.at[k - 1],
                device_id={"dp": lax.rem(me + k, groups)}, device_id_type=MESH,
            )
        )
        copies[-1].start()
    for k in range(groups):
        p = lax.rem(me + groups - k, groups)
        if k > 0:
            copies[k - 1].wait_recv()
        for s in range(2):
            kv = kv_ref[p, :, s * tokens : (s + 1) * tokens, :].reshape(span, 128)
            kid = idr_ref[s, :, pl.ds(pl.multiple_of(p * span, 128), span)]

            def block(i, _, s=s, kv=kv, kid=kid, k=k):
                at = s * steps + i
                q = q_ref[:, pl.ds(i * SLOTS, SLOTS), s * tokens : (s + 1) * tokens, :].reshape(heads * CHUNK, 128)
                qid = as_column(own_ref[s, :, pl.ds(pl.multiple_of(i * CHUNK, CHUNK), CHUNK)])
                qid = jnp.concatenate([qid] * heads, axis=0)
                scores = lax.dot_general(q, kv, NT, preferred_element_type=jnp.float32)
                scores = jnp.where(kid <= qid, scores, NEG)
                peak = jnp.max(scores, axis=-1, keepdims=True)
                if k > 0:
                    old = top[at]
                    peak = jnp.maximum(old, peak)
                weight = jnp.exp(scores - peak)
                summed = jnp.sum(weight, axis=-1, keepdims=True)
                mixed = jnp.dot(weight.astype(jnp.bfloat16), kv, preferred_element_type=jnp.float32)
                if k > 0:
                    factor = jnp.exp(old - peak)
                    summed = summed + total[at] * factor
                    mixed = mixed + acc[at] * factor
                if k < groups - 1:
                    top[at] = peak
                    total[at] = summed
                    acc[at] = mixed
                else:
                    mixed = mixed / summed
                    first, second = mixed[:CHUNK], mixed[CHUNK:]
                    out = jnp.where(low_lanes(first.shape), pltpu.roll(first, HEAD_DIM, 1), second)
                    o_ref[pl.ds(i * SLOTS, SLOTS), s * tokens : (s + 1) * tokens, :] = out.astype(jnp.bfloat16).reshape(SLOTS, tokens, 128)
                    lse_ref[at] = as_row(peak + jnp.log(summed))
                return 0

            for first in range(0, steps, 2):
                lax.fori_loop(first, first + 2, block, 0)
                tick()
    for cp in copies:
        cp.wait_send()


def attend(groups, h, w, cos, sin, id_a, id_b, cid, jobs):
    tokens = cos.shape[1]
    rows = 2 * tokens
    blocks = 2 * TEAM * tokens // CHUNK
    f32, bf16 = jnp.float32, jnp.bfloat16
    return call(
        jobs, cid, attend_kernel, [h, w, cos, sin, id_a, id_b],
        [
            jax.ShapeDtypeStruct((2, TEAM, rows, 128), bf16),
            jax.ShapeDtypeStruct((groups, TEAM, rows, 128), bf16),
            jax.ShapeDtypeStruct((TEAM, rows, 128), bf16),
            jax.ShapeDtypeStruct((blocks, 1, 2 * CHUNK), f32),
        ],
        [
            pltpu.VMEM((blocks, 2 * CHUNK, 1), f32), pltpu.VMEM((blocks, 2 * CHUNK, 1), f32),
            pltpu.VMEM((blocks, 2 * CHUNK, 128), f32), dma_sems(groups - 1), dma_sems(groups - 1),
        ],
    )


def attend_back_kernel(groups, tick, dm_ref, wo_ref, q_ref, kv_ref, o_ref, lse_ref, cos_ref, sin_ref, all_ref, own_ref, d_ref, do, gz, delta, dq, dkv, out_buf, in_buf, ssem, rsem):
    me = lax.axis_index("dp")
    tokens = cos_ref.shape[1]
    span = TEAM * tokens
    steps = span // CHUNK
    f32, bf16 = jnp.float32, jnp.bfloat16

    def project(g, _):
        part = lax.dot_general(dm_ref[g], wo_ref[...], NT, preferred_element_type=f32).astype(bf16)
        do[g] = part
        part = part.astype(f32)
        low = low_lanes(part.shape)
        gz[0, g] = jnp.where(low, 0.0, pltpu.roll(part, HEAD_DIM, 1)).astype(bf16)
        gz[1, g] = jnp.where(low, 0.0, part).astype(bf16)
        return 0

    lax.fori_loop(0, TEAM, project, 0)
    tick()
    for s in range(2):

        def deltas(i, _, s=s):
            here = (pl.ds(i * SLOTS, SLOTS), slice(s * tokens, (s + 1) * tokens), slice(None))
            both = do[here].reshape(CHUNK, 128).astype(f32) * o_ref[here].reshape(CHUNK, 128).astype(f32)
            low = low_lanes(both.shape)
            first = jnp.sum(jnp.where(low, both, 0.0), axis=-1, keepdims=True)
            second = jnp.sum(jnp.where(low, 0.0, both), axis=-1, keepdims=True)
            delta[s * steps + i] = as_row(jnp.concatenate([first, second], axis=0))
            return 0

        lax.fori_loop(0, steps, deltas, 0)
    copies = []
    order = list(range(1, groups)) + [0]
    for turn, k in enumerate(order):
        p = lax.rem(me + k, groups)
        for s in range(2):
            kv = kv_ref[p, :, s * tokens : (s + 1) * tokens, :].reshape(span, 128)
            kid = as_column(all_ref[s, :, pl.ds(pl.multiple_of(p * span, span), span)])

            def block(i, _, s=s, kv=kv, kid=kid, turn=turn):
                at = s * steps + i
                here = (slice(None), pl.ds(i * SLOTS, SLOTS), slice(s * tokens, (s + 1) * tokens), slice(None))
                q = q_ref[here].reshape(2 * CHUNK, 128)
                g = gz[here].reshape(2 * CHUNK, 128)
                qid = own_ref[s, :, pl.ds(pl.multiple_of(i * CHUNK, CHUNK), CHUNK)]
                qid = jnp.concatenate([qid] * 2, axis=1)
                scores = lax.dot_general(kv, q, NT, preferred_element_type=f32)
                prob = jnp.where(kid <= qid, jnp.exp(scores - lse_ref[at]), 0.0)
                dp = lax.dot_general(kv, g, NT, preferred_element_type=f32)
                ds = (prob * (dp - delta[at])).astype(bf16)
                part = jnp.dot(ds, q, preferred_element_type=f32)
                part = part + jnp.dot(prob.astype(bf16), g, preferred_element_type=f32)
                dkv[s] = dkv[s] + part
                mine = lax.dot_general(ds, kv, TN, preferred_element_type=f32)
                if turn == 0:
                    dq[at] = mine
                else:
                    dq[at] = dq[at] + mine
                return 0

            dkv[s] = jnp.zeros((span, 128), f32)
            for first in range(0, steps, 2):
                lax.fori_loop(first, first + 2, block, 0)
                tick()
            if k > 0:
                out_buf[k - 1, :, s * tokens : (s + 1) * tokens, :] = dkv[s].astype(bf16).reshape(TEAM, tokens, 128)
        if k > 0:
            copies.append(
                pltpu.make_async_remote_copy(
                    src_ref=out_buf.at[k - 1], dst_ref=in_buf.at[k - 1], send_sem=ssem.at[k - 1], recv_sem=rsem.at[k - 1],
                    device_id={"dp": p}, device_id_type=MESH,
                )
            )
            copies[-1].start()
    for cp in copies:
        cp.wait_recv()
    for s in range(2):

        def finish(i, _, s=s):
            here = (pl.ds(i * SLOTS, SLOTS), slice(s * tokens, (s + 1) * tokens), slice(None))
            cos = cos_ref[pl.ds(i * SLOTS, SLOTS)].reshape(CHUNK, 128)
            sin = sin_ref[pl.ds(i * SLOTS, SLOTS)].reshape(CHUNK, 128)
            both = dq[s * steps + i]
            first, second = both[:CHUNK], both[CHUNK:]
            qp = jnp.where(low_lanes(first.shape), first, pltpu.roll(second, HEAD_DIM, 1))
            kvp = dkv[s, pl.ds(pl.multiple_of(i * CHUNK, CHUNK), CHUNK), :]
            for k in range(1, groups):
                kvp = kvp + in_buf[(k - 1,) + here].reshape(CHUNK, 128).astype(f32)
            low = low_lanes(qp.shape)
            qp = qp * cos - swapped(qp) * sin
            kvp = kvp * jnp.where(low, cos / SCALE, 1.0) - swapped(kvp) * jnp.where(low, sin / SCALE, 0.0)
            both = jnp.concatenate([qp, kvp], axis=1).astype(bf16)
            d_ref[here] = both.reshape(SLOTS, tokens, 256)
            return 0

        lax.fori_loop(0, steps, finish, 0)
    for cp in copies:
        cp.wait_send()


def attend_back(groups, dm, wo, q, kv, o, lse, cos, sin, id_a, id_b, cid, jobs):
    tokens = cos.shape[1]
    rows = 2 * tokens
    span = TEAM * tokens
    blocks = 2 * span // CHUNK
    peers = max(groups - 1, 1)
    f32, bf16 = jnp.float32, jnp.bfloat16
    return call(
        jobs, cid, attend_back_kernel, [dm, wo, q, kv, o, lse, cos, sin, id_a, id_b],
        [jax.ShapeDtypeStruct((TEAM, rows, 256), bf16)],
        [
            pltpu.VMEM((TEAM, rows, 128), bf16), pltpu.VMEM((2, TEAM, rows, 128), bf16),
            pltpu.VMEM((blocks, 1, 2 * CHUNK), f32), pltpu.VMEM((blocks, 2 * CHUNK, 128), f32),
            pltpu.VMEM((2, span, 128), f32),
            pltpu.VMEM((peers, TEAM, rows, 128), bf16), pltpu.VMEM((peers, TEAM, rows, 128), bf16),
            dma_sems(groups - 1), dma_sems(groups - 1),
        ],
    )


def ffn_kernel(h_ref, c_ref, g_ref, u_ref, d_ref, a_ref, dg_ref, du_ref, wg_ref, wu_ref, wd_ref, *sums):
    step = pl.program_id(0)
    slots, rows, model = h_ref.shape
    h = h_ref[...].reshape(slots * rows, model)
    c = c_ref[...].reshape(slots * rows, model)
    f32, bf16 = jnp.float32, jnp.bfloat16
    gate = jnp.dot(h, g_ref[...], preferred_element_type=f32)
    up = jnp.dot(h, u_ref[...], preferred_element_type=f32)
    da = jnp.dot(c, d_ref[...], preferred_element_type=f32)
    sig = 1.0 / (1.0 + jnp.exp(-gate))
    silu = gate * sig
    active = (silu * up).astype(bf16)
    d_gate = (da * up * sig * (1.0 + gate * (1.0 - sig))).astype(bf16)
    d_up = (da * silu).astype(bf16)
    for ref, value in ((a_ref, active), (dg_ref, d_gate), (du_ref, d_up)):
        ref[...] = value.reshape(slots, rows, -1)

    @pl.when(step == 0)
    def _():
        for total in sums:
            total[...] = jnp.zeros_like(total)

    wide = 512
    for first in range(0, model, wide):
        here = slice(first, first + wide)
        for total, left, right in zip(sums, (h_ref, h_ref, c_ref), (d_gate, d_up, active)):
            left = left[:, :, here].reshape(slots * rows, wide)
            total[here, :] += lax.dot_general(left, right, TN, preferred_element_type=f32)

    @pl.when(step == pl.num_programs(0) - 1)
    def _():
        for ref, total in zip((wg_ref, wu_ref, wd_ref), sums):
            ref[...] = total[...].astype(bf16)


def ffn(h, c, w_gate, w_up, w_down):
    team, rows, model = h.shape
    ff = w_gate.shape[1]
    bf16 = jnp.bfloat16
    tall = pl.BlockSpec((FFN_SLOTS, rows, model), lambda i: (i, 0, 0))
    weight = pl.BlockSpec((model, ff), lambda i: (0, 0))
    return pl.pallas_call(
        ffn_kernel,
        grid=(team // FFN_SLOTS,),
        in_specs=[tall, tall, weight, weight, weight],
        out_specs=[pl.BlockSpec((FFN_SLOTS, rows, ff), lambda i: (i, 0, 0))] * 3 + [weight] * 3,
        out_shape=[jax.ShapeDtypeStruct((team, rows, ff), bf16)] * 3 + [jax.ShapeDtypeStruct((model, ff), bf16)] * 3,
        scratch_shapes=[pltpu.VMEM((model, ff), jnp.float32)] * 3,
        cost_estimate=COST,
        compiler_params=pltpu.CompilerParams(vmem_limit_bytes=60 << 20),
    )(h, c, w_gate, w_up, w_down)


def rotation_tables(positions):
    half = HEAD_DIM // 2
    lane = jnp.arange(128, dtype=jnp.int32)
    freqs = rope_base ** (-(lane % half).astype(jnp.float32) * 2.0 / HEAD_DIM)
    angles = positions.astype(jnp.float32)[:, None] * freqs[None, :]
    sign = jnp.where(lane % HEAD_DIM < half, -SCALE, SCALE)
    return (jnp.cos(angles) * SCALE).reshape(TEAM, -1, 128), (jnp.sin(angles) * sign).reshape(TEAM, -1, 128)


def norm_back(grad, normed, scale):
    return scale * (grad - normed * jnp.mean(grad * normed, axis=-1, keepdims=True))


def after(x, *others):
    return lax.optimization_barrier((x,) + others)[0]


def local(
    layer_input, attn_gain, query_weight, key_matrix, value_matrix, output_weight, ffn_gain,
    gate_weight, up_weight, down_weight, block_ids, cotangent,
):
    f32, bf16 = jnp.float32, jnp.bfloat16
    seqs, tokens, model = layer_input.shape
    rows = seqs * tokens
    groups = lax.axis_size("dp")
    group = lax.axis_index("dp")
    devices = groups * TEAM
    share = query_weight.shape[0]
    span = TEAM * tokens
    heads = QUERY_HEADS // TEAM
    ff = gate_weight.shape[1] // TEAM
    twin = TEAM // KEY_HEADS
    cut = heads * HEAD_DIM

    gain_one = attn_gain.astype(f32)[:, None]
    gain_two = ffn_gain.astype(f32)[:, None]

    def scaled(weight, gain):
        return (weight.astype(f32) * gain).astype(bf16)

    def doubled(weight):
        split = weight.reshape(share, KEY_HEADS, 1, HEAD_DIM)
        return jnp.broadcast_to(split, (share, KEY_HEADS, twin, HEAD_DIM)).reshape(share, TEAM, HEAD_DIM)

    def deal(k):
        return [(j, ((j + k) % groups) * TEAM + j // groups) for j in range(devices)]

    def by_member(weight):
        return jnp.moveaxis(weight.reshape(share, TEAM, -1), 1, 0)

    def in_order(mine, far):
        mine = mine.reshape(TEAM * share, -1)
        far = far.reshape((-1,) + mine.shape)
        if groups == 1:
            return mine
        if groups == 2:
            first = group == 0
            return jnp.concatenate([jnp.where(first, mine, far[0]), jnp.where(first, far[0], mine)])
        blocks = jnp.concatenate([mine[None], far])
        return jnp.take(blocks, lax.rem(group - jnp.arange(groups) + groups, groups), axis=0).reshape(model, -1)

    pack_q = by_member(scaled(query_weight, gain_one))
    pack_kv = jnp.concatenate(
        [doubled(scaled(key_matrix, gain_one)), doubled(scaled(value_matrix, gain_one))], axis=-1
    )
    pack_kv = jnp.moveaxis(pack_kv, 1, 0)
    x = layer_input.reshape(rows, model).astype(f32)
    norm_one = lax.rsqrt(jnp.mean(x * x, axis=-1, keepdims=True) + epsilon)
    normed_one = x * norm_one
    c_own = cotangent.reshape(rows, model)
    _, (w_q, w_kv, (h_one,)) = call(
        [Swap(pack_q, ORDER_A, True), Swap(pack_kv, ORDER_B, True), Gather(normed_one.astype(bf16), Z_FIRST, 3)], 1
    )
    w_in = jnp.concatenate([in_order(*w_q), in_order(*w_kv)], axis=-1)

    late_weight = after(output_weight, h_one)
    dealt = jnp.stack([lax.ppermute(late_weight, ALL, deal(k)) for k in range(groups)])
    if groups > 1:
        dealt = jnp.take(dealt, lax.rem(group - jnp.arange(groups) + groups, groups), axis=0)
    w_out = dealt.reshape(-1, model)

    cos, sin = rotation_tables(group * span + jnp.arange(span, dtype=jnp.int32))
    all_ids = block_ids.astype(f32)[:, None, :]
    ids = lax.dynamic_slice_in_dim(all_ids, group * span, span, 2)
    packs = (by_member(scaled(gate_weight, gain_two)), by_member(scaled(up_weight, gain_two)), by_member(down_weight))
    (q, kv, o, lse), own = attend(
        groups, h_one, w_in, cos, sin, ids, all_ids, 2,
        [Swap(a, order, patience=2) for a, order in zip(packs, (ORDER_A, ORDER_B, ORDER_C))],
    )
    own_gate, own_up, own_down = [a[0].reshape(TEAM * share, ff) for a in own]

    _, ((far_gate,), (branch,)) = call([Errand(own_gate, False), Scatter([(o, w_out)], False, EVEN)], 3)
    middle = x + branch
    norm_two = lax.rsqrt(jnp.mean(middle * middle, axis=-1, keepdims=True) + epsilon)
    normed_two = middle * norm_two
    _, ((far_up,), (far_down,), (h_two,), (c_all,)) = call(
        [Errand(own_up, False), Errand(own_down, False), Gather(normed_two.astype(bf16), Z_FIRST), Gather(c_own, Z_FIRST)], 4
    )
    w_gate, w_up, w_down = in_order(own_gate, far_gate), in_order(own_up, far_up), in_order(own_down, far_down)
    active, d_gate, d_up, *g_ffn = ffn(h_two, c_all, w_gate, w_up, w_down)
    g_gate, g_up, g_down = [a.reshape(groups, TEAM * share, -1) for a in g_ffn]

    def outer(left, right):
        left, right = left.reshape(-1, left.shape[-1]), right.reshape(-1, right.shape[-1])
        left, right = lax.optimization_barrier((left, right))
        out = lax.dot_general(left, right, TN, preferred_element_type=f32)
        return out.astype(bf16).reshape(groups, TEAM * share, -1)

    def total(mine, far):
        out = lax.dynamic_index_in_dim(mine, group, 0, keepdims=False).astype(f32)
        for k in range(groups - 1):
            out = out + far[k].astype(f32)
        return out.astype(bf16).reshape(TEAM, share, -1)

    def home(piece):
        return jnp.moveaxis(piece[0].reshape(TEAM, share, -1).astype(f32), 0, 1)

    _, ((far_gate,), (dn_two,)) = call(
        [Errand(g_gate, True), Scatter([(d_gate, w_gate), (d_up, w_up)], True, EVEN)], 5
    )
    middle_grad = c_own.astype(f32) + norm_back(dn_two, normed_two, norm_two)
    _, ((far_up,), (middle_low,)) = call([Errand(g_up, True), Gather(middle_grad.astype(bf16), Z_FIRST)], 6)
    w_part, middle_low = lax.optimization_barrier((outer(o, middle_low), middle_low))
    w_part = w_part.reshape(groups, -1, model)
    pieces = []
    for k in range(groups):
        pick = lax.rem(group + groups - k, groups) if groups > 1 else 0
        mine = lax.dynamic_index_in_dim(w_part, pick, 0, keepdims=False)
        pieces.append(lax.ppermute(mine, ALL, [(b, a) for a, b in deal(k)]).astype(f32))
    grad_output = sum(pieces)
    (d_in,), ((far_down,), home_gate, home_up, (produced,)) = attend_back(
        groups, middle_low, w_out, q, kv, o, lse, cos, sin, all_ids, ids, 7,
        [
            Errand(g_down, True), Swap(total(g_gate, far_gate), ORDER_A, patience=2),
            Swap(total(g_up, far_up), ORDER_B, patience=2), Scatter([(active, w_down)], True, Z_LAST),
        ],
    )
    layer_output = (middle + produced).reshape(seqs, tokens, model)
    d_in, grad_output = lax.optimization_barrier((d_in, grad_output))
    attn = outer(h_one, d_in).reshape(groups, TEAM, share, -1)
    sum_down = total(g_down, far_down)
    thirds = (sum_down[..., : ff // 4], sum_down[..., ff // 4 : ff // 2], sum_down[..., ff // 2 :])
    _, ((dn_one,), home_a, home_b, home_c, home_q, home_kv) = call(
        [
            Scatter([(d_in, w_in)], True, EVEN), *[Swap(a, o) for a, o in zip(thirds, (ORDER_A, ORDER_B, ORDER_C))],
            Swap(attn[..., :cut], ORDER_A, reduce=6), Swap(attn[..., cut:], ORDER_B, reduce=6),
        ],
        8,
    )
    input_grad = (middle_grad + norm_back(dn_one, normed_one, norm_one)).reshape(seqs, tokens, model)

    grad_gate, grad_up = home(home_gate).reshape(share, -1), home(home_up).reshape(share, -1)
    grad_down = jnp.concatenate([home(a) for a in (home_a, home_b, home_c)], axis=-1).reshape(share, -1)
    grad_query = home(home_q).reshape(share, -1)
    pair = home_kv[0].reshape(KEY_HEADS, twin, share, 2 * HEAD_DIM).astype(f32).sum(axis=1)
    pair = jnp.moveaxis(pair, 0, 1)
    grad_key, grad_value = pair[..., :HEAD_DIM].reshape(share, -1), pair[..., HEAD_DIM:].reshape(share, -1)

    def gain_grad(*both):
        return sum(jnp.sum(weight.astype(f32) * grad, axis=-1) for weight, grad in both)

    grad_gain_one = gain_grad((query_weight, grad_query), (key_matrix, grad_key), (value_matrix, grad_value))
    grad_gain_two = gain_grad((gate_weight, grad_gate), (up_weight, grad_up))
    return (
        layer_output, input_grad, grad_gain_one, grad_query * gain_one, grad_key * gain_one, grad_value * gain_one,
        grad_output, grad_gain_two, grad_gate * gain_two, grad_up * gain_two, grad_down,
    )


def solution(mesh):
    fine = Mesh(mesh.devices.reshape(-1, 2, 2, 2, 2), ALL)
    token = P(None, ALL, None)
    row = P(ALL, None)
    vec = P(ALL)
    in_specs = (token, vec, row, row, row, row, vec, row, row, row, P(), token)
    out_specs = (token, token, vec, row, row, row, row, vec, row, row, row)
    return jax.shard_map(local, mesh=fine, in_specs=in_specs, out_specs=out_specs, check_vma=False)
```

```python
import functools
import itertools

import jax
import jax.numpy as jnp
from jax import lax
from jax.experimental import pallas as pl
from jax.experimental.pallas import tpu as pltpu
from jax.sharding import Mesh
from jax.sharding import PartitionSpec as P

QUERY_HEADS = 32
KEY_HEADS = 8
HEAD_DIM = 64
TEAM = 16
SCALE = HEAD_DIM ** (-0.5)
epsilon = 1e-05
rope_base = 500000.0
NT = (((1,), (1,)), ((), ()))
TN = (((0,), (0,)), ((), ()))
TEAM_AXES = ("z", "y", "c", "x")
ALL = ("dp",) + TEAM_AXES
DIMS = ("z", "y", "c", "x")
WEIGHT = {"z": 8, "y": 4, "c": 2, "x": 1}
LINKS = ("x", "y", "z")
MESH = pl.DeviceIdType.MESH
COST = pl.CostEstimate(flops=30_000_000_000, bytes_accessed=1 << 20, transcendentals=0)
EVEN = (("x", "y", "z"), ("y", "z", "x"), ("z", "x", "y"))
PARK = "park"
Z_FIRST = (("z", "x", "y"), ("z", "y", "x"))
Z_LAST = (("x", "y", "z"), ("y", "x", "z"))


def part_rows(rows, count):
    tiles = rows // 16
    base = [tiles // count + (1 if i < tiles % count else 0) for i in range(count)]
    out, at = [], 0
    for b in base:
        out.append((at * 16, b * 16))
        at += b
    return out


def coords():
    return {d: lax.axis_index(d) for d in DIMS}


def slot_of(me, flips=()):
    return sum(((1 - me[d]) if d in flips else me[d]) * WEIGHT[d] for d in DIMS)


def greet(groups):
    barrier = pltpu.get_barrier_semaphore()
    me = coords()
    group = lax.axis_index("dp")
    for d in DIMS:
        pl.semaphore_signal(barrier, inc=1, device_id={d: 1 - me[d]}, device_id_type=MESH)
    for k in range(1, groups):
        pl.semaphore_signal(barrier, inc=1, device_id={"dp": lax.rem(group + k, groups)}, device_id_type=MESH)
    pl.semaphore_wait(barrier, groups - 1 + len(DIMS))


def anywhere():
    return pl.BlockSpec(memory_space=pl.ANY)


def vmem():
    return pl.BlockSpec(memory_space=pltpu.VMEM)


def dma_sems(n):
    return pltpu.SemaphoreType.DMA((max(n, 1),))


def to_groups(groups, make, ssem, rsem):
    me = lax.axis_index("dp")
    copies = []
    for k in range(1, groups):
        peer = lax.rem(me + k, groups)
        src, dst = make(k, peer)
        copies.append(
            pltpu.make_async_remote_copy(
                src_ref=src, dst_ref=dst, send_sem=ssem.at[k - 1], recv_sem=rsem.at[k - 1],
                device_id={"dp": peer}, device_id_type=MESH,
            )
        )
        copies[-1].start()
    return copies


class Errand:
    def __init__(self, array, own_block, turn=0):
        self.inputs, self.own_block, self.turn = [(array, anywhere)], own_block, turn

    def outputs(self, groups):
        a = self.inputs[0][0]
        shape = a.shape[1:] if self.own_block else a.shape
        return [(jax.ShapeDtypeStruct((max(groups - 1, 1),) + shape, a.dtype), anywhere)]

    def scratch(self, groups):
        return [dma_sems(groups - 1), dma_sems(groups - 1)]

    def run(self, groups, src, dst, scratch):
        for _ in range(self.turn):
            yield
        copies = to_groups(
            groups, lambda k, peer: (src[0].at[peer] if self.own_block else src[0], dst[0].at[k - 1]), *scratch
        )
        yield PARK
        for cp in copies:
            cp.wait()


def swap_stages(chain, order, patience, ssem, rsem, lsem):
    me = coords()
    sent = []
    for k, d in enumerate(order):
        lead = (slice(None),) * DIMS.index(d)
        a, z = chain[k], chain[k + 1]
        far = pltpu.make_async_remote_copy(
            src_ref=a.at[lead + (1 - me[d],)], dst_ref=z.at[lead + (me[d],)], send_sem=ssem.at[k],
            recv_sem=rsem.at[k], device_id={d: 1 - me[d]}, device_id_type=MESH,
        )
        near = pltpu.make_async_copy(a.at[lead + (me[d],)], z.at[lead + (me[d],)], lsem.at[k])
        far.start()
        near.start()
        sent.append(far)
        for _ in range(1 if d == "c" else patience):
            yield
        far.wait_recv()
        near.wait()
    return sent


class Swap:
    def __init__(self, array, order, far=False, reduce=0, patience=1):
        lead = array.shape[:1] if reduce else ()
        shape = array.shape[len(lead) + 1 :]
        self.shape, self.dtype = (2, 2, 2, 2) + shape, array.dtype
        self.inputs = [(array.reshape(lead + self.shape), vmem)]
        self.order, self.far, self.reduce, self.patience = order, far, reduce, patience

    def outputs(self, groups):
        out = [(jax.ShapeDtypeStruct(self.shape, self.dtype), vmem)]
        return out + [(jax.ShapeDtypeStruct((max(groups - 1, 1),) + self.shape, self.dtype), anywhere)] * self.far

    def scratch(self, groups):
        extra = [pltpu.VMEM((max(groups - 1, 1),) + self.shape, self.dtype), pltpu.VMEM(self.shape, self.dtype)]
        return (
            [pltpu.VMEM(self.shape, self.dtype)] * 3
            + [dma_sems(4), dma_sems(4), dma_sems(4), dma_sems(groups - 1), dma_sems(groups - 1)]
            + extra * (self.reduce > 0)
        )

    def run(self, groups, src, dst, scratch):
        b1, b2, b3, ssem, rsem, lsem, fs, fr = scratch[:8]
        first = src[0]
        copies = []
        if self.reduce:
            landing, first = scratch[8:]
            copies = to_groups(groups, lambda k, peer: (src[0].at[peer], landing.at[k - 1]), fs, fr)
            for _ in range(self.reduce):
                yield
            for cp in copies:
                cp.wait()
            mine = lax.axis_index("dp")

            def add(i, _):
                at = tuple(lax.rem(i // w, 2) for w in (8, 4, 2, 1))
                total = src[0][(mine,) + at].astype(jnp.float32)
                for k in range(groups - 1):
                    total = total + landing[(k,) + at].astype(jnp.float32)
                first[at] = total.astype(first.dtype)
                return 0

            lax.fori_loop(0, TEAM, add, 0)
        sent = yield from swap_stages([first, b1, b2, b3, dst[0]], self.order, self.patience, ssem, rsem, lsem)
        if self.far:
            copies = to_groups(groups, lambda k, peer: (dst[0], dst[1].at[k - 1]), fs, fr)
            yield PARK
            for cp in copies:
                cp.wait()
        for cp in sent:
            cp.wait_send()


class Gather:
    def __init__(self, x, plan, patience=1, turn=0):
        self.inputs, self.plan, self.patience, self.turn = [(x, vmem)], plan, patience, turn

    def outputs(self, groups):
        x = self.inputs[0][0]
        return [(jax.ShapeDtypeStruct((TEAM,) + x.shape, x.dtype), vmem)]

    def scratch(self, groups):
        return [dma_sems(64), dma_sems(64), pltpu.SemaphoreType.DMA]

    def run(self, groups, src, dst, scratch):
        (x_ref,), (g_ref,), (ssem, rsem, lsem) = src, dst, scratch
        for _ in range(self.turn):
            yield
        me = coords()
        rows = x_ref.shape[0]
        plan = self.plan
        parts = part_rows(rows, len(plan))
        local = pltpu.make_async_copy(x_ref, g_ref.at[slot_of(me)], lsem)
        local.start()
        counter = itertools.count()
        copies = []

        def send(flips, r0, rn, dim):
            i = next(counter)
            s = slot_of(me, flips)
            cp = pltpu.make_async_remote_copy(
                src_ref=g_ref.at[s, pl.ds(r0, rn)] if flips else x_ref.at[pl.ds(r0, rn)],
                dst_ref=g_ref.at[s, pl.ds(r0, rn)], send_sem=ssem.at[i], recv_sem=rsem.at[i],
                device_id={dim: 1 - me[dim]}, device_id_type=MESH,
            )
            cp.start()
            copies.append(cp)
            return cp

        step1 = [send((), r0, rn, plan[p][0]) for p, (r0, rn) in enumerate(parts)]
        step2 = [[send((), r0, rn, plan[p][1])] for p, (r0, rn) in enumerate(parts)]
        step3 = [[send((), r0, rn, plan[p][2])] for p, (r0, rn) in enumerate(parts)]
        core = [send((), 0, rows, "c")]
        for _ in range(self.patience):
            yield
        for p, (r0, rn) in enumerate(parts):
            a, b, c = plan[p]
            step1[p].wait_recv()
            step2[p].append(send((a,), r0, rn, b))
            step3[p].append(send((a,), r0, rn, c))
            core.append(send((a,), r0, rn, "c"))
            yield
        for j in range(2):
            for p, (r0, rn) in enumerate(parts):
                a, b, c = plan[p]
                flips = ((b,), (a, b))[j]
                step2[p][j].wait_recv()
                step3[p].append(send(flips, r0, rn, c))
                core.append(send(flips, r0, rn, "c"))
                yield
        for j in range(4):
            for p, (r0, rn) in enumerate(parts):
                a, b, c = plan[p]
                step3[p][j].wait_recv()
                core.append(send(((c,), (a, c), (b, c), (a, b, c))[j], r0, rn, "c"))
            yield
        for cp in core:
            cp.wait_recv()
        for cp in copies:
            cp.wait_send()
        local.wait()


ROUND = [(1, 1, 1), (0, 1, 1), (1, 0, 1), (1, 1, 0), (1, 0, 0), (0, 1, 0), (0, 0, 1), (0, 0, 0)]


def flips_of(bits, order):
    return tuple(d for b, d in zip(bits, order) if b)


def add_rows(dst, a, b, r0, rn):
    def body(i, _):
        r = pl.multiple_of(r0 + i * 16, 16)
        dst[pl.ds(r, 16)] = (a[pl.ds(r, 16)].astype(jnp.float32) + b[pl.ds(r, 16)].astype(jnp.float32)).astype(dst.dtype)
        return 0

    lax.fori_loop(0, rn // 16, body, 0)


class Scatter:
    def __init__(self, pairs, flip, plan, patience=1):
        self.inputs = [(m, vmem) for pair in pairs for m in pair]
        self.flip, self.plan, self.patience = flip, plan, patience
        w = pairs[0][1]
        self.rows, self.cols = pairs[0][0].shape[1], w.shape[0] if flip else w.shape[1]

    def outputs(self, groups):
        return [(jax.ShapeDtypeStruct((self.rows, self.cols), jnp.float32), vmem)]

    def scratch(self, groups):
        block = [pltpu.VMEM((n, self.rows, self.cols), jnp.bfloat16) for n in (8, 8, 8, 4, 2)]
        return block + [pltpu.VMEM((self.rows, self.cols), jnp.bfloat16), dma_sems(32), dma_sems(32)]

    def run(self, groups, src, dst, scratch):
        part, acc, cbuf, b1, b2, b3, ssem, rsem = scratch
        (o_ref,) = dst
        pairs = list(zip(src[::2], src[1::2]))
        me = coords()
        plan, rows, cols = self.plan, self.rows, self.cols
        parts = part_rows(rows, len(plan))
        counter = itertools.count()
        copies = []

        def send(a, z, dim):
            i = next(counter)
            cp = pltpu.make_async_remote_copy(
                src_ref=a, dst_ref=z, send_sem=ssem.at[i], recv_sem=rsem.at[i],
                device_id={dim: 1 - me[dim]}, device_id_type=MESH,
            )
            cp.start()
            copies.append(cp)
            return cp

        def products(theirs, z, ours, y):
            def column(j, _):
                here = pl.ds(pl.multiple_of(j * 512, 512), 512)
                total = None
                for a, w in pairs:
                    left = jnp.concatenate([a[theirs], a[ours]], axis=0)
                    if self.flip:
                        out = lax.dot_general(left, w[here, :], NT, preferred_element_type=jnp.float32)
                    else:
                        out = jnp.dot(left, w[:, here], preferred_element_type=jnp.float32)
                    total = out if total is None else total + out
                total = total.astype(z.dtype)
                z[:, here] = total[:rows]
                y[:, here] = total[rows:]
                return 0

            lax.fori_loop(0, cols // 512, column, 0)

        def key(flips):
            return sum((1 << i) for i, d in enumerate(LINKS) if d in flips)

        s1 = [{} for _ in plan]
        core = []

        def own(fl):
            k = key(fl)
            core[ROUND.index(tuple(int(d in fl) for d in LINKS))].wait_recv()
            add_rows(acc.at[k], acc.at[k], cbuf.at[k], 0, rows)
            for p, (r0, rn) in enumerate(parts):
                a, b, c = plan[p]
                if a in fl:
                    j = (1 if b in fl else 0) + (2 if c in fl else 0)
                    s1[p][j] = send(acc.at[k, pl.ds(r0, rn)], b1.at[j, pl.ds(r0, rn)], a)

        for n, bits in enumerate(ROUND):
            fl = flips_of(bits, LINKS)
            products(slot_of(me, fl + ("c",)), part.at[key(fl)], slot_of(me, fl), acc.at[key(fl)])
            core.append(send(part.at[key(fl)], cbuf.at[key(fl)], "c"))
            if n > 0:
                own(flips_of(ROUND[n - 1], LINKS))
            if n % 2 == 1:
                yield
        own(())
        for _ in range(self.patience):
            yield
        s2 = [{} for _ in plan]
        for bb, cc in ((1, 1), (1, 0), (0, 1), (0, 0)):
            for p, (r0, rn) in enumerate(parts):
                a, b, c = plan[p]
                s1[p][bb + 2 * cc].wait_recv()
                k = key(flips_of((bb, cc), (b, c)))
                add_rows(acc.at[k], acc.at[k], b1.at[bb + 2 * cc], r0, rn)
                if bb:
                    s2[p][cc] = send(acc.at[k, pl.ds(r0, rn)], b2.at[cc, pl.ds(r0, rn)], b)
            if cc == 0:
                for _ in range(self.patience if bb == 0 else 1):
                    yield
        s3 = []
        for cc in (1, 0):
            for p, (r0, rn) in enumerate(parts):
                a, b, c = plan[p]
                s2[p][cc].wait_recv()
                k = key((c,) if cc else ())
                add_rows(acc.at[k], acc.at[k], b2.at[cc], r0, rn)
                if cc:
                    s3.append(send(acc.at[k, pl.ds(r0, rn)], b3.at[pl.ds(r0, rn)], c))
            yield
        for p, (r0, rn) in enumerate(parts):
            s3[p].wait_recv()
            add_rows(o_ref, acc.at[0], b3, r0, rn)
        for cp in copies:
            cp.wait_send()


class Relay:
    def __init__(self, scatter, extras, change, send, plan):
        self.scatter, self.change, self.send = scatter, change, send
        self.inputs = scatter.inputs + [(a, vmem) for a in extras]
        self.shape = (scatter.rows, scatter.cols)
        self.gather = Gather(jax.ShapeDtypeStruct(self.shape, jnp.bfloat16), plan)

    def outputs(self, groups):
        return self.scatter.outputs(groups) + self.gather.outputs(groups)

    def scratch(self, groups):
        own = [pltpu.VMEM(self.shape, jnp.bfloat16)]
        return self.scatter.scratch(groups) + self.gather.scratch(groups) + own

    def run(self, groups, src, dst, scratch):
        n = len(self.scatter.inputs)
        m = len(self.scatter.scratch(groups))
        kept, gathered = dst
        low = scratch[-1]
        yield from self.scatter.run(groups, src[:n], (kept,), scratch[:m])

        def rows(i, _):
            here = pl.ds(pl.multiple_of(i * 16, 16), 16)
            value = self.change(kept[here, :], *[a[here, :] for a in src[n:]])
            kept[here, :] = value
            low[here, :] = self.send(value).astype(low.dtype)
            return 0

        lax.fori_loop(0, self.shape[0] // 16, rows, 0)
        yield from self.gather.run(groups, (low,), (gathered,), scratch[m:-1])


def call(jobs, cid, body=None, inputs=(), outputs=(), scratch=()):
    groups = lax.axis_size("dp")
    jobs = list(jobs)
    n_in, n_out, n_scratch = len(inputs), len(outputs), len(scratch)
    job_in = [job.inputs for job in jobs]
    job_out = [job.outputs(groups) for job in jobs]
    job_scratch = [job.scratch(groups) for job in jobs]

    def kernel(*refs):
        def take(n):
            nonlocal refs
            head, refs = refs[:n], refs[n:]
            return head

        ins = take(n_in)
        src = [take(len(o)) for o in job_in]
        outs = take(n_out)
        dst = [take(len(o)) for o in job_out]
        scr = take(n_scratch)
        own = [take(len(o)) for o in job_scratch]
        greet(groups)
        alive = [job.run(groups, a, z, m) for job, a, z, m in zip(jobs, src, dst, own)]

        parked = []

        def tick():
            for job in list(alive):
                state = next(job, alive)
                if state is not None:
                    alive.remove(job)
                if state is PARK:
                    parked.append(job)

        tick()
        if body is not None:
            body(groups, tick, *ins, *outs, *scr)
        while alive:
            tick()
        for job in parked:
            next(job, None)

    out = pl.pallas_call(
        kernel,
        out_shape=list(outputs) + [o for each in job_out for o, _ in each],
        in_specs=[vmem()] * n_in + [place() for each in job_in for _, place in each],
        out_specs=[vmem()] * n_out + [place() for each in job_out for _, place in each],
        scratch_shapes=list(scratch) + [o for each in job_scratch for o in each],
        cost_estimate=COST,
        compiler_params=pltpu.CompilerParams(collective_id=cid, has_side_effects=True, vmem_limit_bytes=60 << 20),
    )(*inputs, *[a for each in job_in for a, _ in each])
    main, rest = list(out[:n_out]), list(out[n_out:])
    got = []
    for each in job_out:
        got.append(rest[: len(each)])
        rest = rest[len(each) :]
    return main, got


NEG = -1e30
CHUNK = 256
SLOTS = 4
GATHER_PLAN = Z_FIRST
FFN_SLOTS = 4
ORDER_A = ("c", "x", "y", "z")
ORDER_B = ("c", "y", "z", "x")
ORDER_C = ("c", "z", "x", "y")


def swapped(v):
    lane = lax.broadcasted_iota(jnp.int32, v.shape, 1)
    low = lax.rem(lane, HEAD_DIM) < HEAD_DIM // 2
    return jnp.where(low, pltpu.roll(v, 128 - HEAD_DIM // 2, 1), pltpu.roll(v, HEAD_DIM // 2, 1))


def low_lanes(shape):
    return lax.broadcasted_iota(jnp.int32, shape, 1) < HEAD_DIM


def as_row(column):
    return jnp.transpose(jnp.broadcast_to(column, (column.shape[0], 128)))[0:1]


def as_column(row):
    return jnp.transpose(jnp.broadcast_to(row, (128, row.shape[1])))[:, 0:1]


def attend_kernel(groups, tick, h_ref, w_ref, cos_ref, sin_ref, own_ref, idr_ref, q_ref, kv_ref, o_ref, lse_ref, top, total, acc, ssem, rsem):
    me = lax.axis_index("dp")
    tokens = cos_ref.shape[1]
    span = TEAM * tokens
    steps = span // CHUNK
    heads = q_ref.shape[0]

    def project(g, _):
        raw = jnp.dot(h_ref[g], w_ref[...], preferred_element_type=jnp.float32)
        cos = jnp.concatenate([cos_ref[g]] * 2, axis=0)
        sin = jnp.concatenate([sin_ref[g]] * 2, axis=0)
        qp, kvp = raw[:, :128], raw[:, 128:]
        low = low_lanes(qp.shape)
        qp = qp * cos + swapped(qp) * sin
        kvp = kvp * jnp.where(low, cos / SCALE, 1.0) + swapped(kvp) * jnp.where(low, sin / SCALE, 0.0)
        q_ref[0, g] = jnp.where(low, qp, 0.0).astype(jnp.bfloat16)
        q_ref[1, g] = jnp.where(low, pltpu.roll(qp, HEAD_DIM, 1), 0.0).astype(jnp.bfloat16)
        kv_ref[me, g] = kvp.astype(jnp.bfloat16)
        return 0

    lax.fori_loop(0, TEAM, project, 0)
    tick()
    copies = []
    for k in range(1, groups):
        copies.append(
            pltpu.make_async_remote_copy(
                src_ref=kv_ref.at[me], dst_ref=kv_ref.at[me], send_sem=ssem.at[k - 1], recv_sem=rsem.at[k - 1],
                device_id={"dp": lax.rem(me + k, groups)}, device_id_type=MESH,
            )
        )
        copies[-1].start()
    for k in range(groups):
        p = lax.rem(me + groups - k, groups)
        if k > 0:
            copies[k - 1].wait_recv()
        for s in range(2):
            kv = kv_ref[p, :, s * tokens : (s + 1) * tokens, :].reshape(span, 128)
            kid = idr_ref[s, :, pl.ds(pl.multiple_of(p * span, 128), span)]

            def block(i, _, s=s, kv=kv, kid=kid, k=k):
                at = s * steps + i
                q = q_ref[:, pl.ds(i * SLOTS, SLOTS), s * tokens : (s + 1) * tokens, :].reshape(heads * CHUNK, 128)
                qid = as_column(own_ref[s, :, pl.ds(pl.multiple_of(i * CHUNK, CHUNK), CHUNK)])
                qid = jnp.concatenate([qid] * heads, axis=0)
                scores = lax.dot_general(q, kv, NT, preferred_element_type=jnp.float32)
                scores = jnp.where(kid <= qid, scores, NEG)
                peak = jnp.max(scores, axis=-1, keepdims=True)
                if k > 0:
                    old = top[at]
                    peak = jnp.maximum(old, peak)
                weight = jnp.exp(scores - peak)
                summed = jnp.sum(weight, axis=-1, keepdims=True)
                mixed = jnp.dot(weight.astype(jnp.bfloat16), kv, preferred_element_type=jnp.float32)
                if k > 0:
                    factor = jnp.exp(old - peak)
                    summed = summed + total[at] * factor
                    mixed = mixed + acc[at] * factor
                if k < groups - 1:
                    top[at] = peak
                    total[at] = summed
                    acc[at] = mixed
                else:
                    mixed = mixed / summed
                    first, second = mixed[:CHUNK], mixed[CHUNK:]
                    out = jnp.where(low_lanes(first.shape), pltpu.roll(first, HEAD_DIM, 1), second)
                    o_ref[pl.ds(i * SLOTS, SLOTS), s * tokens : (s + 1) * tokens, :] = out.astype(jnp.bfloat16).reshape(SLOTS, tokens, 128)
                    lse_ref[at] = as_row(peak + jnp.log(summed))
                return 0

            for first in range(0, steps, 2):
                lax.fori_loop(first, first + 2, block, 0)
                tick()
    for cp in copies:
        cp.wait_send()


def attend(groups, h, w, cos, sin, id_a, id_b, cid, jobs):
    tokens = cos.shape[1]
    rows = 2 * tokens
    blocks = 2 * TEAM * tokens // CHUNK
    f32, bf16 = jnp.float32, jnp.bfloat16
    return call(
        jobs, cid, attend_kernel, [h, w, cos, sin, id_a, id_b],
        [
            jax.ShapeDtypeStruct((2, TEAM, rows, 128), bf16),
            jax.ShapeDtypeStruct((groups, TEAM, rows, 128), bf16),
            jax.ShapeDtypeStruct((TEAM, rows, 128), bf16),
            jax.ShapeDtypeStruct((blocks, 1, 2 * CHUNK), f32),
        ],
        [
            pltpu.VMEM((blocks, 2 * CHUNK, 1), f32), pltpu.VMEM((blocks, 2 * CHUNK, 1), f32),
            pltpu.VMEM((blocks, 2 * CHUNK, 128), f32), dma_sems(groups - 1), dma_sems(groups - 1),
        ],
    )


def attend_back_kernel(groups, tick, dm_ref, wo_ref, q_ref, kv_ref, o_ref, lse_ref, cos_ref, sin_ref, all_ref, own_ref, d_ref, do, gz, delta, dq, dkv, out_buf, in_buf, ssem, rsem):
    me = lax.axis_index("dp")
    tokens = cos_ref.shape[1]
    span = TEAM * tokens
    steps = span // CHUNK
    f32, bf16 = jnp.float32, jnp.bfloat16

    def project(g, _):
        part = lax.dot_general(dm_ref[g], wo_ref[...], NT, preferred_element_type=f32).astype(bf16)
        do[g] = part
        part = part.astype(f32)
        low = low_lanes(part.shape)
        gz[0, g] = jnp.where(low, 0.0, pltpu.roll(part, HEAD_DIM, 1)).astype(bf16)
        gz[1, g] = jnp.where(low, 0.0, part).astype(bf16)
        return 0

    lax.fori_loop(0, TEAM, project, 0)
    tick()
    for s in range(2):

        def deltas(i, _, s=s):
            here = (pl.ds(i * SLOTS, SLOTS), slice(s * tokens, (s + 1) * tokens), slice(None))
            both = do[here].reshape(CHUNK, 128).astype(f32) * o_ref[here].reshape(CHUNK, 128).astype(f32)
            low = low_lanes(both.shape)
            first = jnp.sum(jnp.where(low, both, 0.0), axis=-1, keepdims=True)
            second = jnp.sum(jnp.where(low, 0.0, both), axis=-1, keepdims=True)
            delta[s * steps + i] = as_row(jnp.concatenate([first, second], axis=0))
            return 0

        lax.fori_loop(0, steps, deltas, 0)
    copies = []
    order = list(range(1, groups)) + [0]
    for turn, k in enumerate(order):
        p = lax.rem(me + k, groups)
        for s in range(2):
            kv = kv_ref[p, :, s * tokens : (s + 1) * tokens, :].reshape(span, 128)
            kid = as_column(all_ref[s, :, pl.ds(pl.multiple_of(p * span, span), span)])

            def block(i, _, s=s, kv=kv, kid=kid, turn=turn):
                at = s * steps + i
                here = (slice(None), pl.ds(i * SLOTS, SLOTS), slice(s * tokens, (s + 1) * tokens), slice(None))
                q = q_ref[here].reshape(2 * CHUNK, 128)
                g = gz[here].reshape(2 * CHUNK, 128)
                qid = own_ref[s, :, pl.ds(pl.multiple_of(i * CHUNK, CHUNK), CHUNK)]
                qid = jnp.concatenate([qid] * 2, axis=1)
                scores = lax.dot_general(kv, q, NT, preferred_element_type=f32)
                prob = jnp.where(kid <= qid, jnp.exp(scores - lse_ref[at]), 0.0)
                dp = lax.dot_general(kv, g, NT, preferred_element_type=f32)
                ds = (prob * (dp - delta[at])).astype(bf16)
                part = jnp.dot(ds, q, preferred_element_type=f32)
                part = part + jnp.dot(prob.astype(bf16), g, preferred_element_type=f32)
                dkv[s] = dkv[s] + part
                mine = lax.dot_general(ds, kv, TN, preferred_element_type=f32)
                if turn == 0:
                    dq[at] = mine
                else:
                    dq[at] = dq[at] + mine
                return 0

            dkv[s] = jnp.zeros((span, 128), f32)
            for first in range(0, steps, 2):
                lax.fori_loop(first, first + 2, block, 0)
                tick()
            if k > 0:
                out_buf[k - 1, :, s * tokens : (s + 1) * tokens, :] = dkv[s].astype(bf16).reshape(TEAM, tokens, 128)
        if k > 0:
            copies.append(
                pltpu.make_async_remote_copy(
                    src_ref=out_buf.at[k - 1], dst_ref=in_buf.at[k - 1], send_sem=ssem.at[k - 1], recv_sem=rsem.at[k - 1],
                    device_id={"dp": p}, device_id_type=MESH,
                )
            )
            copies[-1].start()
    for cp in copies:
        cp.wait_recv()
    for s in range(2):

        def finish(i, _, s=s):
            here = (pl.ds(i * SLOTS, SLOTS), slice(s * tokens, (s + 1) * tokens), slice(None))
            cos = cos_ref[pl.ds(i * SLOTS, SLOTS)].reshape(CHUNK, 128)
            sin = sin_ref[pl.ds(i * SLOTS, SLOTS)].reshape(CHUNK, 128)
            both = dq[s * steps + i]
            first, second = both[:CHUNK], both[CHUNK:]
            qp = jnp.where(low_lanes(first.shape), first, pltpu.roll(second, HEAD_DIM, 1))
            kvp = dkv[s, pl.ds(pl.multiple_of(i * CHUNK, CHUNK), CHUNK), :]
            for k in range(1, groups):
                kvp = kvp + in_buf[(k - 1,) + here].reshape(CHUNK, 128).astype(f32)
            low = low_lanes(qp.shape)
            qp = qp * cos - swapped(qp) * sin
            kvp = kvp * jnp.where(low, cos / SCALE, 1.0) - swapped(kvp) * jnp.where(low, sin / SCALE, 0.0)
            both = jnp.concatenate([qp, kvp], axis=1).astype(bf16)
            d_ref[here] = both.reshape(SLOTS, tokens, 256)
            return 0

        lax.fori_loop(0, steps, finish, 0)
    for cp in copies:
        cp.wait_send()


def attend_back(groups, dm, wo, q, kv, o, lse, cos, sin, id_a, id_b, cid, jobs):
    tokens = cos.shape[1]
    rows = 2 * tokens
    span = TEAM * tokens
    blocks = 2 * span // CHUNK
    peers = max(groups - 1, 1)
    f32, bf16 = jnp.float32, jnp.bfloat16
    return call(
        jobs, cid, attend_back_kernel, [dm, wo, q, kv, o, lse, cos, sin, id_a, id_b],
        [jax.ShapeDtypeStruct((TEAM, rows, 256), bf16)],
        [
            pltpu.VMEM((TEAM, rows, 128), bf16), pltpu.VMEM((2, TEAM, rows, 128), bf16),
            pltpu.VMEM((blocks, 1, 2 * CHUNK), f32), pltpu.VMEM((blocks, 2 * CHUNK, 128), f32),
            pltpu.VMEM((2, span, 128), f32),
            pltpu.VMEM((peers, TEAM, rows, 128), bf16), pltpu.VMEM((peers, TEAM, rows, 128), bf16),
            dma_sems(groups - 1), dma_sems(groups - 1),
        ],
    )


def ffn_kernel(h_ref, c_ref, g_ref, u_ref, d_ref, a_ref, dg_ref, du_ref, wg_ref, wu_ref, wd_ref, *sums):
    step = pl.program_id(0)
    slots, rows, model = h_ref.shape
    h = h_ref[...].reshape(slots * rows, model)
    c = c_ref[...].reshape(slots * rows, model)
    f32, bf16 = jnp.float32, jnp.bfloat16
    gate = jnp.dot(h, g_ref[...], preferred_element_type=f32)
    up = jnp.dot(h, u_ref[...], preferred_element_type=f32)
    da = jnp.dot(c, d_ref[...], preferred_element_type=f32)
    sig = 1.0 / (1.0 + jnp.exp(-gate))
    silu = gate * sig
    active = (silu * up).astype(bf16)
    d_gate = (da * up * sig * (1.0 + gate * (1.0 - sig))).astype(bf16)
    d_up = (da * silu).astype(bf16)
    for ref, value in ((a_ref, active), (dg_ref, d_gate), (du_ref, d_up)):
        ref[...] = value.reshape(slots, rows, -1)

    @pl.when(step == 0)
    def _():
        for total in sums:
            total[...] = jnp.zeros_like(total)

    wide = 512
    for first in range(0, model, wide):
        here = slice(first, first + wide)
        for total, left, right in zip(sums, (h_ref, h_ref, c_ref), (d_gate, d_up, active)):
            left = left[:, :, here].reshape(slots * rows, wide)
            total[here, :] += lax.dot_general(left, right, TN, preferred_element_type=f32)

    @pl.when(step == pl.num_programs(0) - 1)
    def _():
        for ref, total in zip((wg_ref, wu_ref, wd_ref), sums):
            ref[...] = total[...].astype(bf16)


def ffn(h, c, w_gate, w_up, w_down):
    team, rows, model = h.shape
    ff = w_gate.shape[1]
    bf16 = jnp.bfloat16
    tall = pl.BlockSpec((FFN_SLOTS, rows, model), lambda i: (i, 0, 0))
    weight = pl.BlockSpec((model, ff), lambda i: (0, 0))
    return pl.pallas_call(
        ffn_kernel,
        grid=(team // FFN_SLOTS,),
        in_specs=[tall, tall, weight, weight, weight],
        out_specs=[pl.BlockSpec((FFN_SLOTS, rows, ff), lambda i: (i, 0, 0))] * 3 + [weight] * 3,
        out_shape=[jax.ShapeDtypeStruct((team, rows, ff), bf16)] * 3 + [jax.ShapeDtypeStruct((model, ff), bf16)] * 3,
        scratch_shapes=[pltpu.VMEM((model, ff), jnp.float32)] * 3,
        cost_estimate=COST,
        compiler_params=pltpu.CompilerParams(vmem_limit_bytes=60 << 20),
    )(h, c, w_gate, w_up, w_down)


def rotation_tables(positions):
    half = HEAD_DIM // 2
    lane = jnp.arange(128, dtype=jnp.int32)
    freqs = rope_base ** (-(lane % half).astype(jnp.float32) * 2.0 / HEAD_DIM)
    angles = positions.astype(jnp.float32)[:, None] * freqs[None, :]
    sign = jnp.where(lane % HEAD_DIM < half, -SCALE, SCALE)
    return (jnp.cos(angles) * SCALE).reshape(TEAM, -1, 128), (jnp.sin(angles) * sign).reshape(TEAM, -1, 128)


def norm_back(grad, normed, scale):
    return scale * (grad - normed * jnp.mean(grad * normed, axis=-1, keepdims=True))


def rms(values):
    return lax.rsqrt(jnp.mean(values * values, axis=-1, keepdims=True) + epsilon)


def after(x, *others):
    return lax.optimization_barrier((x,) + others)[0]


def local(
    layer_input, attn_gain, query_weight, key_matrix, value_matrix, output_weight, ffn_gain,
    gate_weight, up_weight, down_weight, block_ids, cotangent,
):
    f32, bf16 = jnp.float32, jnp.bfloat16
    seqs, tokens, model = layer_input.shape
    rows = seqs * tokens
    groups = lax.axis_size("dp")
    group = lax.axis_index("dp")
    devices = groups * TEAM
    share = query_weight.shape[0]
    span = TEAM * tokens
    heads = QUERY_HEADS // TEAM
    ff = gate_weight.shape[1] // TEAM
    twin = TEAM // KEY_HEADS
    cut = heads * HEAD_DIM

    gain_one = attn_gain.astype(f32)[:, None]
    gain_two = ffn_gain.astype(f32)[:, None]

    def scaled(weight, gain):
        return (weight.astype(f32) * gain).astype(bf16)

    def doubled(weight):
        split = weight.reshape(share, KEY_HEADS, 1, HEAD_DIM)
        return jnp.broadcast_to(split, (share, KEY_HEADS, twin, HEAD_DIM)).reshape(share, TEAM, HEAD_DIM)

    def deal(k):
        return [(j, ((j + k) % groups) * TEAM + j // groups) for j in range(devices)]

    def by_member(weight):
        return jnp.moveaxis(weight.reshape(share, TEAM, -1), 1, 0)

    def in_order(mine, far):
        mine = mine.reshape(TEAM * share, -1)
        far = far.reshape((-1,) + mine.shape)
        if groups == 1:
            return mine
        if groups == 2:
            first = group == 0
            return jnp.concatenate([jnp.where(first, mine, far[0]), jnp.where(first, far[0], mine)])
        blocks = jnp.concatenate([mine[None], far])
        return jnp.take(blocks, lax.rem(group - jnp.arange(groups) + groups, groups), axis=0).reshape(model, -1)

    pack_q = by_member(scaled(query_weight, gain_one))
    pack_kv = jnp.concatenate(
        [doubled(scaled(key_matrix, gain_one)), doubled(scaled(value_matrix, gain_one))], axis=-1
    )
    pack_kv = jnp.moveaxis(pack_kv, 1, 0)
    x = layer_input.reshape(rows, model).astype(f32)
    norm_one = rms(x)
    normed_one = x * norm_one
    c_own = cotangent.reshape(rows, model)
    _, (w_q, w_kv, (h_one,)) = call(
        [Swap(pack_q, ORDER_A, True), Swap(pack_kv, ORDER_B, True), Gather(normed_one.astype(bf16), Z_FIRST, 3)], 1
    )
    w_in = jnp.concatenate([in_order(*w_q), in_order(*w_kv)], axis=-1)

    late_weight = after(output_weight, h_one)
    dealt = jnp.stack([lax.ppermute(late_weight, ALL, deal(k)) for k in range(groups)])
    if groups > 1:
        dealt = jnp.take(dealt, lax.rem(group - jnp.arange(groups) + groups, groups), axis=0)
    w_out = dealt.reshape(-1, model)

    cos, sin = rotation_tables(group * span + jnp.arange(span, dtype=jnp.int32))
    all_ids = block_ids.astype(f32)[:, None, :]
    ids = lax.dynamic_slice_in_dim(all_ids, group * span, span, 2)
    packs = (by_member(scaled(gate_weight, gain_two)), by_member(scaled(up_weight, gain_two)), by_member(down_weight))
    (q, kv, o, lse), own = attend(
        groups, h_one, w_in, cos, sin, ids, all_ids, 2,
        [Swap(a, order, patience=2) for a, order in zip(packs, (ORDER_A, ORDER_B, ORDER_C))],
    )
    own_gate, own_up, own_down = [a[0].reshape(TEAM * share, ff) for a in own]

    _, ((far_gate,), (far_up,), (far_down,), (middle, h_two), (c_all,)) = call(
        [
            Errand(own_gate, False), Errand(own_up, False, 10), Errand(own_down, False, 16),
            Relay(Scatter([(o, w_out)], False, EVEN), [x], lambda total, x: x + total, lambda mid: mid * rms(mid), GATHER_PLAN),
            Gather(c_own, GATHER_PLAN, 1, 12),
        ],
        3,
    )
    w_gate, w_up, w_down = in_order(own_gate, far_gate), in_order(own_up, far_up), in_order(own_down, far_down)
    active, d_gate, d_up, *g_ffn = ffn(h_two, c_all, w_gate, w_up, w_down)
    g_gate, g_up, g_down = [a.reshape(groups, TEAM * share, -1) for a in g_ffn]

    def outer(left, right):
        left, right = left.reshape(-1, left.shape[-1]), right.reshape(-1, right.shape[-1])
        left, right = lax.optimization_barrier((left, right))
        out = lax.dot_general(left, right, TN, preferred_element_type=f32)
        return out.astype(bf16).reshape(groups, TEAM * share, -1)

    def total(mine, far):
        out = lax.dynamic_index_in_dim(mine, group, 0, keepdims=False).astype(f32)
        for k in range(groups - 1):
            out = out + far[k].astype(f32)
        return out.astype(bf16).reshape(TEAM, share, -1)

    def home(piece):
        return jnp.moveaxis(piece[0].reshape(TEAM, share, -1).astype(f32), 0, 1)

    def back(total, c, mid):
        scale = rms(mid)
        return c.astype(f32) + norm_back(total, mid * scale, scale)

    _, ((far_gate,), (far_up,), (middle_grad, middle_low)) = call(
        [
            Errand(g_gate, True), Errand(g_up, True, 10),
            Relay(
                Scatter([(d_gate, w_gate), (d_up, w_up)], True, EVEN), [c_own, middle], back, lambda grad: grad, GATHER_PLAN
            ),
        ],
        5,
    )
    w_part, middle_low = lax.optimization_barrier((outer(o, middle_low), middle_low))
    w_part = w_part.reshape(groups, -1, model)
    pieces = []
    for k in range(groups):
        pick = lax.rem(group + groups - k, groups) if groups > 1 else 0
        mine = lax.dynamic_index_in_dim(w_part, pick, 0, keepdims=False)
        pieces.append(lax.ppermute(mine, ALL, [(b, a) for a, b in deal(k)]).astype(f32))
    grad_output = sum(pieces)
    (d_in,), ((far_down,), home_gate, home_up, (produced,)) = attend_back(
        groups, middle_low, w_out, q, kv, o, lse, cos, sin, all_ids, ids, 7,
        [
            Errand(g_down, True), Swap(total(g_gate, far_gate), ORDER_A, patience=2),
            Swap(total(g_up, far_up), ORDER_B, patience=2), Scatter([(active, w_down)], True, Z_LAST),
        ],
    )
    layer_output = (middle + produced).reshape(seqs, tokens, model)
    d_in, grad_output = lax.optimization_barrier((d_in, grad_output))
    attn = outer(h_one, d_in).reshape(groups, TEAM, share, -1)
    sum_down = total(g_down, far_down)
    thirds = (sum_down[..., : ff // 4], sum_down[..., ff // 4 : ff // 2], sum_down[..., ff // 2 :])
    _, ((dn_one,), home_a, home_b, home_c, home_q, home_kv) = call(
        [
            Scatter([(d_in, w_in)], True, EVEN), *[Swap(a, o) for a, o in zip(thirds, (ORDER_A, ORDER_B, ORDER_C))],
            Swap(attn[..., :cut], ORDER_A, reduce=6), Swap(attn[..., cut:], ORDER_B, reduce=6),
        ],
        8,
    )
    input_grad = (middle_grad + norm_back(dn_one, normed_one, norm_one)).reshape(seqs, tokens, model)

    grad_gate, grad_up = home(home_gate).reshape(share, -1), home(home_up).reshape(share, -1)
    grad_down = jnp.concatenate([home(a) for a in (home_a, home_b, home_c)], axis=-1).reshape(share, -1)
    grad_query = home(home_q).reshape(share, -1)
    pair = home_kv[0].reshape(KEY_HEADS, twin, share, 2 * HEAD_DIM).astype(f32).sum(axis=1)
    pair = jnp.moveaxis(pair, 0, 1)
    grad_key, grad_value = pair[..., :HEAD_DIM].reshape(share, -1), pair[..., HEAD_DIM:].reshape(share, -1)

    def gain_grad(*both):
        return sum(jnp.sum(weight.astype(f32) * grad, axis=-1) for weight, grad in both)

    grad_gain_one = gain_grad((query_weight, grad_query), (key_matrix, grad_key), (value_matrix, grad_value))
    grad_gain_two = gain_grad((gate_weight, grad_gate), (up_weight, grad_up))
    return (
        layer_output, input_grad, grad_gain_one, grad_query * gain_one, grad_key * gain_one, grad_value * gain_one,
        grad_output, grad_gain_two, grad_gate * gain_two, grad_up * gain_two, grad_down,
    )


def solution(mesh):
    fine = Mesh(mesh.devices.reshape(-1, 2, 2, 2, 2), ALL)
    token = P(None, ALL, None)
    row = P(ALL, None)
    vec = P(ALL)
    in_specs = (token, vec, row, row, row, row, vec, row, row, row, P(), token)
    out_specs = (token, token, vec, row, row, row, row, vec, row, row, row)
    return jax.shard_map(local, mesh=fine, in_specs=in_specs, out_specs=out_specs, check_vma=False)
```

```python
import functools
import itertools

import jax
import jax.numpy as jnp
from jax import lax
from jax.experimental import pallas as pl
from jax.experimental.pallas import tpu as pltpu
from jax.sharding import Mesh
from jax.sharding import PartitionSpec as P

QUERY_HEADS = 32
KEY_HEADS = 8
HEAD_DIM = 64
TEAM = 16
SCALE = HEAD_DIM ** (-0.5)
epsilon = 1e-05
rope_base = 500000.0
NT = (((1,), (1,)), ((), ()))
TN = (((0,), (0,)), ((), ()))
TEAM_AXES = ("z", "y", "c", "x")
ALL = ("dp",) + TEAM_AXES
DIMS = ("z", "y", "c", "x")
WEIGHT = {"z": 8, "y": 4, "c": 2, "x": 1}
LINKS = ("x", "y", "z")
MESH = pl.DeviceIdType.MESH
COST = pl.CostEstimate(flops=30_000_000_000, bytes_accessed=1 << 20, transcendentals=0)
EVEN = (("x", "y", "z"), ("y", "z", "x"), ("z", "x", "y"))
PARK = "park"
Z_FIRST = (("z", "x", "y"), ("z", "y", "x"))
Z_LAST = (("x", "y", "z"), ("y", "x", "z"))


def part_rows(rows, count):
    tiles = rows // 16
    base = [tiles // count + (1 if i < tiles % count else 0) for i in range(count)]
    out, at = [], 0
    for b in base:
        out.append((at * 16, b * 16))
        at += b
    return out


def coords():
    return {d: lax.axis_index(d) for d in DIMS}


def slot_of(me, flips=()):
    return sum(((1 - me[d]) if d in flips else me[d]) * WEIGHT[d] for d in DIMS)


def greet(groups):
    barrier = pltpu.get_barrier_semaphore()
    me = coords()
    group = lax.axis_index("dp")
    for d in DIMS:
        pl.semaphore_signal(barrier, inc=1, device_id={d: 1 - me[d]}, device_id_type=MESH)
    for k in range(1, groups):
        pl.semaphore_signal(barrier, inc=1, device_id={"dp": lax.rem(group + k, groups)}, device_id_type=MESH)
    pl.semaphore_wait(barrier, groups - 1 + len(DIMS))


def anywhere():
    return pl.BlockSpec(memory_space=pl.ANY)


def vmem():
    return pl.BlockSpec(memory_space=pltpu.VMEM)


def dma_sems(n):
    return pltpu.SemaphoreType.DMA((max(n, 1),))


def to_groups(groups, make, ssem, rsem):
    me = lax.axis_index("dp")
    copies = []
    for k in range(1, groups):
        peer = lax.rem(me + k, groups)
        src, dst = make(k, peer)
        copies.append(
            pltpu.make_async_remote_copy(
                src_ref=src, dst_ref=dst, send_sem=ssem.at[k - 1], recv_sem=rsem.at[k - 1],
                device_id={"dp": peer}, device_id_type=MESH,
            )
        )
        copies[-1].start()
    return copies


class Errand:
    def __init__(self, array, own_block, turn=0):
        self.inputs, self.own_block, self.turn = [(array, anywhere)], own_block, turn

    def outputs(self, groups):
        a = self.inputs[0][0]
        shape = a.shape[1:] if self.own_block else a.shape
        return [(jax.ShapeDtypeStruct((max(groups - 1, 1),) + shape, a.dtype), anywhere)]

    def scratch(self, groups):
        return [dma_sems(groups - 1), dma_sems(groups - 1)]

    def run(self, groups, src, dst, scratch):
        for _ in range(self.turn):
            yield
        copies = to_groups(
            groups, lambda k, peer: (src[0].at[peer] if self.own_block else src[0], dst[0].at[k - 1]), *scratch
        )
        yield PARK
        for cp in copies:
            cp.wait()


def swap_stages(chain, order, patience, ssem, rsem, lsem):
    me = coords()
    sent = []
    for k, d in enumerate(order):
        lead = (slice(None),) * DIMS.index(d)
        a, z = chain[k], chain[k + 1]
        far = pltpu.make_async_remote_copy(
            src_ref=a.at[lead + (1 - me[d],)], dst_ref=z.at[lead + (me[d],)], send_sem=ssem.at[k],
            recv_sem=rsem.at[k], device_id={d: 1 - me[d]}, device_id_type=MESH,
        )
        near = pltpu.make_async_copy(a.at[lead + (me[d],)], z.at[lead + (me[d],)], lsem.at[k])
        far.start()
        near.start()
        sent.append(far)
        for _ in range(1 if d == "c" else patience):
            yield
        far.wait_recv()
        near.wait()
    return sent


class Swap:
    def __init__(self, array, order, far=False, reduce=0, patience=1):
        lead = array.shape[:1] if reduce else ()
        shape = array.shape[len(lead) + 1 :]
        self.shape, self.dtype = (2, 2, 2, 2) + shape, array.dtype
        self.inputs = [(array.reshape(lead + self.shape), vmem)]
        self.order, self.far, self.reduce, self.patience = order, far, reduce, patience

    def outputs(self, groups):
        out = [(jax.ShapeDtypeStruct(self.shape, self.dtype), vmem)]
        return out + [(jax.ShapeDtypeStruct((max(groups - 1, 1),) + self.shape, self.dtype), anywhere)] * self.far

    def scratch(self, groups):
        extra = [pltpu.VMEM((max(groups - 1, 1),) + self.shape, self.dtype), pltpu.VMEM(self.shape, self.dtype)]
        return (
            [pltpu.VMEM(self.shape, self.dtype)] * 3
            + [dma_sems(4), dma_sems(4), dma_sems(4), dma_sems(groups - 1), dma_sems(groups - 1)]
            + extra * (self.reduce > 0)
        )

    def run(self, groups, src, dst, scratch):
        b1, b2, b3, ssem, rsem, lsem, fs, fr = scratch[:8]
        first = src[0]
        copies = []
        if self.reduce:
            landing, first = scratch[8:]
            copies = to_groups(groups, lambda k, peer: (src[0].at[peer], landing.at[k - 1]), fs, fr)
            for _ in range(self.reduce):
                yield
            for cp in copies:
                cp.wait()
            mine = lax.axis_index("dp")

            def add(i, _):
                at = tuple(lax.rem(i // w, 2) for w in (8, 4, 2, 1))
                total = src[0][(mine,) + at].astype(jnp.float32)
                for k in range(groups - 1):
                    total = total + landing[(k,) + at].astype(jnp.float32)
                first[at] = total.astype(first.dtype)
                return 0

            lax.fori_loop(0, TEAM, add, 0)
        sent = yield from swap_stages([first, b1, b2, b3, dst[0]], self.order, self.patience, ssem, rsem, lsem)
        if self.far:
            copies = to_groups(groups, lambda k, peer: (dst[0], dst[1].at[k - 1]), fs, fr)
            yield PARK
            for cp in copies:
                cp.wait()
        for cp in sent:
            cp.wait_send()


class Gather:
    def __init__(self, x, plan, patience=1, turn=0):
        self.inputs, self.plan, self.patience, self.turn = [(x, vmem)], plan, patience, turn

    def outputs(self, groups):
        x = self.inputs[0][0]
        return [(jax.ShapeDtypeStruct((TEAM,) + x.shape, x.dtype), vmem)]

    def scratch(self, groups):
        return [dma_sems(64), dma_sems(64), pltpu.SemaphoreType.DMA]

    def run(self, groups, src, dst, scratch):
        (x_ref,), (g_ref,), (ssem, rsem, lsem) = src, dst, scratch
        for _ in range(self.turn):
            yield
        me = coords()
        rows = x_ref.shape[0]
        plan = self.plan
        parts = part_rows(rows, len(plan))
        local = pltpu.make_async_copy(x_ref, g_ref.at[slot_of(me)], lsem)
        local.start()
        counter = itertools.count()
        copies = []

        def send(flips, r0, rn, dim):
            i = next(counter)
            s = slot_of(me, flips)
            cp = pltpu.make_async_remote_copy(
                src_ref=g_ref.at[s, pl.ds(r0, rn)] if flips else x_ref.at[pl.ds(r0, rn)],
                dst_ref=g_ref.at[s, pl.ds(r0, rn)], send_sem=ssem.at[i], recv_sem=rsem.at[i],
                device_id={dim: 1 - me[dim]}, device_id_type=MESH,
            )
            cp.start()
            copies.append(cp)
            return cp

        step1 = [send((), r0, rn, plan[p][0]) for p, (r0, rn) in enumerate(parts)]
        step2 = [[send((), r0, rn, plan[p][1])] for p, (r0, rn) in enumerate(parts)]
        step3 = [[send((), r0, rn, plan[p][2])] for p, (r0, rn) in enumerate(parts)]
        core = [send((), 0, rows, "c")]
        for _ in range(self.patience):
            yield
        for p, (r0, rn) in enumerate(parts):
            a, b, c = plan[p]
            step1[p].wait_recv()
            step2[p].append(send((a,), r0, rn, b))
            step3[p].append(send((a,), r0, rn, c))
            core.append(send((a,), r0, rn, "c"))
            yield
        for j in range(2):
            for p, (r0, rn) in enumerate(parts):
                a, b, c = plan[p]
                flips = ((b,), (a, b))[j]
                step2[p][j].wait_recv()
                step3[p].append(send(flips, r0, rn, c))
                core.append(send(flips, r0, rn, "c"))
                yield
        for j in range(4):
            for p, (r0, rn) in enumerate(parts):
                a, b, c = plan[p]
                step3[p][j].wait_recv()
                core.append(send(((c,), (a, c), (b, c), (a, b, c))[j], r0, rn, "c"))
            yield
        for cp in core:
            cp.wait_recv()
        for cp in copies:
            cp.wait_send()
        local.wait()


ROUND = [(1, 1, 1), (0, 1, 1), (1, 0, 1), (1, 1, 0), (1, 0, 0), (0, 1, 0), (0, 0, 1), (0, 0, 0)]


def flips_of(bits, order):
    return tuple(d for b, d in zip(bits, order) if b)


def add_rows(dst, a, b, r0, rn):
    def body(i, _):
        r = pl.multiple_of(r0 + i * 16, 16)
        dst[pl.ds(r, 16)] = (a[pl.ds(r, 16)].astype(jnp.float32) + b[pl.ds(r, 16)].astype(jnp.float32)).astype(dst.dtype)
        return 0

    lax.fori_loop(0, rn // 16, body, 0)


class Scatter:
    def __init__(self, pairs, flip, plan, patience=1):
        self.inputs = [(m, vmem) for pair in pairs for m in pair]
        self.flip, self.plan, self.patience = flip, plan, patience
        w = pairs[0][1]
        self.rows, self.cols = pairs[0][0].shape[1], w.shape[0] if flip else w.shape[1]

    def outputs(self, groups):
        return [(jax.ShapeDtypeStruct((self.rows, self.cols), jnp.float32), vmem)]

    def scratch(self, groups):
        block = [pltpu.VMEM((n, self.rows, self.cols), jnp.bfloat16) for n in (8, 8, 8, 4, 2)]
        return block + [pltpu.VMEM((self.rows, self.cols), jnp.bfloat16), dma_sems(32), dma_sems(32)]

    def run(self, groups, src, dst, scratch):
        part, acc, cbuf, b1, b2, b3, ssem, rsem = scratch
        (o_ref,) = dst
        pairs = list(zip(src[::2], src[1::2]))
        me = coords()
        plan, rows, cols = self.plan, self.rows, self.cols
        parts = part_rows(rows, len(plan))
        counter = itertools.count()
        copies = []

        def send(a, z, dim):
            i = next(counter)
            cp = pltpu.make_async_remote_copy(
                src_ref=a, dst_ref=z, send_sem=ssem.at[i], recv_sem=rsem.at[i],
                device_id={dim: 1 - me[dim]}, device_id_type=MESH,
            )
            cp.start()
            copies.append(cp)
            return cp

        def products(theirs, z, ours, y):
            def column(j, _):
                here = pl.ds(pl.multiple_of(j * 512, 512), 512)
                total = None
                for a, w in pairs:
                    left = jnp.concatenate([a[theirs], a[ours]], axis=0)
                    if self.flip:
                        out = lax.dot_general(left, w[here, :], NT, preferred_element_type=jnp.float32)
                    else:
                        out = jnp.dot(left, w[:, here], preferred_element_type=jnp.float32)
                    total = out if total is None else total + out
                total = total.astype(z.dtype)
                z[:, here] = total[:rows]
                y[:, here] = total[rows:]
                return 0

            lax.fori_loop(0, cols // 512, column, 0)

        def key(flips):
            return sum((1 << i) for i, d in enumerate(LINKS) if d in flips)

        s1 = [{} for _ in plan]
        core = []

        def own(fl):
            k = key(fl)
            core[ROUND.index(tuple(int(d in fl) for d in LINKS))].wait_recv()
            add_rows(acc.at[k], acc.at[k], cbuf.at[k], 0, rows)
            for p, (r0, rn) in enumerate(parts):
                a, b, c = plan[p]
                if a in fl:
                    j = (1 if b in fl else 0) + (2 if c in fl else 0)
                    s1[p][j] = send(acc.at[k, pl.ds(r0, rn)], b1.at[j, pl.ds(r0, rn)], a)

        for n, bits in enumerate(ROUND):
            fl = flips_of(bits, LINKS)
            products(slot_of(me, fl + ("c",)), part.at[key(fl)], slot_of(me, fl), acc.at[key(fl)])
            core.append(send(part.at[key(fl)], cbuf.at[key(fl)], "c"))
            if n > 0:
                own(flips_of(ROUND[n - 1], LINKS))
            if n % 2 == 1:
                yield
        own(())
        for _ in range(self.patience):
            yield
        s2 = [{} for _ in plan]
        for bb, cc in ((1, 1), (1, 0), (0, 1), (0, 0)):
            for p, (r0, rn) in enumerate(parts):
                a, b, c = plan[p]
                s1[p][bb + 2 * cc].wait_recv()
                k = key(flips_of((bb, cc), (b, c)))
                add_rows(acc.at[k], acc.at[k], b1.at[bb + 2 * cc], r0, rn)
                if bb:
                    s2[p][cc] = send(acc.at[k, pl.ds(r0, rn)], b2.at[cc, pl.ds(r0, rn)], b)
            if cc == 0:
                for _ in range(self.patience if bb == 0 else 1):
                    yield
        s3 = []
        for cc in (1, 0):
            for p, (r0, rn) in enumerate(parts):
                a, b, c = plan[p]
                s2[p][cc].wait_recv()
                k = key((c,) if cc else ())
                add_rows(acc.at[k], acc.at[k], b2.at[cc], r0, rn)
                if cc:
                    s3.append(send(acc.at[k, pl.ds(r0, rn)], b3.at[pl.ds(r0, rn)], c))
            yield
        for p, (r0, rn) in enumerate(parts):
            s3[p].wait_recv()
            add_rows(o_ref, acc.at[0], b3, r0, rn)
        for cp in copies:
            cp.wait_send()


class Relay:
    def __init__(self, scatter, extras, change, send, plan):
        self.scatter, self.change, self.send = scatter, change, send
        self.inputs = scatter.inputs + [(a, vmem) for a in extras]
        self.shape = (scatter.rows, scatter.cols)
        self.gather = Gather(jax.ShapeDtypeStruct(self.shape, jnp.bfloat16), plan)

    def outputs(self, groups):
        return self.scatter.outputs(groups) + self.gather.outputs(groups)

    def scratch(self, groups):
        own = [pltpu.VMEM(self.shape, jnp.bfloat16)]
        return self.scatter.scratch(groups) + self.gather.scratch(groups) + own

    def run(self, groups, src, dst, scratch):
        n = len(self.scatter.inputs)
        m = len(self.scatter.scratch(groups))
        kept, gathered = dst
        low = scratch[-1]
        yield from self.scatter.run(groups, src[:n], (kept,), scratch[:m])

        def rows(i, _):
            here = pl.ds(pl.multiple_of(i * 16, 16), 16)
            value = self.change(kept[here, :], *[a[here, :] for a in src[n:]])
            kept[here, :] = value
            low[here, :] = self.send(value).astype(low.dtype)
            return 0

        lax.fori_loop(0, self.shape[0] // 16, rows, 0)
        yield from self.gather.run(groups, (low,), (gathered,), scratch[m:-1])


def call(jobs, cid, body=None, inputs=(), outputs=(), scratch=()):
    groups = lax.axis_size("dp")
    jobs = list(jobs)
    n_in, n_out, n_scratch = len(inputs), len(outputs), len(scratch)
    job_in = [job.inputs for job in jobs]
    job_out = [job.outputs(groups) for job in jobs]
    job_scratch = [job.scratch(groups) for job in jobs]

    def kernel(*refs):
        def take(n):
            nonlocal refs
            head, refs = refs[:n], refs[n:]
            return head

        ins = take(n_in)
        src = [take(len(o)) for o in job_in]
        outs = take(n_out)
        dst = [take(len(o)) for o in job_out]
        scr = take(n_scratch)
        own = [take(len(o)) for o in job_scratch]
        greet(groups)
        alive = [job.run(groups, a, z, m) for job, a, z, m in zip(jobs, src, dst, own)]

        parked = []

        def tick():
            for job in list(alive):
                state = next(job, alive)
                if state is not None:
                    alive.remove(job)
                if state is PARK:
                    parked.append(job)

        tick()
        if body is not None:
            body(groups, tick, *ins, *outs, *scr)
        while alive:
            tick()
        for job in parked:
            next(job, None)

    out = pl.pallas_call(
        kernel,
        out_shape=list(outputs) + [o for each in job_out for o, _ in each],
        in_specs=[vmem()] * n_in + [place() for each in job_in for _, place in each],
        out_specs=[vmem()] * n_out + [place() for each in job_out for _, place in each],
        scratch_shapes=list(scratch) + [o for each in job_scratch for o in each],
        cost_estimate=COST,
        compiler_params=pltpu.CompilerParams(collective_id=cid, has_side_effects=True, vmem_limit_bytes=60 << 20),
    )(*inputs, *[a for each in job_in for a, _ in each])
    main, rest = list(out[:n_out]), list(out[n_out:])
    got = []
    for each in job_out:
        got.append(rest[: len(each)])
        rest = rest[len(each) :]
    return main, got


NEG = -1e30
CHUNK = 256
SLOTS = 4
GATHER_PLAN = Z_FIRST
FFN_SLOTS = 4
ORDER_A = ("c", "x", "y", "z")
ORDER_B = ("c", "y", "z", "x")
ORDER_C = ("c", "z", "x", "y")


def swapped(v):
    lane = lax.broadcasted_iota(jnp.int32, v.shape, 1)
    low = lax.rem(lane, HEAD_DIM) < HEAD_DIM // 2
    return jnp.where(low, pltpu.roll(v, 128 - HEAD_DIM // 2, 1), pltpu.roll(v, HEAD_DIM // 2, 1))


def low_lanes(shape):
    return lax.broadcasted_iota(jnp.int32, shape, 1) < HEAD_DIM


def as_row(column):
    return jnp.transpose(jnp.broadcast_to(column, (column.shape[0], 128)))[0:1]


def as_column(row):
    return jnp.transpose(jnp.broadcast_to(row, (128, row.shape[1])))[:, 0:1]


def attend_kernel(groups, tick, h_ref, w_ref, cos_ref, sin_ref, own_ref, idr_ref, q_ref, kv_ref, o_ref, lse_ref, top, total, acc, ssem, rsem):
    me = lax.axis_index("dp")
    tokens = cos_ref.shape[1]
    span = TEAM * tokens
    steps = span // CHUNK
    heads = q_ref.shape[0]

    def project(g, _):
        raw = jnp.dot(h_ref[g], w_ref[...], preferred_element_type=jnp.float32)
        cos = jnp.concatenate([cos_ref[g]] * 2, axis=0)
        sin = jnp.concatenate([sin_ref[g]] * 2, axis=0)
        qp, kvp = raw[:, :128], raw[:, 128:]
        low = low_lanes(qp.shape)
        qp = qp * cos + swapped(qp) * sin
        kvp = kvp * jnp.where(low, cos / SCALE, 1.0) + swapped(kvp) * jnp.where(low, sin / SCALE, 0.0)
        q_ref[0, g] = jnp.where(low, qp, 0.0).astype(jnp.bfloat16)
        q_ref[1, g] = jnp.where(low, pltpu.roll(qp, HEAD_DIM, 1), 0.0).astype(jnp.bfloat16)
        kv_ref[me, g] = kvp.astype(jnp.bfloat16)
        return 0

    lax.fori_loop(0, TEAM, project, 0)
    tick()
    copies = []
    for k in range(1, groups):
        copies.append(
            pltpu.make_async_remote_copy(
                src_ref=kv_ref.at[me], dst_ref=kv_ref.at[me], send_sem=ssem.at[k - 1], recv_sem=rsem.at[k - 1],
                device_id={"dp": lax.rem(me + k, groups)}, device_id_type=MESH,
            )
        )
        copies[-1].start()

    def block(s, i, kv, kid, begin):
        at = s * steps + i
        q = q_ref[:, pl.ds(i * SLOTS, SLOTS), s * tokens : (s + 1) * tokens, :].reshape(heads * CHUNK, 128)
        scores = lax.dot_general(q, kv, NT, preferred_element_type=jnp.float32)
        if kid is not None:
            qid = as_column(own_ref[s, :, pl.ds(i * CHUNK, CHUNK)])
            scores = jnp.where(kid <= jnp.concatenate([qid] * heads, axis=0), scores, NEG)
        peak = jnp.max(scores, axis=-1, keepdims=True)
        if not begin:
            old = top[at]
            peak = jnp.maximum(old, peak)
        weight = jnp.exp(scores - peak)
        summed = jnp.sum(weight, axis=-1, keepdims=True)
        mixed = jnp.dot(weight.astype(jnp.bfloat16), kv, preferred_element_type=jnp.float32)
        if not begin:
            factor = jnp.exp(old - peak)
            summed = summed + total[at] * factor
            mixed = mixed + acc[at] * factor
        top[at] = peak
        total[at] = summed
        acc[at] = mixed

    for s in range(2):
        for i in range(steps):
            n = min((i + 2) * CHUNK, span)
            kv = kv_ref[me, : n // tokens, s * tokens : (s + 1) * tokens, :].reshape(n, 128)
            block(s, i, kv, idr_ref[s, :, pl.ds(pl.multiple_of(me * span, 128), n)], True)
            if i % 2 == 1:
                tick()
    for k in range(1, groups):
        copies[k - 1].wait_recv()
        for s in range(2):
            for first in range(0, steps, 2):

                @pl.when(me >= k)
                def _(s=s, first=first, k=k):
                    kv = kv_ref[me - k, :, s * tokens : (s + 1) * tokens, :].reshape(span, 128)

                    def earlier(i, _):
                        block(s, i, kv, None, False)
                        return 0

                    lax.fori_loop(first, first + 2, earlier, 0)

                tick()
            if k == groups - 1:

                @pl.when(me < k)
                def _(s=s):
                    kv = kv_ref[me + 1, : CHUNK // tokens, s * tokens : (s + 1) * tokens, :].reshape(CHUNK, 128)
                    kid = idr_ref[s, :, pl.ds(pl.multiple_of((me + 1) * span, 128), CHUNK)]
                    block(s, steps - 1, kv, kid, False)

    for s in range(2):

        def finish(i, _, s=s):
            at = s * steps + i
            mixed = acc[at] / total[at]
            first, second = mixed[:CHUNK], mixed[CHUNK:]
            out = jnp.where(low_lanes(first.shape), pltpu.roll(first, HEAD_DIM, 1), second)
            o_ref[pl.ds(i * SLOTS, SLOTS), s * tokens : (s + 1) * tokens, :] = out.astype(jnp.bfloat16).reshape(SLOTS, tokens, 128)
            lse_ref[at] = as_row(top[at] + jnp.log(total[at]))
            return 0

        lax.fori_loop(0, steps, finish, 0)
    for cp in copies:
        cp.wait_send()


def attend(groups, h, w, cos, sin, id_a, id_b, cid, jobs):
    tokens = cos.shape[1]
    rows = 2 * tokens
    blocks = 2 * TEAM * tokens // CHUNK
    f32, bf16 = jnp.float32, jnp.bfloat16
    return call(
        jobs, cid, attend_kernel, [h, w, cos, sin, id_a, id_b],
        [
            jax.ShapeDtypeStruct((2, TEAM, rows, 128), bf16),
            jax.ShapeDtypeStruct((groups, TEAM, rows, 128), bf16),
            jax.ShapeDtypeStruct((TEAM, rows, 128), bf16),
            jax.ShapeDtypeStruct((blocks, 1, 2 * CHUNK), f32),
        ],
        [
            pltpu.VMEM((blocks, 2 * CHUNK, 1), f32), pltpu.VMEM((blocks, 2 * CHUNK, 1), f32),
            pltpu.VMEM((blocks, 2 * CHUNK, 128), f32), dma_sems(groups - 1), dma_sems(groups - 1),
        ],
    )


def attend_back_kernel(groups, tick, dm_ref, wo_ref, q_ref, kv_ref, o_ref, lse_ref, cos_ref, sin_ref, all_ref, own_ref, d_ref, do, gz, delta, dq, dkv, out_buf, in_buf, ssem, rsem):
    me = lax.axis_index("dp")
    tokens = cos_ref.shape[1]
    span = TEAM * tokens
    steps = span // CHUNK
    f32, bf16 = jnp.float32, jnp.bfloat16

    def project(g, _):
        part = lax.dot_general(dm_ref[g], wo_ref[...], NT, preferred_element_type=f32).astype(bf16)
        do[g] = part
        part = part.astype(f32)
        low = low_lanes(part.shape)
        gz[0, g] = jnp.where(low, 0.0, pltpu.roll(part, HEAD_DIM, 1)).astype(bf16)
        gz[1, g] = jnp.where(low, 0.0, part).astype(bf16)
        return 0

    lax.fori_loop(0, TEAM, project, 0)
    tick()
    for s in range(2):

        def deltas(i, _, s=s):
            here = (pl.ds(i * SLOTS, SLOTS), slice(s * tokens, (s + 1) * tokens), slice(None))
            both = do[here].reshape(CHUNK, 128).astype(f32) * o_ref[here].reshape(CHUNK, 128).astype(f32)
            low = low_lanes(both.shape)
            first = jnp.sum(jnp.where(low, both, 0.0), axis=-1, keepdims=True)
            second = jnp.sum(jnp.where(low, 0.0, both), axis=-1, keepdims=True)
            delta[s * steps + i] = as_row(jnp.concatenate([first, second], axis=0))
            return 0

        lax.fori_loop(0, steps, deltas, 0)
    dq[...] = jnp.zeros_like(dq)
    copies = []

    def block(s, i, n, kv, kid):
        at = s * steps + i
        here = (slice(None), pl.ds(i * SLOTS, SLOTS), slice(s * tokens, (s + 1) * tokens), slice(None))
        q = q_ref[here].reshape(2 * CHUNK, 128)
        g = gz[here].reshape(2 * CHUNK, 128)
        scores = lax.dot_general(kv, q, NT, preferred_element_type=f32)
        prob = jnp.exp(scores - lse_ref[at])
        if kid is not None:
            qid = own_ref[s, :, pl.ds(i * CHUNK, CHUNK)]
            prob = jnp.where(kid <= jnp.concatenate([qid] * 2, axis=1), prob, 0.0)
        dp = lax.dot_general(kv, g, NT, preferred_element_type=f32)
        ds = (prob * (dp - delta[at])).astype(bf16)
        part = jnp.dot(ds, q, preferred_element_type=f32)
        part = part + jnp.dot(prob.astype(bf16), g, preferred_element_type=f32)
        dkv[s, :n, :] = dkv[s, :n, :] + part
        dq[at] = dq[at] + lax.dot_general(ds, kv, TN, preferred_element_type=f32)

    for k in range(1, groups):
        for s in range(2):
            dkv[s] = jnp.zeros((span, 128), f32)
            for first in range(0, steps, 2):

                @pl.when(me + k >= groups)
                def _(s=s, first=first, k=k):
                    kv = kv_ref[me + k - groups, :, s * tokens : (s + 1) * tokens, :].reshape(span, 128)

                    def earlier(i, _):
                        block(s, i, span, kv, None)
                        return 0

                    lax.fori_loop(first, first + 2, earlier, 0)

                tick()
            if k == 1:

                @pl.when(me + 1 < groups)
                def _(s=s):
                    kv = kv_ref[me + 1, : CHUNK // tokens, s * tokens : (s + 1) * tokens, :].reshape(CHUNK, 128)
                    kid = as_column(all_ref[s, :, pl.ds(pl.multiple_of((me + 1) * span, 128), CHUNK)])
                    block(s, steps - 1, CHUNK, kv, kid)

            out_buf[k - 1, :, s * tokens : (s + 1) * tokens, :] = dkv[s].astype(bf16).reshape(TEAM, tokens, 128)
        copies.append(
            pltpu.make_async_remote_copy(
                src_ref=out_buf.at[k - 1], dst_ref=in_buf.at[k - 1], send_sem=ssem.at[k - 1], recv_sem=rsem.at[k - 1],
                device_id={"dp": lax.rem(me + k, groups)}, device_id_type=MESH,
            )
        )
        copies[-1].start()
    for s in range(2):
        dkv[s] = jnp.zeros((span, 128), f32)
        kid = as_column(all_ref[s, :, pl.ds(pl.multiple_of(me * span, 128), span)])
        for i in range(steps):
            n = min((i + 2) * CHUNK, span)
            block(s, i, n, kv_ref[me, : n // tokens, s * tokens : (s + 1) * tokens, :].reshape(n, 128), kid[:n])
            if i % 2 == 1:
                tick()
    for cp in copies:
        cp.wait_recv()
    for s in range(2):

        def finish(i, _, s=s):
            here = (pl.ds(i * SLOTS, SLOTS), slice(s * tokens, (s + 1) * tokens), slice(None))
            cos = cos_ref[pl.ds(i * SLOTS, SLOTS)].reshape(CHUNK, 128)
            sin = sin_ref[pl.ds(i * SLOTS, SLOTS)].reshape(CHUNK, 128)
            both = dq[s * steps + i]
            first, second = both[:CHUNK], both[CHUNK:]
            qp = jnp.where(low_lanes(first.shape), first, pltpu.roll(second, HEAD_DIM, 1))
            kvp = dkv[s, pl.ds(pl.multiple_of(i * CHUNK, CHUNK), CHUNK), :]
            for k in range(1, groups):
                kvp = kvp + in_buf[(k - 1,) + here].reshape(CHUNK, 128).astype(f32)
            low = low_lanes(qp.shape)
            qp = qp * cos - swapped(qp) * sin
            kvp = kvp * jnp.where(low, cos / SCALE, 1.0) - swapped(kvp) * jnp.where(low, sin / SCALE, 0.0)
            both = jnp.concatenate([qp, kvp], axis=1).astype(bf16)
            d_ref[here] = both.reshape(SLOTS, tokens, 256)
            return 0

        lax.fori_loop(0, steps, finish, 0)
    for cp in copies:
        cp.wait_send()


def attend_back(groups, dm, wo, q, kv, o, lse, cos, sin, id_a, id_b, cid, jobs):
    tokens = cos.shape[1]
    rows = 2 * tokens
    span = TEAM * tokens
    blocks = 2 * span // CHUNK
    peers = max(groups - 1, 1)
    f32, bf16 = jnp.float32, jnp.bfloat16
    return call(
        jobs, cid, attend_back_kernel, [dm, wo, q, kv, o, lse, cos, sin, id_a, id_b],
        [jax.ShapeDtypeStruct((TEAM, rows, 256), bf16)],
        [
            pltpu.VMEM((TEAM, rows, 128), bf16), pltpu.VMEM((2, TEAM, rows, 128), bf16),
            pltpu.VMEM((blocks, 1, 2 * CHUNK), f32), pltpu.VMEM((blocks, 2 * CHUNK, 128), f32),
            pltpu.VMEM((2, span, 128), f32),
            pltpu.VMEM((peers, TEAM, rows, 128), bf16), pltpu.VMEM((peers, TEAM, rows, 128), bf16),
            dma_sems(groups - 1), dma_sems(groups - 1),
        ],
    )


def ffn_kernel(h_ref, c_ref, g_ref, u_ref, d_ref, a_ref, dg_ref, du_ref, wg_ref, wu_ref, wd_ref, *sums):
    step = pl.program_id(0)
    slots, rows, model = h_ref.shape
    h = h_ref[...].reshape(slots * rows, model)
    c = c_ref[...].reshape(slots * rows, model)
    f32, bf16 = jnp.float32, jnp.bfloat16
    gate = jnp.dot(h, g_ref[...], preferred_element_type=f32)
    up = jnp.dot(h, u_ref[...], preferred_element_type=f32)
    da = jnp.dot(c, d_ref[...], preferred_element_type=f32)
    sig = 1.0 / (1.0 + jnp.exp(-gate))
    silu = gate * sig
    active = (silu * up).astype(bf16)
    d_gate = (da * up * sig * (1.0 + gate * (1.0 - sig))).astype(bf16)
    d_up = (da * silu).astype(bf16)
    for ref, value in ((a_ref, active), (dg_ref, d_gate), (du_ref, d_up)):
        ref[...] = value.reshape(slots, rows, -1)

    @pl.when(step == 0)
    def _():
        for total in sums:
            total[...] = jnp.zeros_like(total)

    wide = 512
    for first in range(0, model, wide):
        here = slice(first, first + wide)
        for total, left, right in zip(sums, (h_ref, h_ref, c_ref), (d_gate, d_up, active)):
            left = left[:, :, here].reshape(slots * rows, wide)
            total[here, :] += lax.dot_general(left, right, TN, preferred_element_type=f32)

    @pl.when(step == pl.num_programs(0) - 1)
    def _():
        for ref, total in zip((wg_ref, wu_ref, wd_ref), sums):
            ref[...] = total[...].astype(bf16)


def ffn(h, c, w_gate, w_up, w_down):
    team, rows, model = h.shape
    ff = w_gate.shape[1]
    bf16 = jnp.bfloat16
    tall = pl.BlockSpec((FFN_SLOTS, rows, model), lambda i: (i, 0, 0))
    weight = pl.BlockSpec((model, ff), lambda i: (0, 0))
    return pl.pallas_call(
        ffn_kernel,
        grid=(team // FFN_SLOTS,),
        in_specs=[tall, tall, weight, weight, weight],
        out_specs=[pl.BlockSpec((FFN_SLOTS, rows, ff), lambda i: (i, 0, 0))] * 3 + [weight] * 3,
        out_shape=[jax.ShapeDtypeStruct((team, rows, ff), bf16)] * 3 + [jax.ShapeDtypeStruct((model, ff), bf16)] * 3,
        scratch_shapes=[pltpu.VMEM((model, ff), jnp.float32)] * 3,
        cost_estimate=COST,
        compiler_params=pltpu.CompilerParams(vmem_limit_bytes=60 << 20),
    )(h, c, w_gate, w_up, w_down)


def rotation_tables(positions):
    half = HEAD_DIM // 2
    lane = jnp.arange(128, dtype=jnp.int32)
    freqs = rope_base ** (-(lane % half).astype(jnp.float32) * 2.0 / HEAD_DIM)
    angles = positions.astype(jnp.float32)[:, None] * freqs[None, :]
    sign = jnp.where(lane % HEAD_DIM < half, -SCALE, SCALE)
    return (jnp.cos(angles) * SCALE).reshape(TEAM, -1, 128), (jnp.sin(angles) * sign).reshape(TEAM, -1, 128)


def norm_back(grad, normed, scale):
    return scale * (grad - normed * jnp.mean(grad * normed, axis=-1, keepdims=True))


def rms(values):
    return lax.rsqrt(jnp.mean(values * values, axis=-1, keepdims=True) + epsilon)


def after(x, *others):
    return lax.optimization_barrier((x,) + others)[0]


def local(
    layer_input, attn_gain, query_weight, key_matrix, value_matrix, output_weight, ffn_gain,
    gate_weight, up_weight, down_weight, block_ids, cotangent,
):
    f32, bf16 = jnp.float32, jnp.bfloat16
    seqs, tokens, model = layer_input.shape
    rows = seqs * tokens
    groups = lax.axis_size("dp")
    group = lax.axis_index("dp")
    devices = groups * TEAM
    share = query_weight.shape[0]
    span = TEAM * tokens
    heads = QUERY_HEADS // TEAM
    ff = gate_weight.shape[1] // TEAM
    twin = TEAM // KEY_HEADS
    cut = heads * HEAD_DIM

    gain_one = attn_gain.astype(f32)[:, None]
    gain_two = ffn_gain.astype(f32)[:, None]

    def scaled(weight, gain):
        return (weight.astype(f32) * gain).astype(bf16)

    def doubled(weight):
        split = weight.reshape(share, KEY_HEADS, 1, HEAD_DIM)
        return jnp.broadcast_to(split, (share, KEY_HEADS, twin, HEAD_DIM)).reshape(share, TEAM, HEAD_DIM)

    def deal(k):
        return [(j, ((j + k) % groups) * TEAM + j // groups) for j in range(devices)]

    def by_member(weight):
        return jnp.moveaxis(weight.reshape(share, TEAM, -1), 1, 0)

    def in_order(mine, far):
        mine = mine.reshape(TEAM * share, -1)
        far = far.reshape((-1,) + mine.shape)
        if groups == 1:
            return mine
        if groups == 2:
            first = group == 0
            return jnp.concatenate([jnp.where(first, mine, far[0]), jnp.where(first, far[0], mine)])
        blocks = jnp.concatenate([mine[None], far])
        return jnp.take(blocks, lax.rem(group - jnp.arange(groups) + groups, groups), axis=0).reshape(model, -1)

    pack_q = by_member(scaled(query_weight, gain_one))
    pack_kv = jnp.concatenate(
        [doubled(scaled(key_matrix, gain_one)), doubled(scaled(value_matrix, gain_one))], axis=-1
    )
    pack_kv = jnp.moveaxis(pack_kv, 1, 0)
    x = layer_input.reshape(rows, model).astype(f32)
    norm_one = rms(x)
    normed_one = x * norm_one
    c_own = cotangent.reshape(rows, model)
    _, (w_q, w_kv, (h_one,)) = call(
        [Swap(pack_q, ORDER_A, True), Swap(pack_kv, ORDER_B, True), Gather(normed_one.astype(bf16), Z_FIRST, 3)], 1
    )
    w_in = jnp.concatenate([in_order(*w_q), in_order(*w_kv)], axis=-1)

    late_weight = after(output_weight, h_one)
    dealt = jnp.stack([lax.ppermute(late_weight, ALL, deal(k)) for k in range(groups)])
    if groups > 1:
        dealt = jnp.take(dealt, lax.rem(group - jnp.arange(groups) + groups, groups), axis=0)
    w_out = dealt.reshape(-1, model)

    cos, sin = rotation_tables(group * span + jnp.arange(span, dtype=jnp.int32))
    all_ids = block_ids.astype(f32)[:, None, :]
    ids = lax.dynamic_slice_in_dim(all_ids, group * span, span, 2)
    packs = (by_member(scaled(gate_weight, gain_two)), by_member(scaled(up_weight, gain_two)), by_member(down_weight))
    (q, kv, o, lse), own = attend(
        groups, h_one, w_in, cos, sin, ids, all_ids, 2,
        [Swap(a, order, patience=3) for a, order in zip(packs, (ORDER_A, ORDER_B, ORDER_C))],
    )
    own_gate, own_up, own_down = [a[0].reshape(TEAM * share, ff) for a in own]

    _, ((far_gate,), (far_up,), (far_down,), (middle, h_two), (c_all,)) = call(
        [
            Errand(own_gate, False), Errand(own_up, False, 10), Errand(own_down, False, 16),
            Relay(Scatter([(o, w_out)], False, EVEN), [x], lambda total, x: x + total, lambda mid: mid * rms(mid), GATHER_PLAN),
            Gather(c_own, GATHER_PLAN, 1, 12),
        ],
        3,
    )
    w_gate, w_up, w_down = in_order(own_gate, far_gate), in_order(own_up, far_up), in_order(own_down, far_down)
    active, d_gate, d_up, *g_ffn = ffn(h_two, c_all, w_gate, w_up, w_down)
    g_gate, g_up, g_down = [a.reshape(groups, TEAM * share, -1) for a in g_ffn]

    def outer(left, right):
        left, right = left.reshape(-1, left.shape[-1]), right.reshape(-1, right.shape[-1])
        left, right = lax.optimization_barrier((left, right))
        out = lax.dot_general(left, right, TN, preferred_element_type=f32)
        return out.astype(bf16).reshape(groups, TEAM * share, -1)

    def total(mine, far):
        out = lax.dynamic_index_in_dim(mine, group, 0, keepdims=False).astype(f32)
        for k in range(groups - 1):
            out = out + far[k].astype(f32)
        return out.astype(bf16).reshape(TEAM, share, -1)

    def home(piece):
        return jnp.moveaxis(piece[0].reshape(TEAM, share, -1).astype(f32), 0, 1)

    def back(total, c, mid):
        scale = rms(mid)
        return c.astype(f32) + norm_back(total, mid * scale, scale)

    _, ((far_gate,), (far_up,), (middle_grad, middle_low)) = call(
        [
            Errand(g_gate, True), Errand(g_up, True, 10),
            Relay(
                Scatter([(d_gate, w_gate), (d_up, w_up)], True, EVEN), [c_own, middle], back, lambda grad: grad, GATHER_PLAN
            ),
        ],
        5,
    )
    w_part, middle_low = lax.optimization_barrier((outer(o, middle_low), middle_low))
    w_part = w_part.reshape(groups, -1, model)
    pieces = []
    for k in range(groups):
        pick = lax.rem(group + groups - k, groups) if groups > 1 else 0
        mine = lax.dynamic_index_in_dim(w_part, pick, 0, keepdims=False)
        pieces.append(lax.ppermute(mine, ALL, [(b, a) for a, b in deal(k)]).astype(f32))
    grad_output = sum(pieces)
    (d_in,), ((far_down,), home_gate, home_up, (produced,)) = attend_back(
        groups, middle_low, w_out, q, kv, o, lse, cos, sin, all_ids, ids, 7,
        [
            Errand(g_down, True), Swap(total(g_gate, far_gate), ORDER_A, patience=3),
            Swap(total(g_up, far_up), ORDER_B, patience=3), Scatter([(active, w_down)], True, Z_LAST),
        ],
    )
    layer_output = (middle + produced).reshape(seqs, tokens, model)
    d_in, grad_output = lax.optimization_barrier((d_in, grad_output))
    attn = outer(h_one, d_in).reshape(groups, TEAM, share, -1)
    sum_down = total(g_down, far_down)
    thirds = (sum_down[..., : ff // 4], sum_down[..., ff // 4 : ff // 2], sum_down[..., ff // 2 :])
    _, (home_q, home_kv, (dn_one,), home_a, home_b, home_c) = call(
        [
            Swap(attn[..., :cut], ORDER_A, reduce=6), Swap(attn[..., cut:], ORDER_B, reduce=6), Scatter([(d_in, w_in)], True, EVEN),
            *[Swap(a, o, patience=3) for a, o in zip(thirds, (ORDER_A, ORDER_B, ORDER_C))],
        ],
        8,
    )
    input_grad = (middle_grad + norm_back(dn_one, normed_one, norm_one)).reshape(seqs, tokens, model)

    grad_gate, grad_up = home(home_gate).reshape(share, -1), home(home_up).reshape(share, -1)
    grad_down = jnp.concatenate([home(a) for a in (home_a, home_b, home_c)], axis=-1).reshape(share, -1)
    grad_query = home(home_q).reshape(share, -1)
    pair = home_kv[0].reshape(KEY_HEADS, twin, share, 2 * HEAD_DIM).astype(f32).sum(axis=1)
    pair = jnp.moveaxis(pair, 0, 1)
    grad_key, grad_value = pair[..., :HEAD_DIM].reshape(share, -1), pair[..., HEAD_DIM:].reshape(share, -1)

    def gain_grad(*both):
        return sum(jnp.sum(weight.astype(f32) * grad, axis=-1) for weight, grad in both)

    grad_gain_one = gain_grad((query_weight, grad_query), (key_matrix, grad_key), (value_matrix, grad_value))
    grad_gain_two = gain_grad((gate_weight, grad_gate), (up_weight, grad_up))
    return (
        layer_output, input_grad, grad_gain_one, grad_query * gain_one, grad_key * gain_one, grad_value * gain_one,
        grad_output, grad_gain_two, grad_gate * gain_two, grad_up * gain_two, grad_down,
    )


def solution(mesh):
    fine = Mesh(mesh.devices.reshape(-1, 2, 2, 2, 2), ALL)
    token = P(None, ALL, None)
    row = P(ALL, None)
    vec = P(ALL)
    in_specs = (token, vec, row, row, row, row, vec, row, row, row, P(), token)
    out_specs = (token, token, vec, row, row, row, row, vec, row, row, row)
    return jax.shard_map(local, mesh=fine, in_specs=in_specs, out_specs=out_specs, check_vma=False)
```

```python
import functools
import itertools

import jax
import jax.numpy as jnp
from jax import lax
from jax.experimental import pallas as pl
from jax.experimental.pallas import tpu as pltpu
from jax.sharding import Mesh
from jax.sharding import PartitionSpec as P

QUERY_HEADS = 32
KEY_HEADS = 8
HEAD_DIM = 64
TEAM = 16
SCALE = HEAD_DIM ** (-0.5)
epsilon = 1e-05
rope_base = 500000.0
NT = (((1,), (1,)), ((), ()))
TN = (((0,), (0,)), ((), ()))
TEAM_AXES = ("z", "y", "c", "x")
ALL = ("dp",) + TEAM_AXES
DIMS = ("z", "y", "c", "x")
WEIGHT = {"z": 8, "y": 4, "c": 2, "x": 1}
LINKS = ("x", "y", "z")
MESH = pl.DeviceIdType.MESH
COST = pl.CostEstimate(flops=30_000_000_000, bytes_accessed=1 << 20, transcendentals=0)
EVEN = (("x", "y", "z"), ("y", "z", "x"), ("z", "x", "y"))
PARK = "park"
Z_FIRST = (("z", "x", "y"), ("z", "y", "x"))
Z_LAST = (("x", "y", "z"), ("y", "x", "z"))


def part_rows(rows, count):
    tiles = rows // 16
    base = [tiles // count + (1 if i < tiles % count else 0) for i in range(count)]
    out, at = [], 0
    for b in base:
        out.append((at * 16, b * 16))
        at += b
    return out


def coords():
    return {d: lax.axis_index(d) for d in DIMS}


def slot_of(me, flips=()):
    return sum(((1 - me[d]) if d in flips else me[d]) * WEIGHT[d] for d in DIMS)


def greet(groups):
    barrier = pltpu.get_barrier_semaphore()
    me = coords()
    group = lax.axis_index("dp")
    for d in DIMS:
        pl.semaphore_signal(barrier, inc=1, device_id={d: 1 - me[d]}, device_id_type=MESH)
    for k in range(1, groups):
        pl.semaphore_signal(barrier, inc=1, device_id={"dp": lax.rem(group + k, groups)}, device_id_type=MESH)
    pl.semaphore_wait(barrier, groups - 1 + len(DIMS))


def anywhere():
    return pl.BlockSpec(memory_space=pl.ANY)


def vmem():
    return pl.BlockSpec(memory_space=pltpu.VMEM)


def dma_sems(n):
    return pltpu.SemaphoreType.DMA((max(n, 1),))


def to_groups(groups, make, ssem, rsem):
    me = lax.axis_index("dp")
    copies = []
    for k in range(1, groups):
        peer = lax.rem(me + k, groups)
        src, dst = make(k, peer)
        copies.append(
            pltpu.make_async_remote_copy(
                src_ref=src, dst_ref=dst, send_sem=ssem.at[k - 1], recv_sem=rsem.at[k - 1],
                device_id={"dp": peer}, device_id_type=MESH,
            )
        )
        copies[-1].start()
    return copies


class Errand:
    def __init__(self, array, own_block, turn=0):
        self.inputs, self.own_block, self.turn = [(array, anywhere)], own_block, turn

    def outputs(self, groups):
        a = self.inputs[0][0]
        shape = a.shape[1:] if self.own_block else a.shape
        return [(jax.ShapeDtypeStruct((max(groups - 1, 1),) + shape, a.dtype), anywhere)]

    def scratch(self, groups):
        return [dma_sems(groups - 1), dma_sems(groups - 1)]

    def run(self, groups, src, dst, scratch):
        for _ in range(self.turn):
            yield
        copies = to_groups(
            groups, lambda k, peer: (src[0].at[peer] if self.own_block else src[0], dst[0].at[k - 1]), *scratch
        )
        yield PARK
        for cp in copies:
            cp.wait()


def swap_stages(chain, order, patience, ssem, rsem, lsem):
    me = coords()
    sent = []
    for k, d in enumerate(order):
        lead = (slice(None),) * DIMS.index(d)
        a, z = chain[k], chain[k + 1]
        far = pltpu.make_async_remote_copy(
            src_ref=a.at[lead + (1 - me[d],)], dst_ref=z.at[lead + (me[d],)], send_sem=ssem.at[k],
            recv_sem=rsem.at[k], device_id={d: 1 - me[d]}, device_id_type=MESH,
        )
        near = pltpu.make_async_copy(a.at[lead + (me[d],)], z.at[lead + (me[d],)], lsem.at[k])
        far.start()
        near.start()
        sent.append(far)
        for _ in range(1 if d == "c" else patience):
            yield
        far.wait_recv()
        near.wait()
    return sent


class Swap:
    def __init__(self, array, order, far=False, reduce=0, patience=1):
        lead = array.shape[:1] if reduce else ()
        shape = array.shape[len(lead) + 1 :]
        self.shape, self.dtype = (2, 2, 2, 2) + shape, array.dtype
        self.inputs = [(array.reshape(lead + self.shape), vmem)]
        self.order, self.far, self.reduce, self.patience = order, far, reduce, patience

    def outputs(self, groups):
        out = [(jax.ShapeDtypeStruct(self.shape, self.dtype), vmem)]
        return out + [(jax.ShapeDtypeStruct((max(groups - 1, 1),) + self.shape, self.dtype), anywhere)] * self.far

    def scratch(self, groups):
        extra = [pltpu.VMEM((max(groups - 1, 1),) + self.shape, self.dtype), pltpu.VMEM(self.shape, self.dtype)]
        return (
            [pltpu.VMEM(self.shape, self.dtype)] * 3
            + [dma_sems(4), dma_sems(4), dma_sems(4), dma_sems(groups - 1), dma_sems(groups - 1)]
            + extra * (self.reduce > 0)
        )

    def run(self, groups, src, dst, scratch):
        b1, b2, b3, ssem, rsem, lsem, fs, fr = scratch[:8]
        first = src[0]
        copies = []
        if self.reduce:
            landing, first = scratch[8:]
            copies = to_groups(groups, lambda k, peer: (src[0].at[peer], landing.at[k - 1]), fs, fr)
            for _ in range(self.reduce):
                yield
            for cp in copies:
                cp.wait()
            mine = lax.axis_index("dp")

            def add(i, _):
                at = tuple(lax.rem(i // w, 2) for w in (8, 4, 2, 1))
                total = src[0][(mine,) + at].astype(jnp.float32)
                for k in range(groups - 1):
                    total = total + landing[(k,) + at].astype(jnp.float32)
                first[at] = total.astype(first.dtype)
                return 0

            lax.fori_loop(0, TEAM, add, 0)
        sent = yield from swap_stages([first, b1, b2, b3, dst[0]], self.order, self.patience, ssem, rsem, lsem)
        if self.far:
            copies = to_groups(groups, lambda k, peer: (dst[0], dst[1].at[k - 1]), fs, fr)
            yield PARK
            for cp in copies:
                cp.wait()
        for cp in sent:
            cp.wait_send()


class Gather:
    def __init__(self, x, plan, patience=1, turn=0):
        self.inputs, self.plan, self.patience, self.turn = [(x, vmem)], plan, patience, turn

    def outputs(self, groups):
        x = self.inputs[0][0]
        return [(jax.ShapeDtypeStruct((TEAM,) + x.shape, x.dtype), vmem)]

    def scratch(self, groups):
        return [dma_sems(64), dma_sems(64), pltpu.SemaphoreType.DMA]

    def run(self, groups, src, dst, scratch):
        (x_ref,), (g_ref,), (ssem, rsem, lsem) = src, dst, scratch
        for _ in range(self.turn):
            yield
        me = coords()
        rows = x_ref.shape[0]
        plan = self.plan
        parts = part_rows(rows, len(plan))
        local = pltpu.make_async_copy(x_ref, g_ref.at[slot_of(me)], lsem)
        local.start()
        counter = itertools.count()
        copies = []

        def send(flips, r0, rn, dim):
            i = next(counter)
            s = slot_of(me, flips)
            cp = pltpu.make_async_remote_copy(
                src_ref=g_ref.at[s, pl.ds(r0, rn)] if flips else x_ref.at[pl.ds(r0, rn)],
                dst_ref=g_ref.at[s, pl.ds(r0, rn)], send_sem=ssem.at[i], recv_sem=rsem.at[i],
                device_id={dim: 1 - me[dim]}, device_id_type=MESH,
            )
            cp.start()
            copies.append(cp)
            return cp

        step1 = [send((), r0, rn, plan[p][0]) for p, (r0, rn) in enumerate(parts)]
        step2 = [[send((), r0, rn, plan[p][1])] for p, (r0, rn) in enumerate(parts)]
        step3 = [[send((), r0, rn, plan[p][2])] for p, (r0, rn) in enumerate(parts)]
        core = [send((), 0, rows, "c")]
        for _ in range(self.patience):
            yield
        for p, (r0, rn) in enumerate(parts):
            a, b, c = plan[p]
            step1[p].wait_recv()
            step2[p].append(send((a,), r0, rn, b))
            step3[p].append(send((a,), r0, rn, c))
            core.append(send((a,), r0, rn, "c"))
            yield
        for j in range(2):
            for p, (r0, rn) in enumerate(parts):
                a, b, c = plan[p]
                flips = ((b,), (a, b))[j]
                step2[p][j].wait_recv()
                step3[p].append(send(flips, r0, rn, c))
                core.append(send(flips, r0, rn, "c"))
                yield
        for j in range(4):
            for p, (r0, rn) in enumerate(parts):
                a, b, c = plan[p]
                step3[p][j].wait_recv()
                core.append(send(((c,), (a, c), (b, c), (a, b, c))[j], r0, rn, "c"))
            yield
        for cp in core:
            cp.wait_recv()
        for cp in copies:
            cp.wait_send()
        local.wait()


ROUND = [(1, 1, 1), (0, 1, 1), (1, 0, 1), (1, 1, 0), (1, 0, 0), (0, 1, 0), (0, 0, 1), (0, 0, 0)]


def flips_of(bits, order):
    return tuple(d for b, d in zip(bits, order) if b)


def add_rows(dst, a, b, r0, rn):
    def body(i, _):
        r = pl.multiple_of(r0 + i * 16, 16)
        dst[pl.ds(r, 16)] = (a[pl.ds(r, 16)].astype(jnp.float32) + b[pl.ds(r, 16)].astype(jnp.float32)).astype(dst.dtype)
        return 0

    lax.fori_loop(0, rn // 16, body, 0)


class Scatter:
    def __init__(self, pairs, flip, plan, patience=1):
        self.inputs = [(m, vmem) for pair in pairs for m in pair]
        self.flip, self.plan, self.patience = flip, plan, patience
        w = pairs[0][1]
        self.rows, self.cols = pairs[0][0].shape[1], w.shape[0] if flip else w.shape[1]

    def outputs(self, groups):
        return [(jax.ShapeDtypeStruct((self.rows, self.cols), jnp.float32), vmem)]

    def scratch(self, groups):
        block = [pltpu.VMEM((n, self.rows, self.cols), jnp.bfloat16) for n in (8, 8, 8, 4, 2)]
        return block + [pltpu.VMEM((self.rows, self.cols), jnp.bfloat16), dma_sems(32), dma_sems(32)]

    def run(self, groups, src, dst, scratch):
        part, acc, cbuf, b1, b2, b3, ssem, rsem = scratch
        (o_ref,) = dst
        pairs = list(zip(src[::2], src[1::2]))
        me = coords()
        plan, rows, cols = self.plan, self.rows, self.cols
        parts = part_rows(rows, len(plan))
        counter = itertools.count()
        copies = []

        def send(a, z, dim):
            i = next(counter)
            cp = pltpu.make_async_remote_copy(
                src_ref=a, dst_ref=z, send_sem=ssem.at[i], recv_sem=rsem.at[i],
                device_id={dim: 1 - me[dim]}, device_id_type=MESH,
            )
            cp.start()
            copies.append(cp)
            return cp

        def products(theirs, z, ours, y):
            def column(j, _):
                here = pl.ds(pl.multiple_of(j * 512, 512), 512)
                total = None
                for a, w in pairs:
                    left = jnp.concatenate([a[theirs], a[ours]], axis=0)
                    if self.flip:
                        out = lax.dot_general(left, w[here, :], NT, preferred_element_type=jnp.float32)
                    else:
                        out = jnp.dot(left, w[:, here], preferred_element_type=jnp.float32)
                    total = out if total is None else total + out
                total = total.astype(z.dtype)
                z[:, here] = total[:rows]
                y[:, here] = total[rows:]
                return 0

            lax.fori_loop(0, cols // 512, column, 0)

        def key(flips):
            return sum((1 << i) for i, d in enumerate(LINKS) if d in flips)

        s1 = [{} for _ in plan]
        core = []

        def own(fl):
            k = key(fl)
            core[ROUND.index(tuple(int(d in fl) for d in LINKS))].wait_recv()
            add_rows(acc.at[k], acc.at[k], cbuf.at[k], 0, rows)
            for p, (r0, rn) in enumerate(parts):
                a, b, c = plan[p]
                if a in fl:
                    j = (1 if b in fl else 0) + (2 if c in fl else 0)
                    s1[p][j] = send(acc.at[k, pl.ds(r0, rn)], b1.at[j, pl.ds(r0, rn)], a)

        for n, bits in enumerate(ROUND):
            fl = flips_of(bits, LINKS)
            products(slot_of(me, fl + ("c",)), part.at[key(fl)], slot_of(me, fl), acc.at[key(fl)])
            core.append(send(part.at[key(fl)], cbuf.at[key(fl)], "c"))
            if n > 0:
                own(flips_of(ROUND[n - 1], LINKS))
            if n % 2 == 1:
                yield
        own(())
        for _ in range(self.patience):
            yield
        s2 = [{} for _ in plan]
        for bb, cc in ((1, 1), (1, 0), (0, 1), (0, 0)):
            for p, (r0, rn) in enumerate(parts):
                a, b, c = plan[p]
                s1[p][bb + 2 * cc].wait_recv()
                k = key(flips_of((bb, cc), (b, c)))
                add_rows(acc.at[k], acc.at[k], b1.at[bb + 2 * cc], r0, rn)
                if bb:
                    s2[p][cc] = send(acc.at[k, pl.ds(r0, rn)], b2.at[cc, pl.ds(r0, rn)], b)
            if cc == 0:
                for _ in range(self.patience if bb == 0 else 1):
                    yield
        s3 = []
        for cc in (1, 0):
            for p, (r0, rn) in enumerate(parts):
                a, b, c = plan[p]
                s2[p][cc].wait_recv()
                k = key((c,) if cc else ())
                add_rows(acc.at[k], acc.at[k], b2.at[cc], r0, rn)
                if cc:
                    s3.append(send(acc.at[k, pl.ds(r0, rn)], b3.at[pl.ds(r0, rn)], c))
            yield
        for p, (r0, rn) in enumerate(parts):
            s3[p].wait_recv()
            add_rows(o_ref, acc.at[0], b3, r0, rn)
        for cp in copies:
            cp.wait_send()


class Relay:
    def __init__(self, scatter, extras, change, send, plan):
        self.scatter, self.change, self.send = scatter, change, send
        self.inputs = scatter.inputs + [(a, vmem) for a in extras]
        self.shape = (scatter.rows, scatter.cols)
        self.gather = Gather(jax.ShapeDtypeStruct(self.shape, jnp.bfloat16), plan)

    def outputs(self, groups):
        return self.scatter.outputs(groups) + self.gather.outputs(groups)

    def scratch(self, groups):
        own = [pltpu.VMEM(self.shape, jnp.bfloat16)]
        return self.scatter.scratch(groups) + self.gather.scratch(groups) + own

    def run(self, groups, src, dst, scratch):
        n = len(self.scatter.inputs)
        m = len(self.scatter.scratch(groups))
        kept, gathered = dst
        low = scratch[-1]
        yield from self.scatter.run(groups, src[:n], (kept,), scratch[:m])

        def rows(i, _):
            here = pl.ds(pl.multiple_of(i * 16, 16), 16)
            value = self.change(kept[here, :], *[a[here, :] for a in src[n:]])
            kept[here, :] = value
            low[here, :] = self.send(value).astype(low.dtype)
            return 0

        lax.fori_loop(0, self.shape[0] // 16, rows, 0)
        yield from self.gather.run(groups, (low,), (gathered,), scratch[m:-1])


def call(jobs, cid, body=None, inputs=(), outputs=(), scratch=()):
    groups = lax.axis_size("dp")
    jobs = list(jobs)
    n_in, n_out, n_scratch = len(inputs), len(outputs), len(scratch)
    job_in = [job.inputs for job in jobs]
    job_out = [job.outputs(groups) for job in jobs]
    job_scratch = [job.scratch(groups) for job in jobs]

    def kernel(*refs):
        def take(n):
            nonlocal refs
            head, refs = refs[:n], refs[n:]
            return head

        ins = take(n_in)
        src = [take(len(o)) for o in job_in]
        outs = take(n_out)
        dst = [take(len(o)) for o in job_out]
        scr = take(n_scratch)
        own = [take(len(o)) for o in job_scratch]
        greet(groups)
        alive = [job.run(groups, a, z, m) for job, a, z, m in zip(jobs, src, dst, own)]

        parked = []

        def tick():
            for job in list(alive):
                state = next(job, alive)
                if state is not None:
                    alive.remove(job)
                if state is PARK:
                    parked.append(job)

        tick()
        if body is not None:
            body(groups, tick, *ins, *outs, *scr)
        while alive:
            tick()
        for job in parked:
            next(job, None)

    out = pl.pallas_call(
        kernel,
        out_shape=list(outputs) + [o for each in job_out for o, _ in each],
        in_specs=[vmem()] * n_in + [place() for each in job_in for _, place in each],
        out_specs=[vmem()] * n_out + [place() for each in job_out for _, place in each],
        scratch_shapes=list(scratch) + [o for each in job_scratch for o in each],
        cost_estimate=COST,
        compiler_params=pltpu.CompilerParams(collective_id=cid, has_side_effects=True, vmem_limit_bytes=60 << 20),
    )(*inputs, *[a for each in job_in for a, _ in each])
    main, rest = list(out[:n_out]), list(out[n_out:])
    got = []
    for each in job_out:
        got.append(rest[: len(each)])
        rest = rest[len(each) :]
    return main, got


NEG = -1e30
CHUNK = 256
SLOTS = 4
GATHER_PLAN = Z_FIRST
FFN_SLOTS = 4
ORDER_A = ("c", "x", "y", "z")
ORDER_B = ("c", "y", "z", "x")
ORDER_C = ("c", "z", "x", "y")


def swapped(v):
    lane = lax.broadcasted_iota(jnp.int32, v.shape, 1)
    low = lax.rem(lane, HEAD_DIM) < HEAD_DIM // 2
    return jnp.where(low, pltpu.roll(v, 128 - HEAD_DIM // 2, 1), pltpu.roll(v, HEAD_DIM // 2, 1))


def low_lanes(shape):
    return lax.broadcasted_iota(jnp.int32, shape, 1) < HEAD_DIM


def as_row(column):
    return jnp.transpose(jnp.broadcast_to(column, (column.shape[0], 128)))[0:1]


def as_column(row):
    return jnp.transpose(jnp.broadcast_to(row, (128, row.shape[1])))[:, 0:1]


def attend_kernel(groups, tick, h_ref, w_ref, cos_ref, sin_ref, own_ref, idr_ref, q_ref, kv_ref, o_ref, lse_ref, top, total, acc, ssem, rsem):
    me = lax.axis_index("dp")
    tokens = cos_ref.shape[1]
    span = TEAM * tokens
    steps = span // CHUNK
    heads = q_ref.shape[0]

    def project(g, _):
        raw = jnp.dot(h_ref[g], w_ref[...], preferred_element_type=jnp.float32)
        cos = jnp.concatenate([cos_ref[g]] * 2, axis=0)
        sin = jnp.concatenate([sin_ref[g]] * 2, axis=0)
        qp, kvp = raw[:, :128], raw[:, 128:]
        low = low_lanes(qp.shape)
        qp = qp * cos + swapped(qp) * sin
        kvp = kvp * jnp.where(low, cos / SCALE, 1.0) + swapped(kvp) * jnp.where(low, sin / SCALE, 0.0)
        q_ref[0, g] = jnp.where(low, qp, 0.0).astype(jnp.bfloat16)
        q_ref[1, g] = jnp.where(low, pltpu.roll(qp, HEAD_DIM, 1), 0.0).astype(jnp.bfloat16)
        kv_ref[me, g] = kvp.astype(jnp.bfloat16)
        return 0

    lax.fori_loop(0, TEAM, project, 0)
    tick()
    copies = []
    for k in range(1, groups):
        copies.append(
            pltpu.make_async_remote_copy(
                src_ref=kv_ref.at[me], dst_ref=kv_ref.at[me], send_sem=ssem.at[k - 1], recv_sem=rsem.at[k - 1],
                device_id={"dp": lax.rem(me + k, groups)}, device_id_type=MESH,
            )
        )
        copies[-1].start()

    def block(s, i, kv, kid, begin):
        at = s * steps + i
        q = q_ref[:, pl.ds(i * SLOTS, SLOTS), s * tokens : (s + 1) * tokens, :].reshape(heads * CHUNK, 128)
        scores = lax.dot_general(q, kv, NT, preferred_element_type=jnp.float32)
        if kid is not None:
            qid = as_column(own_ref[s, :, pl.ds(i * CHUNK, CHUNK)])
            scores = jnp.where(kid <= jnp.concatenate([qid] * heads, axis=0), scores, NEG)
        peak = jnp.max(scores, axis=-1, keepdims=True)
        if not begin:
            old = top[at]
            peak = jnp.maximum(old, peak)
        weight = jnp.exp(scores - peak)
        summed = jnp.sum(weight, axis=-1, keepdims=True)
        mixed = jnp.dot(weight.astype(jnp.bfloat16), kv, preferred_element_type=jnp.float32)
        if not begin:
            factor = jnp.exp(old - peak)
            summed = summed + total[at] * factor
            mixed = mixed + acc[at] * factor
        top[at] = peak
        total[at] = summed
        acc[at] = mixed

    for s in range(2):
        for i in range(steps):
            n = min((i + 2) * CHUNK, span)
            kv = kv_ref[me, : n // tokens, s * tokens : (s + 1) * tokens, :].reshape(n, 128)
            block(s, i, kv, idr_ref[s, :, pl.ds(pl.multiple_of(me * span, 128), n)], True)
            if i % 2 == 1:
                tick()
    for k in range(1, groups):
        copies[k - 1].wait_recv()
        for s in range(2):
            for first in range(0, steps, 2):

                @pl.when(me >= k)
                def _(s=s, first=first, k=k):
                    kv = kv_ref[me - k, :, s * tokens : (s + 1) * tokens, :].reshape(span, 128)

                    def earlier(i, _):
                        block(s, i, kv, None, False)
                        return 0

                    lax.fori_loop(first, first + 2, earlier, 0)

                tick()
            if k == groups - 1:

                @pl.when(me < k)
                def _(s=s):
                    kv = kv_ref[me + 1, : CHUNK // tokens, s * tokens : (s + 1) * tokens, :].reshape(CHUNK, 128)
                    kid = idr_ref[s, :, pl.ds(pl.multiple_of((me + 1) * span, 128), CHUNK)]
                    block(s, steps - 1, kv, kid, False)

    for s in range(2):

        def finish(i, _, s=s):
            at = s * steps + i
            mixed = acc[at] / total[at]
            first, second = mixed[:CHUNK], mixed[CHUNK:]
            out = jnp.where(low_lanes(first.shape), pltpu.roll(first, HEAD_DIM, 1), second)
            o_ref[pl.ds(i * SLOTS, SLOTS), s * tokens : (s + 1) * tokens, :] = out.astype(jnp.bfloat16).reshape(SLOTS, tokens, 128)
            lse_ref[at] = as_row(top[at] + jnp.log(total[at]))
            return 0

        lax.fori_loop(0, steps, finish, 0)
    for cp in copies:
        cp.wait_send()


def attend(groups, h, w, cos, sin, id_a, id_b, cid, jobs):
    tokens = cos.shape[1]
    rows = 2 * tokens
    blocks = 2 * TEAM * tokens // CHUNK
    f32, bf16 = jnp.float32, jnp.bfloat16
    return call(
        jobs, cid, attend_kernel, [h, w, cos, sin, id_a, id_b],
        [
            jax.ShapeDtypeStruct((2, TEAM, rows, 128), bf16),
            jax.ShapeDtypeStruct((groups, TEAM, rows, 128), bf16),
            jax.ShapeDtypeStruct((TEAM, rows, 128), bf16),
            jax.ShapeDtypeStruct((blocks, 1, 2 * CHUNK), f32),
        ],
        [
            pltpu.VMEM((blocks, 2 * CHUNK, 1), f32), pltpu.VMEM((blocks, 2 * CHUNK, 1), f32),
            pltpu.VMEM((blocks, 2 * CHUNK, 128), f32), dma_sems(groups - 1), dma_sems(groups - 1),
        ],
    )


def attend_back_kernel(groups, tick, dm_ref, wo_ref, q_ref, kv_ref, o_ref, lse_ref, cos_ref, sin_ref, all_ref, own_ref, d_ref, do, gz, delta, dq, dkv, out_buf, in_buf, ssem, rsem):
    me = lax.axis_index("dp")
    tokens = cos_ref.shape[1]
    span = TEAM * tokens
    steps = span // CHUNK
    f32, bf16 = jnp.float32, jnp.bfloat16

    def project(g, _):
        part = lax.dot_general(dm_ref[g], wo_ref[...], NT, preferred_element_type=f32).astype(bf16)
        do[g] = part
        part = part.astype(f32)
        low = low_lanes(part.shape)
        gz[0, g] = jnp.where(low, 0.0, pltpu.roll(part, HEAD_DIM, 1)).astype(bf16)
        gz[1, g] = jnp.where(low, 0.0, part).astype(bf16)
        return 0

    lax.fori_loop(0, TEAM, project, 0)
    tick()
    for s in range(2):

        def deltas(i, _, s=s):
            here = (pl.ds(i * SLOTS, SLOTS), slice(s * tokens, (s + 1) * tokens), slice(None))
            both = do[here].reshape(CHUNK, 128).astype(f32) * o_ref[here].reshape(CHUNK, 128).astype(f32)
            low = low_lanes(both.shape)
            first = jnp.sum(jnp.where(low, both, 0.0), axis=-1, keepdims=True)
            second = jnp.sum(jnp.where(low, 0.0, both), axis=-1, keepdims=True)
            delta[s * steps + i] = as_row(jnp.concatenate([first, second], axis=0))
            return 0

        lax.fori_loop(0, steps, deltas, 0)
    dq[...] = jnp.zeros_like(dq)
    copies = []

    def block(s, i, n, kv, kid):
        at = s * steps + i
        here = (slice(None), pl.ds(i * SLOTS, SLOTS), slice(s * tokens, (s + 1) * tokens), slice(None))
        q = q_ref[here].reshape(2 * CHUNK, 128)
        g = gz[here].reshape(2 * CHUNK, 128)
        scores = lax.dot_general(kv, q, NT, preferred_element_type=f32)
        prob = jnp.exp(scores - lse_ref[at])
        if kid is not None:
            qid = own_ref[s, :, pl.ds(i * CHUNK, CHUNK)]
            prob = jnp.where(kid <= jnp.concatenate([qid] * 2, axis=1), prob, 0.0)
        dp = lax.dot_general(kv, g, NT, preferred_element_type=f32)
        ds = (prob * (dp - delta[at])).astype(bf16)
        part = jnp.dot(ds, q, preferred_element_type=f32)
        part = part + jnp.dot(prob.astype(bf16), g, preferred_element_type=f32)
        dkv[s, :n, :] = dkv[s, :n, :] + part
        dq[at] = dq[at] + lax.dot_general(ds, kv, TN, preferred_element_type=f32)

    for k in range(1, groups):
        for s in range(2):
            dkv[s] = jnp.zeros((span, 128), f32)
            for first in range(0, steps, 2):

                @pl.when(me + k >= groups)
                def _(s=s, first=first, k=k):
                    kv = kv_ref[me + k - groups, :, s * tokens : (s + 1) * tokens, :].reshape(span, 128)

                    def earlier(i, _):
                        block(s, i, span, kv, None)
                        return 0

                    lax.fori_loop(first, first + 2, earlier, 0)

                tick()
            if k == 1:

                @pl.when(me + 1 < groups)
                def _(s=s):
                    kv = kv_ref[me + 1, : CHUNK // tokens, s * tokens : (s + 1) * tokens, :].reshape(CHUNK, 128)
                    kid = as_column(all_ref[s, :, pl.ds(pl.multiple_of((me + 1) * span, 128), CHUNK)])
                    block(s, steps - 1, CHUNK, kv, kid)

            out_buf[k - 1, :, s * tokens : (s + 1) * tokens, :] = dkv[s].astype(bf16).reshape(TEAM, tokens, 128)
        copies.append(
            pltpu.make_async_remote_copy(
                src_ref=out_buf.at[k - 1], dst_ref=in_buf.at[k - 1], send_sem=ssem.at[k - 1], recv_sem=rsem.at[k - 1],
                device_id={"dp": lax.rem(me + k, groups)}, device_id_type=MESH,
            )
        )
        copies[-1].start()
    for s in range(2):
        dkv[s] = jnp.zeros((span, 128), f32)
        kid = as_column(all_ref[s, :, pl.ds(pl.multiple_of(me * span, 128), span)])
        for i in range(steps):
            n = min((i + 2) * CHUNK, span)
            block(s, i, n, kv_ref[me, : n // tokens, s * tokens : (s + 1) * tokens, :].reshape(n, 128), kid[:n])
            if i % 2 == 1:
                tick()
    for cp in copies:
        cp.wait_recv()
    for s in range(2):

        def finish(i, _, s=s):
            here = (pl.ds(i * SLOTS, SLOTS), slice(s * tokens, (s + 1) * tokens), slice(None))
            cos = cos_ref[pl.ds(i * SLOTS, SLOTS)].reshape(CHUNK, 128)
            sin = sin_ref[pl.ds(i * SLOTS, SLOTS)].reshape(CHUNK, 128)
            both = dq[s * steps + i]
            first, second = both[:CHUNK], both[CHUNK:]
            qp = jnp.where(low_lanes(first.shape), first, pltpu.roll(second, HEAD_DIM, 1))
            kvp = dkv[s, pl.ds(pl.multiple_of(i * CHUNK, CHUNK), CHUNK), :]
            for k in range(1, groups):
                kvp = kvp + in_buf[(k - 1,) + here].reshape(CHUNK, 128).astype(f32)
            low = low_lanes(qp.shape)
            qp = qp * cos - swapped(qp) * sin
            kvp = kvp * jnp.where(low, cos / SCALE, 1.0) - swapped(kvp) * jnp.where(low, sin / SCALE, 0.0)
            both = jnp.concatenate([qp, kvp], axis=1).astype(bf16)
            d_ref[here] = both.reshape(SLOTS, tokens, 256)
            return 0

        lax.fori_loop(0, steps, finish, 0)
    for cp in copies:
        cp.wait_send()


def attend_back(groups, dm, wo, q, kv, o, lse, cos, sin, id_a, id_b, cid, jobs):
    tokens = cos.shape[1]
    rows = 2 * tokens
    span = TEAM * tokens
    blocks = 2 * span // CHUNK
    peers = max(groups - 1, 1)
    f32, bf16 = jnp.float32, jnp.bfloat16
    return call(
        jobs, cid, attend_back_kernel, [dm, wo, q, kv, o, lse, cos, sin, id_a, id_b],
        [jax.ShapeDtypeStruct((TEAM, rows, 256), bf16)],
        [
            pltpu.VMEM((TEAM, rows, 128), bf16), pltpu.VMEM((2, TEAM, rows, 128), bf16),
            pltpu.VMEM((blocks, 1, 2 * CHUNK), f32), pltpu.VMEM((blocks, 2 * CHUNK, 128), f32),
            pltpu.VMEM((2, span, 128), f32),
            pltpu.VMEM((peers, TEAM, rows, 128), bf16), pltpu.VMEM((peers, TEAM, rows, 128), bf16),
            dma_sems(groups - 1), dma_sems(groups - 1),
        ],
    )


def ffn_kernel(h_ref, c_ref, g_ref, u_ref, d_ref, a_ref, dg_ref, du_ref, wg_ref, wu_ref, wd_ref, *sums):
    step = pl.program_id(0)
    slots, rows, model = h_ref.shape
    h = h_ref[...].reshape(slots * rows, model)
    c = c_ref[...].reshape(slots * rows, model)
    f32, bf16 = jnp.float32, jnp.bfloat16
    gate = jnp.dot(h, g_ref[...], preferred_element_type=f32)
    up = jnp.dot(h, u_ref[...], preferred_element_type=f32)
    da = jnp.dot(c, d_ref[...], preferred_element_type=f32)
    sig = 1.0 / (1.0 + jnp.exp(-gate))
    silu = gate * sig
    active = (silu * up).astype(bf16)
    d_gate = (da * up * sig * (1.0 + gate * (1.0 - sig))).astype(bf16)
    d_up = (da * silu).astype(bf16)
    for ref, value in ((a_ref, active), (dg_ref, d_gate), (du_ref, d_up)):
        ref[...] = value.reshape(slots, rows, -1)

    @pl.when(step == 0)
    def _():
        for total in sums:
            total[...] = jnp.zeros_like(total)

    wide = 512
    for first in range(0, model, wide):
        here = slice(first, first + wide)
        for total, left, right in zip(sums, (h_ref, h_ref, c_ref), (d_gate, d_up, active)):
            left = left[:, :, here].reshape(slots * rows, wide)
            total[here, :] += lax.dot_general(left, right, TN, preferred_element_type=f32)

    @pl.when(step == pl.num_programs(0) - 1)
    def _():
        for ref, total in zip((wg_ref, wu_ref, wd_ref), sums):
            ref[...] = total[...].astype(bf16)


def ffn(h, c, w_gate, w_up, w_down):
    team, rows, model = h.shape
    ff = w_gate.shape[1]
    bf16 = jnp.bfloat16
    tall = pl.BlockSpec((FFN_SLOTS, rows, model), lambda i: (i, 0, 0))
    weight = pl.BlockSpec((model, ff), lambda i: (0, 0))
    return pl.pallas_call(
        ffn_kernel,
        grid=(team // FFN_SLOTS,),
        in_specs=[tall, tall, weight, weight, weight],
        out_specs=[pl.BlockSpec((FFN_SLOTS, rows, ff), lambda i: (i, 0, 0))] * 3 + [weight] * 3,
        out_shape=[jax.ShapeDtypeStruct((team, rows, ff), bf16)] * 3 + [jax.ShapeDtypeStruct((model, ff), bf16)] * 3,
        scratch_shapes=[pltpu.VMEM((model, ff), jnp.float32)] * 3,
        cost_estimate=COST,
        compiler_params=pltpu.CompilerParams(vmem_limit_bytes=60 << 20),
    )(h, c, w_gate, w_up, w_down)


def rotation_tables(positions):
    half = HEAD_DIM // 2
    lane = jnp.arange(128, dtype=jnp.int32)
    freqs = rope_base ** (-(lane % half).astype(jnp.float32) * 2.0 / HEAD_DIM)
    angles = positions.astype(jnp.float32)[:, None] * freqs[None, :]
    sign = jnp.where(lane % HEAD_DIM < half, -SCALE, SCALE)
    return (jnp.cos(angles) * SCALE).reshape(TEAM, -1, 128), (jnp.sin(angles) * sign).reshape(TEAM, -1, 128)


def norm_back(grad, normed, scale):
    return scale * (grad - normed * jnp.mean(grad * normed, axis=-1, keepdims=True))


def rms(values):
    return lax.rsqrt(jnp.mean(values * values, axis=-1, keepdims=True) + epsilon)


def after(x, *others):
    return lax.optimization_barrier((x,) + others)[0]


def local(
    layer_input, attn_gain, query_weight, key_matrix, value_matrix, output_weight, ffn_gain,
    gate_weight, up_weight, down_weight, block_ids, cotangent,
):
    f32, bf16 = jnp.float32, jnp.bfloat16
    seqs, tokens, model = layer_input.shape
    rows = seqs * tokens
    groups = lax.axis_size("dp")
    group = lax.axis_index("dp")
    devices = groups * TEAM
    share = query_weight.shape[0]
    span = TEAM * tokens
    heads = QUERY_HEADS // TEAM
    ff = gate_weight.shape[1] // TEAM
    twin = TEAM // KEY_HEADS
    cut = heads * HEAD_DIM

    gain_one = attn_gain.astype(f32)[:, None]
    gain_two = ffn_gain.astype(f32)[:, None]

    def scaled(weight, gain):
        return (weight.astype(f32) * gain).astype(bf16)

    def doubled(weight):
        split = weight.reshape(share, KEY_HEADS, 1, HEAD_DIM)
        return jnp.broadcast_to(split, (share, KEY_HEADS, twin, HEAD_DIM)).reshape(share, TEAM, HEAD_DIM)

    def deal(k):
        return [(j, ((j + k) % groups) * TEAM + j // groups) for j in range(devices)]

    def by_member(weight):
        return jnp.moveaxis(weight.reshape(share, TEAM, -1), 1, 0)

    def in_order(mine, far):
        mine = mine.reshape(TEAM * share, -1)
        far = far.reshape((-1,) + mine.shape)
        if groups == 1:
            return mine
        if groups == 2:
            first = group == 0
            return jnp.concatenate([jnp.where(first, mine, far[0]), jnp.where(first, far[0], mine)])
        blocks = jnp.concatenate([mine[None], far])
        return jnp.take(blocks, lax.rem(group - jnp.arange(groups) + groups, groups), axis=0).reshape(model, -1)

    pack_q = by_member(scaled(query_weight, gain_one))
    pack_kv = jnp.concatenate(
        [doubled(scaled(key_matrix, gain_one)), doubled(scaled(value_matrix, gain_one))], axis=-1
    )
    pack_kv = jnp.moveaxis(pack_kv, 1, 0)
    x = layer_input.reshape(rows, model).astype(f32)
    norm_one = rms(x)
    normed_one = x * norm_one
    c_own = cotangent.reshape(rows, model)
    _, (w_q, w_kv, (h_one,)) = call(
        [Swap(pack_q, ORDER_A, True), Swap(pack_kv, ORDER_B, True), Gather(normed_one.astype(bf16), Z_FIRST, 3)], 1
    )
    w_in = jnp.concatenate([in_order(*w_q), in_order(*w_kv)], axis=-1)

    late_weight = after(output_weight, h_one)
    dealt = jnp.stack([lax.ppermute(late_weight, ALL, deal(k)) for k in range(groups)])
    if groups > 1:
        dealt = jnp.take(dealt, lax.rem(group - jnp.arange(groups) + groups, groups), axis=0)
    w_out = dealt.reshape(-1, model)

    cos, sin = rotation_tables(group * span + jnp.arange(span, dtype=jnp.int32))
    all_ids = block_ids.astype(f32)[:, None, :]
    ids = lax.dynamic_slice_in_dim(all_ids, group * span, span, 2)
    packs = (by_member(scaled(gate_weight, gain_two)), by_member(scaled(up_weight, gain_two)), by_member(down_weight))
    (q, kv, o, lse), own = attend(
        groups, h_one, w_in, cos, sin, ids, all_ids, 2,
        [Swap(a, order, patience=3) for a, order in zip(packs, (ORDER_A, ORDER_B, ORDER_C))],
    )
    own_gate, own_up, own_down = [a[0].reshape(TEAM * share, ff) for a in own]

    _, ((far_gate,), (far_up,), (far_down,), (middle, h_two), (c_all,)) = call(
        [
            Errand(own_gate, False), Errand(own_up, False, 10), Errand(own_down, False, 16),
            Relay(Scatter([(o, w_out)], False, EVEN), [x], lambda total, x: x + total, lambda mid: mid * rms(mid), GATHER_PLAN),
            Gather(c_own, GATHER_PLAN, 1, 12),
        ],
        3,
    )
    w_gate, w_up, w_down = in_order(own_gate, far_gate), in_order(own_up, far_up), in_order(own_down, far_down)
    active, d_gate, d_up, *g_ffn = ffn(h_two, c_all, w_gate, w_up, w_down)
    g_gate, g_up, g_down = [a.reshape(groups, TEAM * share, -1) for a in g_ffn]

    def outer(left, right):
        left, right = left.reshape(-1, left.shape[-1]), right.reshape(-1, right.shape[-1])
        left, right = lax.optimization_barrier((left, right))
        out = lax.dot_general(left, right, TN, preferred_element_type=f32)
        return out.astype(bf16).reshape(groups, TEAM * share, -1)

    def total(mine, far):
        out = lax.dynamic_index_in_dim(mine, group, 0, keepdims=False).astype(f32)
        for k in range(groups - 1):
            out = out + far[k].astype(f32)
        return out.astype(bf16).reshape(TEAM, share, -1)

    def home(piece):
        return jnp.moveaxis(piece[0].reshape(TEAM, share, -1).astype(f32), 0, 1)

    def back(total, c, mid):
        scale = rms(mid)
        return c.astype(f32) + norm_back(total, mid * scale, scale)

    _, ((far_gate,), (far_up,), (middle_grad, middle_low)) = call(
        [
            Errand(g_gate, True), Errand(g_up, True, 10),
            Relay(
                Scatter([(d_gate, w_gate), (d_up, w_up)], True, EVEN), [c_own, middle], back, lambda grad: grad, GATHER_PLAN
            ),
        ],
        5,
    )
    w_part, middle_low = lax.optimization_barrier((outer(o, middle_low), middle_low))
    w_part = w_part.reshape(groups, -1, model)
    pieces = []
    for k in range(groups):
        pick = lax.rem(group + groups - k, groups) if groups > 1 else 0
        mine = lax.dynamic_index_in_dim(w_part, pick, 0, keepdims=False)
        pieces.append(lax.ppermute(mine, ALL, [(b, a) for a, b in deal(k)]).astype(f32))
    grad_output = sum(pieces)
    (d_in,), ((far_down,), home_gate, home_up, (produced,)) = attend_back(
        groups, middle_low, w_out, q, kv, o, lse, cos, sin, all_ids, ids, 7,
        [
            Errand(g_down, True), Swap(total(g_gate, far_gate), ORDER_A, patience=3),
            Swap(total(g_up, far_up), ORDER_B, patience=3), Scatter([(active, w_down)], True, Z_LAST, 2),
        ],
    )
    layer_output = (middle + produced).reshape(seqs, tokens, model)
    attn = outer(h_one, d_in).reshape(groups, TEAM, share, -1)
    sum_down = total(g_down, far_down)
    thirds = (sum_down[..., : ff // 4], sum_down[..., ff // 4 : ff // 2], sum_down[..., ff // 2 :])
    _, (home_q, home_kv, (dn_one,), home_a, home_b, home_c) = call(
        [
            Swap(attn[..., :cut], ORDER_A, reduce=6), Swap(attn[..., cut:], ORDER_B, reduce=6), Scatter([(d_in, w_in)], True, EVEN),
            *[Swap(a, o, patience=3) for a, o in zip(thirds, (ORDER_A, ORDER_B, ORDER_C))],
        ],
        8,
    )
    input_grad = (middle_grad + norm_back(dn_one, normed_one, norm_one)).reshape(seqs, tokens, model)

    grad_gate, grad_up = home(home_gate).reshape(share, -1), home(home_up).reshape(share, -1)
    grad_down = jnp.concatenate([home(a) for a in (home_a, home_b, home_c)], axis=-1).reshape(share, -1)
    grad_query = home(home_q).reshape(share, -1)
    pair = home_kv[0].reshape(KEY_HEADS, twin, share, 2 * HEAD_DIM).astype(f32).sum(axis=1)
    pair = jnp.moveaxis(pair, 0, 1)
    grad_key, grad_value = pair[..., :HEAD_DIM].reshape(share, -1), pair[..., HEAD_DIM:].reshape(share, -1)

    def gain_grad(*both):
        return sum(jnp.sum(weight.astype(f32) * grad, axis=-1) for weight, grad in both)

    grad_gain_one = gain_grad((query_weight, grad_query), (key_matrix, grad_key), (value_matrix, grad_value))
    grad_gain_two = gain_grad((gate_weight, grad_gate), (up_weight, grad_up))
    return (
        layer_output, input_grad, grad_gain_one, grad_query * gain_one, grad_key * gain_one, grad_value * gain_one,
        grad_output, grad_gain_two, grad_gate * gain_two, grad_up * gain_two, grad_down,
    )


def solution(mesh):
    fine = Mesh(mesh.devices.reshape(-1, 2, 2, 2, 2), ALL)
    token = P(None, ALL, None)
    row = P(ALL, None)
    vec = P(ALL)
    in_specs = (token, vec, row, row, row, row, vec, row, row, row, P(), token)
    out_specs = (token, token, vec, row, row, row, row, vec, row, row, row)
    return jax.shard_map(local, mesh=fine, in_specs=in_specs, out_specs=out_specs, check_vma=False)
```
